32 devices in a mesh: dp: 8 (over z, x), seq: 4 (over y, core).
Axes of the slice: x: 2, y: 2, z: 4, core: 2. Of those that a mesh axis runs over, the one named last changes fastest.
Arguments:
- tokens: bfloat16 [8, 512, 8192], P('dp', 'seq'), may hold values from -6 to 6
- gain: float32 [8192], replicated, may hold values from 0.25 to 1.75
- w_t: bfloat16 [512, 8192], P('dp', 'seq'), may hold values from -0.0625 to 0.0625
- grad_values: bfloat16 [8, 512, 512], P('dp', 'seq'), may hold values from -6 to 6
- owner: int32 [512], replicated, may hold values from 0 to 7, as said below
- master: float32 [8, 128, 8192], P('dp', None, 'seq'), may hold values from -0.0625 to 0.0625
- moment1: float32 [8, 128, 8192], P('dp', None, 'seq'), may hold values from -0.024 to 0.024
- moment2: float32 [8, 128, 8192], P('dp', None, 'seq'), may hold values from 1e-06 to 4e-05
Outputs:
- values: bfloat16 [8, 512, 512], P('dp', 'seq')
- grad_x: bfloat16 [8, 512, 8192], P('dp', 'seq')
- new_master: float32 [8, 128, 8192], P('dp', None, 'seq')
- new_moment1: float32 [8, 128, 8192], P('dp', None, 'seq')
- new_moment2: float32 [8, 128, 8192], P('dp', None, 'seq')
The draws below stay inside these ranges and needn't reach their ends.
Inputs may be any that keep to these rules, and one draw needn't show every extreme that they name: `owner`: each index of dp owns at most 128 rows and some own exactly 128; some may own none.
All inputs are finite; a program needn't handle non-finite values.
Results may differ from the reference program's by a relative error of at most 0.012.
Values may be sent and summed in bfloat16 or wider, within the bound.
No kernel may reach another device: no remote copies, remote signals or barrier semaphores. Data moves between devices by JAX's collectives and lax.ppermute only.
A program may use at most 128 MiB of HBM per device.

```python
import math
import jax
import jax.numpy as jnp
from jax import lax

D = 8192
F = 512
LEN = 512
CAP = 128
N_DP = 8


def draw_owner(key, part):
    first_key, second_key = jax.random.split(jax.random.fold_in(key, 11))
    pair_count = max(N_DP // 8, 1)
    row_order = jax.random.permutation(first_key, F)
    row_label = row_order % N_DP
    row_label = jnp.where((row_label >= pair_count) & (row_label < 2 * pair_count), row_label - pair_count, row_label)
    device_order = jax.random.permutation(second_key, N_DP)
    return device_order[row_label].astype(jnp.int32)


def strengthened(values, key, source, target, blocks, factor):
    def block_of(dim):
        return (jnp.arange(values.shape[dim]) // (values.shape[dim] // blocks)).reshape((-1,) + (1,) * (values.ndim - 1 - dim))

    near = jax.random.permutation(key, blocks)[block_of(target)]
    other_side = (block_of(target) + blocks // 2) % blocks
    return jnp.where((block_of(source) == near) | (block_of(source) == other_side), factor * values, values)


def shard_levels(stream_key, shape, cuts, smallest, largest):
    level = 1.0
    for axis_at, parts in cuts:
        draws = jax.random.uniform(jax.random.fold_in(jax.random.fold_in(stream_key, 6), axis_at), (parts,), jnp.float32, smallest / len(cuts), largest / len(cuts))
        level = level * jnp.repeat(jnp.exp(draws), shape[axis_at] // parts).reshape((-1,) + (1,) * (len(shape) - 1 - axis_at))
    return level


def bell_draw(own_key, shape, scale, most, pieces=(), held_as=jnp.bfloat16):
    entries = jax.random.normal(own_key, shape, jnp.float32) * scale
    if len(pieces) > 0:
        entries = shard_levels(own_key, shape, pieces, -0.22, 0.18) * entries
    return jnp.clip(entries, min=-most, max=most).astype(held_as)


def gaussian_with(own_key, shape, deviation, reach, cuts, heavy, kind=jnp.bfloat16):
    array = deviation * jax.random.normal(own_key, shape, jnp.float32)
    if cuts:
        array = array * shard_levels(own_key, shape, cuts, -0.22, 0.18)
    return jnp.clip(strengthened(array, jax.random.fold_in(own_key, 3), *heavy), -reach, reach).astype(kind)


def setup_inputs(seed: int = 0) -> dict:
    streams_of = jax.random.split(jax.random.key(seed), 9)
    tokens = bell_draw(streams_of[0], (N_DP, LEN, D), 1.0, 6.0, ((0, 8), (1, 4)))
    gain = jnp.clip(1.0 + 0.15 * jax.random.normal(streams_of[1], (D,), jnp.float32), 0.25, 1.75)
    w_t = bell_draw(streams_of[2], (F, D), D ** -0.5, 0.0625, ((0, 8), (1, 4)))
    grad_values = gaussian_with(streams_of[3], (N_DP, LEN, F), 1.0, 6.0, ((0, 8), (1, 4)), (0, 2, 8, 2.0))
    owner = draw_owner(jax.random.fold_in(streams_of[8], 71), 0)
    master = bell_draw(streams_of[5], (N_DP, CAP, D), D ** -0.5, 0.0625, ((0, 8), (2, 4)), jnp.float32)
    moment1 = bell_draw(streams_of[6], (N_DP, CAP, D), 0.004, 0.024, ((0, 8), (2, 4)), jnp.float32)
    moment2 = jnp.clip(jnp.exp(math.log(3.9999998989515007e-05) - 3.6888794 * jax.random.uniform(streams_of[7], (N_DP, CAP, D), jnp.float32) ** shard_levels(streams_of[7], (N_DP, CAP, D), ((0, 8), (2, 4)), -0.2, 0.2)), 9.999999974752427e-07, 3.9999998989515007e-05)
    return {"tokens": tokens, "gain": gain, "w_t": w_t, "grad_values": grad_values, "owner": owner, "master": master, "moment1": moment1, "moment2": moment2}


beta_one = 0.9
beta_two = 0.95
learn_rate = 0.001
adam_eps = 1e-08
bias_one = 1.0 - 0.9 ** 10
bias_two = 1.0 - 0.95 ** 10

def reference(tokens, gain, w_t, grad_values, owner, master, moment1, moment2):

    def one_sequence(carry, inputs):
        seq_tokens, seq_grads = inputs
        tok_float = seq_tokens.astype(jnp.float32)
        inv_rms = lax.rsqrt(lax.optimization_barrier(jnp.mean(tok_float * tok_float, axis=-1, keepdims=True)) + 1e-05)
        scaled = tok_float * inv_rms
        normed = (scaled * gain).astype(jnp.bfloat16)
        values = lax.dot_general(normed, w_t, (((1,), (1,)), ((), ())), preferred_element_type=jnp.float32).astype(jnp.bfloat16)
        grad_normed = jnp.dot(seq_grads, w_t, preferred_element_type=jnp.float32).astype(jnp.bfloat16)
        weighted = gain * grad_normed.astype(jnp.float32)
        grad_x = (inv_rms * (weighted - scaled * lax.optimization_barrier(jnp.mean(weighted * scaled, axis=-1, keepdims=True)))).astype(jnp.bfloat16)
        block = lax.dot_general(seq_grads, normed, (((0,), (0,)), ((), ())), preferred_element_type=jnp.float32)
        return (carry + block, (values, grad_x))
    summed, outputs = lax.scan(one_sequence, jnp.zeros((F, D), jnp.float32), (tokens, grad_values))
    values, grad_x = outputs
    weight_grad = summed / (LEN * N_DP)
    onehot = (owner[:, None] == jnp.arange(N_DP, dtype=jnp.int32)[None, :]).astype(jnp.int32)
    prior_count = jnp.cumsum(onehot, axis=0) - onehot
    slot_row = lax.optimization_barrier(jnp.sum(prior_count * onehot, axis=1))
    select_all = ((owner[None, None, :] == jnp.arange(N_DP, dtype=jnp.int32)[:, None, None]) & (slot_row[None, None, :] == jnp.arange(CAP, dtype=jnp.int32)[None, :, None])).astype(jnp.float32)
    slot_grad = jnp.einsum('pjf,fd->pjd', select_all, weight_grad, precision=lax.Precision.HIGHEST)
    occupied = lax.optimization_barrier(jnp.sum(select_all, axis=-1, keepdims=True))
    new_moment1 = (beta_one * moment1 + (1.0 - beta_one) * slot_grad) * occupied
    new_moment2 = (beta_two * moment2 + (1.0 - beta_two) * slot_grad * slot_grad) * occupied
    step_dir = new_moment1 / bias_one / (jnp.sqrt(new_moment2 / bias_two) + adam_eps)
    new_master = (master - learn_rate * step_dir) * occupied
    return (values, grad_x, new_master, new_moment1, new_moment2)
```

```python
import functools

import jax
import jax.numpy as jnp
from jax import lax
from jax.experimental import pallas as pl
from jax.experimental.pallas import tpu as pltpu
from jax.sharding import PartitionSpec as P

beta_one = 0.9
beta_two = 0.95
learn_rate = 0.001
adam_eps = 1e-08
bias_one = 1.0 - 0.9**10
bias_two = 1.0 - 0.95**10
norm_eps = 1e-05

bf16 = jnp.bfloat16
f32 = jnp.float32


def norm_kernel(offs, tok_ref, gain_ref, *out_refs):
    width = out_refs[0].shape[-1]
    tok = tok_ref[...].astype(f32)
    inv_rms = lax.rsqrt(jnp.mean(tok * tok, axis=-1, keepdims=True) + norm_eps)
    for k, out_ref in enumerate(out_refs):
        for j in range(2):
            cols = pl.ds(pl.multiple_of(offs[2 * k + j] * width, width), width)
            scaled = tok_ref[:, cols].astype(f32) * inv_rms
            out_ref[j] = (scaled * gain_ref[:, cols]).astype(bf16)


def norm_blocks(offs, tokens, gain, chips, width):
    rows, model = tokens.shape
    step = min(rows, 32)
    return pl.pallas_call(
        norm_kernel,
        grid_spec=pltpu.PrefetchScalarGridSpec(
            num_scalar_prefetch=1,
            grid=(rows // step,),
            in_specs=[
                pl.BlockSpec((step, model), lambda i, offs: (i, 0)),
                pl.BlockSpec((1, model), lambda i, offs: (0, 0)),
            ],
            out_specs=[pl.BlockSpec((2, step, width), lambda i, offs: (0, i, 0))] * chips,
        ),
        out_shape=[jax.ShapeDtypeStruct((2, rows, width), bf16)] * chips,
        compiler_params=pltpu.CompilerParams(vmem_limit_bytes=24 * 1024 * 1024),
        name="norm_blocks",
    )(offs, tokens, gain)


def grad_x_kernel(offs, tok_ref, gain_ref, *refs):
    grad_refs, out_ref = refs[:-1], refs[-1]
    model = tok_ref.shape[-1]
    width = grad_refs[0].shape[-1]
    tok = tok_ref[...].astype(f32)
    inv_rms = lax.rsqrt(jnp.mean(tok * tok, axis=-1, keepdims=True) + norm_eps)
    total = jnp.zeros((tok.shape[0], 1), f32)
    for k, grad_ref in enumerate(grad_refs):
        for j in range(2):
            cols = pl.ds(pl.multiple_of(offs[2 * k + j] * width, width), width)
            weighted = gain_ref[:, cols] * grad_ref[j].astype(f32)
            scaled = tok_ref[:, cols].astype(f32) * inv_rms
            total += jnp.sum(weighted * scaled, axis=-1, keepdims=True)
    mean = total / model
    for k, grad_ref in enumerate(grad_refs):
        for j in range(2):
            cols = pl.ds(pl.multiple_of(offs[2 * k + j] * width, width), width)
            weighted = gain_ref[:, cols] * grad_ref[j].astype(f32)
            scaled = tok_ref[:, cols].astype(f32) * inv_rms
            out_ref[:, cols] = (inv_rms * (weighted - scaled * mean)).astype(bf16)


def grad_x_blocks(offs, tokens, gain, grads):
    rows, model = tokens.shape
    width = grads[0].shape[-1]
    step = min(rows, 32)
    return pl.pallas_call(
        grad_x_kernel,
        grid_spec=pltpu.PrefetchScalarGridSpec(
            num_scalar_prefetch=1,
            grid=(rows // step,),
            in_specs=[
                pl.BlockSpec((step, model), lambda i, offs: (i, 0)),
                pl.BlockSpec((1, model), lambda i, offs: (0, 0)),
            ]
            + [pl.BlockSpec((2, step, width), lambda i, offs: (0, i, 0))] * len(grads),
            out_specs=pl.BlockSpec((step, model), lambda i, offs: (i, 0)),
        ),
        out_shape=jax.ShapeDtypeStruct((rows, model), bf16),
        compiler_params=pltpu.CompilerParams(vmem_limit_bytes=24 * 1024 * 1024),
        name="grad_x_blocks",
    )(offs, tokens, gain, *grads)


def on_device(groups, seqs, tokens, gain, w_t, grad_values, owner, master, moment1, moment2):
    planes = groups // 2
    chips = seqs
    tokens, value_grad = tokens[0], grad_values[0]
    rows, model = tokens.shape
    feats = owner.shape[0]
    slots = master.shape[1]
    width = model // (2 * seqs)
    share = w_t.shape[0]

    own_dp = lax.axis_index("dp")
    own_seq = lax.axis_index("seq")
    own_x, own_z = own_dp % 2, own_dp // 2
    own_core = own_seq % 2

    def permute(value, target):
        pairs = []
        for dp in range(groups):
            for seq in range(seqs):
                to = target(dp, seq)
                if to is not None:
                    pairs.append((dp * seqs + seq, to[0] * seqs + to[1]))
        return lax.ppermute(value, ("dp", "seq"), pairs)

    def to_chip(value, k):
        return permute(value, lambda dp, seq: (dp ^ (k & 1), seq ^ (k >> 1 << 1)))

    def to_core(value):
        return permute(value, lambda dp, seq: (dp, seq ^ 1))

    def to_x(value):
        return permute(value, lambda dp, seq: (dp ^ 1, seq))

    def to_plane(value, turn):
        return permute(value, lambda dp, seq: ((dp + 2 * turn) % groups, seq))

    offs = jnp.stack(
        [
            ((own_seq ^ (k >> 1 << 1)) ^ j) * 2 + (own_x ^ (k & 1))
            for k in range(chips)
            for j in range(2)
        ]
    ).astype(jnp.int32)
    gain_row = gain[None, :]

    grads = [value_grad] + [to_chip(value_grad, k) for k in range(1, chips)]
    grads_core = jnp.concatenate(grads, axis=0)
    grads_other = to_core(grads_core)

    halves = w_t.reshape(share, 2, width)
    w_keep = lax.dynamic_index_in_dim(halves, own_x, 1, keepdims=False)
    w_got = to_x(lax.dynamic_index_in_dim(halves, 1 - own_x, 1, keepdims=False))
    first = own_x == 0
    w_plane = jnp.concatenate(
        [jnp.where(first, w_keep, w_got), jnp.where(first, w_got, w_keep)], axis=0
    )
    w_own = jnp.zeros((planes, 2 * share, width), bf16)
    w_own = lax.dynamic_update_index_in_dim(w_own, w_plane, own_z, 0)
    for turn in range(1, planes):
        w_own = lax.dynamic_update_index_in_dim(
            w_own, to_plane(w_plane, turn), (own_z - turn) % planes, 0
        )
    w_own = w_own.reshape(feats, width)
    w_other = to_core(w_own)

    normed = norm_blocks(offs, tokens, gain_row, chips, width)
    normed = [normed[0]] + [to_chip(normed[k], k) for k in range(1, chips)]
    cols_own = jnp.concatenate([n[0] for n in normed], axis=0)
    cols_other = jnp.concatenate([n[1] for n in normed], axis=0)
    cols_far = to_core(cols_other)

    index = jnp.arange(feats, dtype=jnp.int32)
    same = (owner[:, None] == owner[None, :]) & (index[None, :] < index[:, None])
    slot = owner * slots + jnp.sum(same.astype(jnp.int32), axis=1)
    select = (slot[:, None] == jnp.arange(groups * slots, dtype=jnp.int32)[None, :]).astype(bf16)
    count = jnp.sum((owner == own_dp).astype(jnp.int32))
    occupied = (jnp.arange(slots, dtype=jnp.int32) < count).astype(f32)[:, None]
    grads_sel = jnp.dot(
        jnp.concatenate([grads_core, grads_other], axis=0), select, preferred_element_type=f32
    ).astype(bf16)
    partial = lax.dot_general(
        grads_sel,
        jnp.concatenate([cols_own, cols_far], axis=0),
        (((0,), (0,)), ((), ())),
        preferred_element_type=f32,
    ).astype(bf16)
    partial = partial.reshape(planes, 2 * slots, width)

    def block(at):
        return lax.dynamic_index_in_dim(partial, jnp.clip(at, 0, planes - 1), 0, keepdims=False)

    right = left = None
    for step in range(1, planes):
        send_right = block(planes - step + own_z)
        send_left = block(step + own_z - planes)
        if right is not None:
            send_right = (send_right.astype(f32) + right.astype(f32)).astype(bf16)
            send_left = (send_left.astype(f32) + left.astype(f32)).astype(bf16)
        right = permute(
            send_right, lambda dp, seq: (dp + 2, seq) if dp // 2 < min(step, planes - 1) else None
        )
        left = permute(
            send_left,
            lambda dp, seq: (dp - 2, seq) if planes - 1 - dp // 2 < min(step, planes - 1) else None,
        )
    mine = block(own_z).astype(f32) + right.astype(f32) + left.astype(f32)
    mine = mine.reshape(2, slots, width)
    kept = lax.dynamic_index_in_dim(mine, own_x, 0, keepdims=False)
    got = to_x(lax.dynamic_index_in_dim(mine, 1 - own_x, 0, keepdims=False).astype(bf16)).astype(f32)

    grad_blocks = [
        jnp.dot(grads_core, w, preferred_element_type=f32).astype(bf16).reshape(chips, rows, width)
        for w in (w_own, w_other)
    ]
    grad_blocks = jnp.stack(grad_blocks, axis=1)
    grad_home = [grad_blocks[0]] + [to_chip(grad_blocks[k], k) for k in range(1, chips)]
    grad_x = grad_x_blocks(offs, tokens, gain_row, grad_home)

    dims = (((1,), (1,)), ((), ()))
    value_part = lax.dot_general(cols_own, w_own, dims, preferred_element_type=f32)
    value_part += lax.dot_general(cols_other, w_other, dims, preferred_element_type=f32)
    value_part = value_part.reshape(chips, rows, feats)
    values = value_part[0]
    for k in range(1, chips):
        values += to_chip(value_part[k].astype(bf16), k).astype(f32)
    values = values.astype(bf16)

    token_total = rows * seqs * groups
    slot_grad = jnp.concatenate([jnp.where(first, kept, got), jnp.where(first, got, kept)], axis=1)
    slot_grad = slot_grad / token_total
    new_moment1 = (beta_one * moment1[0] + (1.0 - beta_one) * slot_grad) * occupied
    new_moment2 = (beta_two * moment2[0] + (1.0 - beta_two) * slot_grad * slot_grad) * occupied
    step_dir = new_moment1 / bias_one / (jnp.sqrt(new_moment2 / bias_two) + adam_eps)
    new_master = (master[0] - learn_rate * step_dir) * occupied
    return (values[None], grad_x[None], new_master[None], new_moment1[None], new_moment2[None])


def solution(mesh):
    placed = (
        P("dp", "seq", None),
        P(),
        P("dp", "seq"),
        P("dp", "seq", None),
        P(),
        P("dp", None, "seq"),
        P("dp", None, "seq"),
        P("dp", None, "seq"),
    )
    return jax.shard_map(
        functools.partial(on_device, mesh.shape["dp"], mesh.shape["seq"]),
        mesh=mesh,
        in_specs=placed,
        out_specs=(
            P("dp", "seq", None),
            P("dp", "seq", None),
            P("dp", None, "seq"),
            P("dp", None, "seq"),
            P("dp", None, "seq"),
        ),
        check_vma=False,
    )
```

```python
import functools

import jax
import jax.numpy as jnp
from jax import lax
from jax.experimental import pallas as pl
from jax.experimental.pallas import tpu as pltpu
from jax.sharding import PartitionSpec as P

beta_one = 0.9
beta_two = 0.95
learn_rate = 0.001
adam_eps = 1e-08
bias_one = 1.0 - 0.9**10
bias_two = 1.0 - 0.95**10
norm_eps = 1e-05

bf16 = jnp.bfloat16
f32 = jnp.float32


def cost(flops, moved):
    return pl.CostEstimate(flops=flops, bytes_accessed=moved, transcendentals=0)


def limit(mib):
    return pltpu.CompilerParams(vmem_limit_bytes=mib * 1024 * 1024)


def column_block(k, j, width):
    seq = lax.axis_index("seq") ^ (k >> 1 << 1) ^ j
    x = (lax.axis_index("dp") % 2) ^ (k & 1)
    return pl.ds(pl.multiple_of((seq * 2 + x) * width, width), width)


def norm_kernel(tok_ref, gain_ref, *out_refs):
    width = out_refs[0].shape[-1]
    tok = tok_ref[...].astype(f32)
    inv_rms = lax.rsqrt(jnp.mean(tok * tok, axis=-1, keepdims=True) + norm_eps)
    for k, out_ref in enumerate(out_refs):
        for j in range(2):
            cols = column_block(k, j, width)
            scaled = tok_ref[:, cols].astype(f32) * inv_rms
            out_ref[j] = (scaled * gain_ref[:, cols]).astype(bf16)


def norm_blocks(tokens, gain, chips, width):
    rows, model = tokens.shape
    step = min(rows, 32)
    return pl.pallas_call(
        norm_kernel,
        grid=(rows // step,),
        in_specs=[
            pl.BlockSpec((step, model), lambda i: (i, 0)),
            pl.BlockSpec((1, model), lambda i: (0, 0)),
        ],
        out_specs=[pl.BlockSpec((2, step, width), lambda i: (0, i, 0))] * chips,
        out_shape=[jax.ShapeDtypeStruct((2, rows, width), bf16)] * chips,
        compiler_params=limit(24),
        cost_estimate=cost(8 * rows * model, 4 * rows * model),
        name="norm_blocks",
    )(tokens, gain)


def grad_x_kernel(tok_ref, gain_ref, *refs):
    grad_refs, out_ref = refs[:-1], refs[-1]
    model = tok_ref.shape[-1]
    width = grad_refs[0].shape[-1]
    tok = tok_ref[...].astype(f32)
    inv_rms = lax.rsqrt(jnp.mean(tok * tok, axis=-1, keepdims=True) + norm_eps)
    total = jnp.zeros((tok.shape[0], 1), f32)
    for k, grad_ref in enumerate(grad_refs):
        for j in range(2):
            cols = column_block(k, j, width)
            weighted = gain_ref[:, cols] * grad_ref[j].astype(f32)
            scaled = tok_ref[:, cols].astype(f32) * inv_rms
            total += jnp.sum(weighted * scaled, axis=-1, keepdims=True)
    mean = total / model
    for k, grad_ref in enumerate(grad_refs):
        for j in range(2):
            cols = column_block(k, j, width)
            weighted = gain_ref[:, cols] * grad_ref[j].astype(f32)
            scaled = tok_ref[:, cols].astype(f32) * inv_rms
            out_ref[:, cols] = (inv_rms * (weighted - scaled * mean)).astype(bf16)


def grad_x_blocks(tokens, gain, grads):
    rows, model = tokens.shape
    width = grads[0].shape[-1]
    step = min(rows, 32)
    return pl.pallas_call(
        grad_x_kernel,
        grid=(rows // step,),
        in_specs=[
            pl.BlockSpec((step, model), lambda i: (i, 0)),
            pl.BlockSpec((1, model), lambda i: (0, 0)),
        ]
        + [pl.BlockSpec((2, step, width), lambda i: (0, i, 0))] * len(grads),
        out_specs=pl.BlockSpec((step, model), lambda i: (i, 0)),
        out_shape=jax.ShapeDtypeStruct((rows, model), bf16),
        compiler_params=limit(24),
        cost_estimate=cost(16 * rows * model, 6 * rows * model),
        name="grad_x_blocks",
    )(tokens, gain, *grads)


def select_kernel(slots, owner_row_ref, owner_col_ref, *refs):
    grad_refs, out_ref, held = refs[:-2], refs[-2], refs[-1]
    rows = grad_refs[0].shape[0]
    feats = owner_row_ref.shape[1]
    owner = owner_row_ref[...]
    lower = lax.broadcasted_iota(jnp.int32, (feats, feats), 0) < lax.broadcasted_iota(
        jnp.int32, (feats, feats), 1
    )
    same = (owner_col_ref[...] == owner) & lower
    place = jnp.sum(same.astype(f32), axis=0, keepdims=True).astype(jnp.int32)
    own_x = lax.axis_index("dp") % 2
    slot = (owner ^ own_x) * slots + place
    for i, grad_ref in enumerate(grad_refs):
        held[i * rows : (i + 1) * rows, :] = grad_ref[...]
    step = 256
    for at in range(0, out_ref.shape[0], step):
        index = at + lax.broadcasted_iota(jnp.int32, (step, feats), 0)
        chosen = (index == slot).astype(f32).astype(bf16)
        out_ref[at : at + step, :] = lax.dot_general(
            chosen, held[...], (((1,), (1,)), ((), ())), preferred_element_type=f32
        ).astype(bf16)


def select_grads(owner, grads, groups, slots):
    feats = owner.shape[0]
    total = grads[0].shape[0] * len(grads)
    return pl.pallas_call(
        functools.partial(select_kernel, slots),
        out_shape=jax.ShapeDtypeStruct((groups * slots, total), bf16),
        scratch_shapes=[pltpu.VMEM((total, feats), bf16)],
        compiler_params=limit(40),
        cost_estimate=cost(2 * groups * slots * total * feats, 2 * groups * slots * total),
        name="select_grads",
    )(owner[None, :], owner[:, None], *grads)


def weight_kernel(planes, sel_ref, *refs):
    count = 2 * planes
    piece_refs, out_refs, held = refs[: -count - 1], refs[-count - 1 : -1], refs[-1]
    rights, lefts = out_refs[: planes - 1], out_refs[planes - 1 : 2 * planes - 2]
    mine_ref, other_ref = out_refs[-2:]
    rows = piece_refs[0].shape[1]
    block = sel_ref.shape[0] // planes
    slots = block // 2
    z = lax.axis_index("dp") // 2
    for i, ref in enumerate(piece_refs):
        held[i * rows : (i + 1) * rows, :] = ref[0]

    def product(plane, part, height):
        at = pl.multiple_of(plane * block + part * height, height)
        return jnp.dot(sel_ref[pl.ds(at, height), :], held[...], preferred_element_type=f32)

    for step in range(1, planes):
        far = planes - step

        @pl.when(z + far < planes)
        def _():
            rights[step - 1][...] = product(z + far, 0, block).astype(bf16)

        @pl.when(z - far >= 0)
        def _():
            lefts[step - 1][...] = product(z - far, 0, block).astype(bf16)

    other_ref[...] = product(z, 1, slots).astype(bf16)
    mine_ref[...] = product(z, 0, slots)


def weight_blocks(selected, own_pieces, far_pieces, planes):
    slots_all, total = selected.shape
    _, rows, width = own_pieces[0].shape
    block = slots_all // planes
    shapes = [jax.ShapeDtypeStruct((block, width), bf16)] * (2 * planes - 2) + [
        jax.ShapeDtypeStruct((block // 2, width), f32),
        jax.ShapeDtypeStruct((block // 2, width), bf16),
    ]
    whole = lambda shape: pl.BlockSpec(shape, lambda i: (0,) * len(shape))
    outs = pl.pallas_call(
        functools.partial(weight_kernel, planes),
        grid=(1,),
        in_specs=[whole(selected.shape)]
        + [pl.BlockSpec((1, rows, width), lambda i: (0, 0, 0))] * len(own_pieces)
        + [pl.BlockSpec((1, rows, width), lambda i: (1, 0, 0))] * len(far_pieces),
        out_specs=[whole(s.shape) for s in shapes],
        out_shape=shapes,
        scratch_shapes=[pltpu.VMEM((total, width), bf16)],
        compiler_params=limit(40),
        cost_estimate=cost(2 * slots_all * total * width, 4 * total * width),
        name="weight_blocks",
    )(selected, *own_pieces, *far_pieces)
    return outs[: planes - 1], outs[planes - 1 : 2 * planes - 2], outs[-2], outs[-1]


def gather_weight(planes, piece_refs, held):
    dp = lax.axis_index("dp")
    own_x, own_z = dp % 2, dp // 2
    for j in range(2):
        for turn in range(planes):
            ref = piece_refs[j * planes + turn]
            share = ref.shape[0] // 2
            plane = lax.rem(own_z + planes - turn, planes)
            for i in range(2):
                at = pl.multiple_of((plane * 2 + (own_x ^ i)) * share, share)
                held[j, pl.ds(at, share), :] = ref[i * share : (i + 1) * share, :]


def grad_normed_kernel(planes, chips, *refs):
    grad_refs, piece_refs, out_refs, held = (
        refs[:chips],
        refs[chips : chips + 2 * planes],
        refs[chips + 2 * planes : -1],
        refs[-1],
    )
    gather_weight(planes, piece_refs, held)
    for k in (*range(1, chips), 0):
        for j in range(2):
            out_refs[k][j] = jnp.dot(
                grad_refs[k][...], held[j], preferred_element_type=f32
            ).astype(bf16)


def grad_normed_blocks(grads, weights, planes):
    chips = len(grads)
    rows, feats = grads[0].shape
    width = weights[0].shape[-1]
    return pl.pallas_call(
        functools.partial(grad_normed_kernel, planes, chips),
        out_shape=[jax.ShapeDtypeStruct((2, rows, width), bf16)] * chips,
        scratch_shapes=[pltpu.VMEM((2, feats, width), bf16)],
        compiler_params=limit(40),
        cost_estimate=cost(4 * chips * rows * feats * width, 4 * chips * rows * width),
        name="grad_normed_blocks",
    )(*grads, *weights)


def values_kernel(planes, chips, *refs):
    piece_refs, weight_refs, out_refs, held = (
        refs[:chips],
        refs[chips : chips + 2 * planes],
        refs[chips + 2 * planes : -1],
        refs[-1],
    )
    gather_weight(planes, weight_refs, held)
    dims = (((1,), (1,)), ((), ()))
    for k in (*range(1, chips), 0):
        part = lax.dot_general(piece_refs[k][0], held[0], dims, preferred_element_type=f32)
        part += lax.dot_general(piece_refs[k][1], held[1], dims, preferred_element_type=f32)
        out_refs[k][...] = part.astype(out_refs[k].dtype)


def value_parts(pieces, weights, planes, feats):
    chips = len(pieces)
    _, rows, width = pieces[0].shape
    return pl.pallas_call(
        functools.partial(values_kernel, planes, chips),
        out_shape=[
            jax.ShapeDtypeStruct((rows, feats), bf16 if k else f32) for k in range(chips)
        ],
        scratch_shapes=[pltpu.VMEM((2, feats, width), bf16)],
        compiler_params=limit(40),
        cost_estimate=cost(4 * chips * rows * feats * width, 4 * chips * rows * width),
        name="value_parts",
    )(*pieces, *weights)


def relay_kernel(a_ref, b_ref, c_ref, d_ref, *out_refs):
    half = len(out_refs) // 2
    for add_ref, got_ref, outs in (
        (a_ref, b_ref, out_refs[:half]),
        (c_ref, d_ref, out_refs[half:]),
    ):
        height = outs[0].shape[0]
        for i, out_ref in enumerate(outs):
            part = slice(i * height, (i + 1) * height)
            total = add_ref[part, :].astype(f32) + got_ref[part, :].astype(f32)
            out_ref[...] = total.astype(bf16)


def relay(right, got_right, left, got_left, parts):
    height, width = right.shape
    outs = pl.pallas_call(
        relay_kernel,
        out_shape=[jax.ShapeDtypeStruct((height // parts, width), bf16)] * (2 * parts),
        compiler_params=limit(16),
        cost_estimate=cost(2 * height * width, 12 * height * width),
        name="relay",
    )(right, got_right, left, got_left)
    return outs[:parts], outs[parts:]


def adam_kernel(token_total, owner_ref, *refs):
    part_refs, state_refs, out_refs = refs[:6], refs[6:9], refs[9:]
    master_ref, moment1_ref, moment2_ref = state_refs
    width = part_refs[0].shape[-1]
    step = part_refs[0].shape[0]
    dp = lax.axis_index("dp")
    owned = (owner_ref[...] == dp).astype(f32)
    count = jnp.sum(owned, axis=1, keepdims=True)
    index = pl.program_id(0) * step + lax.broadcasted_iota(jnp.int32, (step, 1), 0)
    occupied = (index.astype(f32) < count).astype(f32)
    for i in range(2):
        total = part_refs[3 * i][...].astype(f32)
        total += part_refs[3 * i + 1][...].astype(f32)
        total += part_refs[3 * i + 2][...].astype(f32)
        cols = pl.ds(pl.multiple_of(((dp % 2) ^ i) * width, width), width)
        slot_grad = total / token_total
        new_moment1 = (
            beta_one * moment1_ref[:, cols] + (1.0 - beta_one) * slot_grad
        ) * occupied
        new_moment2 = (
            beta_two * moment2_ref[:, cols] + (1.0 - beta_two) * slot_grad * slot_grad
        ) * occupied
        step_dir = new_moment1 / bias_one / (jnp.sqrt(new_moment2 / bias_two) + adam_eps)
        out_refs[0][:, cols] = (master_ref[:, cols] - learn_rate * step_dir) * occupied
        out_refs[1][:, cols] = new_moment1
        out_refs[2][:, cols] = new_moment2


def adam(owner, parts, states, token_total):
    slots, cols = states[0].shape
    width = parts[0].shape[-1]
    step = min(slots, 32)
    return pl.pallas_call(
        functools.partial(adam_kernel, token_total),
        grid=(slots // step,),
        in_specs=[pl.BlockSpec((1, owner.shape[0]), lambda i: (0, 0))]
        + [pl.BlockSpec((step, width), lambda i: (i, 0))] * 6
        + [pl.BlockSpec((step, cols), lambda i: (i, 0))] * 3,
        out_specs=[pl.BlockSpec((step, cols), lambda i: (i, 0))] * 3,
        out_shape=[jax.ShapeDtypeStruct((slots, cols), f32)] * 3,
        compiler_params=limit(24),
        cost_estimate=cost(20 * slots * cols, 30 * slots * cols),
        name="adam",
    )(owner[None, :], *parts, *states)


def on_device(groups, seqs, tokens, gain, w_t, grad_values, owner, master, moment1, moment2):
    planes = groups // 2
    chips = seqs
    tokens, value_grad = tokens[0], grad_values[0]
    rows, model = tokens.shape
    feats = owner.shape[0]
    slots = master.shape[1]
    width = model // (2 * seqs)
    own_x = lax.axis_index("dp") % 2

    def permute(value, target):
        pairs = []
        for dp in range(groups):
            for seq in range(seqs):
                to = target(dp, seq)
                if to is not None:
                    pairs.append((dp * seqs + seq, to[0] * seqs + to[1]))
        return lax.ppermute(value, ("dp", "seq"), pairs)

    def to_chip(value, k):
        return permute(value, lambda dp, seq: (dp ^ (k & 1), seq ^ (k >> 1 << 1)))

    def to_core(value):
        return permute(value, lambda dp, seq: (dp, seq ^ 1))

    def to_x(value):
        return permute(value, lambda dp, seq: (dp ^ 1, seq))

    def to_plane(value, turn):
        return permute(value, lambda dp, seq: ((dp + 2 * turn) % groups, seq))

    def along(value, step, way, flip=0):
        def target(dp, seq):
            z = dp // 2 if way > 0 else planes - 1 - dp // 2
            return ((dp + 2 * way) ^ flip, seq) if z < step else None

        return permute(value, target)

    w_keep = lax.dynamic_slice_in_dim(w_t, own_x * width, width, 1)
    w_got = to_x(lax.dynamic_slice_in_dim(w_t, (1 - own_x) * width, width, 1))

    grads = [value_grad] + [to_chip(value_grad, k) for k in range(1, chips)]
    grads_far = [to_core(g) for g in grads]

    gain_row = gain[None, :]
    normed = norm_blocks(tokens, gain_row, chips, width)
    normed = [normed[0]] + [to_chip(normed[k], k) for k in range(1, chips)]
    normed_far = [to_core(n) for n in normed]

    w_plane = jnp.concatenate([w_keep, w_got], axis=0)
    w_own = [w_plane] + [to_plane(w_plane, turn) for turn in range(1, planes)]
    weights = w_own + [to_core(w) for w in w_own]

    selected = select_grads(owner, grads + grads_far, groups, slots)

    grad_blocks = grad_normed_blocks(grads, weights, planes)
    grad_home = [grad_blocks[0]] + [to_chip(grad_blocks[k], k) for k in range(1, chips)]

    rights, lefts, mine, other = weight_blocks(selected, normed, normed_far, planes)
    other = to_x(other)
    right, left = along(rights[0], 1, 1), along(lefts[0], 1, -1)
    for step in range(2, planes - 1):
        (right,), (left,) = relay(rights[step - 1], right, lefts[step - 1], left, 1)
        right, left = along(right, step, 1), along(left, step, -1)
    last = planes - 1
    send_right, send_left = relay(rights[last - 1], right, lefts[last - 1], left, 2)
    parts = [mine, along(send_right[0], last, 1), along(send_left[0], last, -1)]
    parts += [other, along(send_right[1], last, 1, 1), along(send_left[1], last, -1, 1)]

    value_part = value_parts(normed, weights, planes, feats)
    values = value_part[0]
    for k in range(1, chips):
        values += to_chip(value_part[k], k).astype(f32)
    values = values.astype(bf16)

    grad_x = grad_x_blocks(tokens, gain_row, grad_home)
    states = adam(owner, parts, (master[0], moment1[0], moment2[0]), rows * seqs * groups)
    return (values[None], grad_x[None], *(s[None] for s in states))


def solution(mesh):
    placed = (
        P("dp", "seq", None),
        P(),
        P("dp", "seq"),
        P("dp", "seq", None),
        P(),
        P("dp", None, "seq"),
        P("dp", None, "seq"),
        P("dp", None, "seq"),
    )
    return jax.shard_map(
        functools.partial(on_device, mesh.shape["dp"], mesh.shape["seq"]),
        mesh=mesh,
        in_specs=placed,
        out_specs=(
            P("dp", "seq", None),
            P("dp", "seq", None),
            P("dp", None, "seq"),
            P("dp", None, "seq"),
            P("dp", None, "seq"),
        ),
        check_vma=False,
    )
```

```python
import functools

import jax
import jax.numpy as jnp
from jax import lax
from jax.experimental import pallas as pl
from jax.experimental.pallas import tpu as pltpu
from jax.sharding import PartitionSpec as P

beta_one = 0.9
beta_two = 0.95
learn_rate = 0.001
adam_eps = 1e-08
bias_one = 1.0 - 0.9**10
bias_two = 1.0 - 0.95**10
norm_eps = 1e-05
column_parts = 1

bf16 = jnp.bfloat16
f32 = jnp.float32


def cost(flops, moved):
    return pl.CostEstimate(flops=flops, bytes_accessed=moved, transcendentals=0)


def limit(mib):
    return pltpu.CompilerParams(vmem_limit_bytes=mib * 1024 * 1024)


def column_block(k, j, width, part=0, parts=1):
    seq = lax.axis_index("seq") ^ (k >> 1 << 1) ^ j
    x = (lax.axis_index("dp") % 2) ^ (k & 1)
    return pl.ds(pl.multiple_of(((seq * 2 + x) * parts + part) * width, width), width)


def norm_kernel(parts, tok_ref, gain_ref, grad_ref, *refs):
    out_refs = [refs[i : i + parts] for i in range(0, len(refs), parts)]
    chips = len(out_refs)
    feats = grad_ref.shape[-1]
    width = (out_refs[0][0].shape[-1] - feats) // 2
    tok = tok_ref[...].astype(f32)
    inv_rms = lax.rsqrt(jnp.mean(tok * tok, axis=-1, keepdims=True) + norm_eps)
    for k in (*range(1, chips), 0):
        for part in range(parts):
            out_ref = out_refs[k][part]
            for j in range(2):
                cols = column_block(k, j, width, part, parts)
                scaled = tok_ref[:, cols].astype(f32) * inv_rms
                out_ref[:, j * width : (j + 1) * width] = (scaled * gain_ref[:, cols]).astype(bf16)
            if part == 0:
                out_ref[:, 2 * width : 2 * width + feats] = grad_ref[...]


def norm_blocks(tokens, gain, grads, chips, width, parts):
    rows, model = tokens.shape
    feats = grads.shape[-1]
    step = min(rows, 32)
    lanes = [2 * width // parts + (feats if part == 0 else 0) for part in range(parts)]
    outs = pl.pallas_call(
        functools.partial(norm_kernel, parts),
        grid=(rows // step,),
        in_specs=[
            pl.BlockSpec((step, model), lambda i: (i, 0)),
            pl.BlockSpec((1, model), lambda i: (0, 0)),
            pl.BlockSpec((step, feats), lambda i: (i, 0)),
        ],
        out_specs=[pl.BlockSpec((step, n), lambda i: (i, 0)) for n in lanes] * chips,
        out_shape=[jax.ShapeDtypeStruct((rows, n), bf16) for n in lanes] * chips,
        compiler_params=limit(24),
        cost_estimate=cost(8 * rows * model, 4 * rows * model),
        name="norm_blocks",
    )(tokens, gain, grads)
    return [outs[i : i + parts] for i in range(0, len(outs), parts)]


def join_kernel(a_ref, b_ref, *refs):
    out_ref = refs[-1]
    half = a_ref.shape[0]
    out_ref[:half, :] = a_ref[...]
    out_ref[half:, :] = b_ref[...]


def join(a, b, after):
    rows, width = a.shape
    return pl.pallas_call(
        join_kernel,
        in_specs=[pl.BlockSpec(memory_space=pltpu.VMEM)] * 2
        + [pl.BlockSpec(memory_space=pl.ANY)] * len(after),
        out_shape=jax.ShapeDtypeStruct((2 * rows, width), a.dtype),
        compiler_params=limit(16),
        cost_estimate=cost(0, 8 * rows * width),
        name="join",
    )(a, b, *after)


def select_kernel(slots, owner_row_ref, owner_col_ref, out_ref):
    feats = owner_row_ref.shape[1]
    owner = owner_row_ref[...]
    lower = lax.broadcasted_iota(jnp.int32, (feats, feats), 0) < lax.broadcasted_iota(
        jnp.int32, (feats, feats), 1
    )
    same = (owner_col_ref[...] == owner) & lower
    place = jnp.sum(same.astype(f32), axis=0, keepdims=True).astype(jnp.int32)
    own_x = lax.axis_index("dp") % 2
    slot = (owner ^ own_x) * slots + place
    step = 256
    for at in range(0, out_ref.shape[0], step):
        index = at + lax.broadcasted_iota(jnp.int32, (step, feats), 0)
        out_ref[at : at + step, :] = (index == slot).astype(f32).astype(bf16)


def select_rows(owner, groups, slots):
    feats = owner.shape[0]
    return pl.pallas_call(
        functools.partial(select_kernel, slots),
        out_shape=jax.ShapeDtypeStruct((groups * slots, feats), bf16),
        compiler_params=limit(24),
        cost_estimate=cost(4 * groups * slots * feats, 2 * groups * slots * feats),
        name="select_rows",
    )(owner[None, :], owner[:, None])


def weight_kernel(planes, chips, plan, *refs):
    sel_ref, refs = refs[0], refs[1:]
    first, refs = refs[: 2 * chips], refs[2 * chips :]
    pieces, refs = refs[: 2 * chips], refs[2 * chips :]
    out_refs, (grads, held, base) = refs[-len(plan) - 4 : -3], refs[-3:]
    rows, feats = first[0].shape[0], sel_ref.shape[1]
    width = held.shape[1]
    block = sel_ref.shape[0] // planes
    z = lax.axis_index("dp") // 2
    for i in range(2 * chips):
        j = i // chips
        at = slice(i * rows, (i + 1) * rows)
        grads[at, :] = first[i][:, first[i].shape[1] - feats :]
        held[at, :] = pieces[i][:, j * width : (j + 1) * width]
    for at in range(0, feats, 256):
        base[at : at + 256, :] = lax.dot_general(
            grads[:, at : at + 256],
            held[...],
            (((0,), (0,)), ((), ())),
            preferred_element_type=f32,
        ).astype(bf16)

    def chosen(plane):
        at = pl.multiple_of(plane * block, block)
        return jnp.dot(sel_ref[pl.ds(at, block), :], base[...], preferred_element_type=f32)

    for (step, even), out_ref in zip(plan, out_refs):
        ahead = planes - step
        plane = jnp.where((z % 2 == 0) == even, z + ahead, z - ahead)

        @pl.when((plane >= 0) & (plane < planes))
        def _():
            out_ref[...] = chosen(plane).astype(bf16)

    out_refs[-1][...] = chosen(z).astype(bf16)


def weight_blocks(selected, first, pieces, planes, plan, after):
    chips = len(first) // 2
    slots_all, feats = selected.shape
    rows = first[0].shape[0]
    lanes = pieces[0].shape[1] - (feats if pieces[0] is first[0] else 0)
    width = lanes // 2
    total = 2 * chips * rows
    block = slots_all // planes
    return pl.pallas_call(
        functools.partial(weight_kernel, planes, chips, plan),
        in_specs=[pl.BlockSpec(memory_space=pltpu.VMEM)] * (1 + 4 * chips)
        + [pl.BlockSpec(memory_space=pl.ANY)] * len(after),
        out_shape=[jax.ShapeDtypeStruct((block, width), bf16)] * (len(plan) + 1),
        scratch_shapes=[
            pltpu.VMEM((total, feats), bf16),
            pltpu.VMEM((total, width), bf16),
            pltpu.VMEM((feats, width), bf16),
        ],
        compiler_params=limit(40),
        cost_estimate=cost(2 * (slots_all + total) * feats * width, 4 * total * width),
        name="weight_blocks",
    )(selected, *first, *pieces, *after)


def gather_weight(planes, piece_refs, held):
    dp = lax.axis_index("dp")
    own_x, own_z = dp % 2, dp // 2
    for j in range(2):
        for turn in range(planes):
            ref = piece_refs[j * planes + turn]
            share = ref.shape[0] // 2
            for i in range(2):
                at = pl.multiple_of(((own_z ^ turn) * 2 + (own_x ^ i)) * share, share)
                held[j, pl.ds(at, share), :] = ref[i * share : (i + 1) * share, :]


def back_kernel(planes, chips, parts, *refs):
    piece_refs, refs = refs[: chips * parts], refs[chips * parts :]
    weight_refs, refs = refs[: 2 * planes], refs[2 * planes :]
    out_refs, own_ref, held = refs[-chips - 2 : -2], refs[-2], refs[-1]
    _, feats, width = held.shape
    part_width = width // parts
    gather_weight(planes, weight_refs, held)
    dims = (((1,), (1,)), ((), ()))
    for k in (*range(1, chips), 0):
        pieces = piece_refs[k * parts : (k + 1) * parts]
        grads = pieces[0][:, pieces[0].shape[1] - feats :]
        total = None
        for j in range(2):
            out_refs[k][:, j * width : (j + 1) * width] = jnp.dot(
                grads, held[j], preferred_element_type=f32
            ).astype(bf16)
            for part in range(parts):
                term = lax.dot_general(
                    pieces[part][:, j * part_width : (j + 1) * part_width],
                    held[j, :, part * part_width : (part + 1) * part_width],
                    dims,
                    preferred_element_type=f32,
                )
                total = term if total is None else total + term
        if k == 0:
            own_ref[...] = total
        else:
            out_refs[k][:, 2 * width :] = total.astype(bf16)


def back_blocks(pieces, weights, planes, feats, after):
    chips, parts = len(pieces), len(pieces[0])
    rows = pieces[0][0].shape[0]
    width = weights[0].shape[-1]
    return pl.pallas_call(
        functools.partial(back_kernel, planes, chips, parts),
        in_specs=[pl.BlockSpec(memory_space=pltpu.VMEM)] * (chips * parts + 2 * planes)
        + [pl.BlockSpec(memory_space=pl.ANY)] * len(after),
        out_shape=[
            jax.ShapeDtypeStruct((rows, 2 * width + (feats if k else 0)), bf16)
            for k in range(chips)
        ]
        + [jax.ShapeDtypeStruct((rows, feats), f32)],
        scratch_shapes=[pltpu.VMEM((2, feats, width), bf16)],
        compiler_params=limit(40),
        cost_estimate=cost(8 * chips * rows * feats * width, 4 * chips * rows * width),
        name="back_blocks",
    )(*[p for piece in pieces for p in piece], *weights, *after)


def grad_x_kernel(tok_ref, gain_ref, part_ref, *refs):
    grad_refs, out_ref, values_ref = refs[:-2], refs[-2], refs[-1]
    model = tok_ref.shape[-1]
    width = grad_refs[0].shape[-1] // 2
    values = part_ref[...]
    for grad_ref in grad_refs[1:]:
        values += grad_ref[:, 2 * width :].astype(f32)
    values_ref[...] = values.astype(bf16)
    tok = tok_ref[...].astype(f32)
    inv_rms = lax.rsqrt(jnp.mean(tok * tok, axis=-1, keepdims=True) + norm_eps)
    total = jnp.zeros((tok.shape[0], 1), f32)
    for k, grad_ref in enumerate(grad_refs):
        for j in range(2):
            cols = column_block(k, j, width)
            weighted = gain_ref[:, cols] * grad_ref[:, j * width : (j + 1) * width].astype(f32)
            scaled = tok_ref[:, cols].astype(f32) * inv_rms
            total += jnp.sum(weighted * scaled, axis=-1, keepdims=True)
    mean = total / model
    for k, grad_ref in enumerate(grad_refs):
        for j in range(2):
            cols = column_block(k, j, width)
            weighted = gain_ref[:, cols] * grad_ref[:, j * width : (j + 1) * width].astype(f32)
            scaled = tok_ref[:, cols].astype(f32) * inv_rms
            out_ref[:, cols] = (inv_rms * (weighted - scaled * mean)).astype(bf16)


def grad_x_blocks(tokens, gain, part, grads):
    rows, model = tokens.shape
    feats = part.shape[-1]
    step = min(rows, 32)
    return pl.pallas_call(
        grad_x_kernel,
        grid=(rows // step,),
        in_specs=[
            pl.BlockSpec((step, model), lambda i: (i, 0)),
            pl.BlockSpec((1, model), lambda i: (0, 0)),
            pl.BlockSpec((step, feats), lambda i: (i, 0)),
        ]
        + [pl.BlockSpec((step, g.shape[1]), lambda i: (i, 0)) for g in grads],
        out_specs=[
            pl.BlockSpec((step, model), lambda i: (i, 0)),
            pl.BlockSpec((step, feats), lambda i: (i, 0)),
        ],
        out_shape=[
            jax.ShapeDtypeStruct((rows, model), bf16),
            jax.ShapeDtypeStruct((rows, feats), bf16),
        ],
        compiler_params=limit(24),
        cost_estimate=cost(16 * rows * model, 6 * rows * model),
        name="grad_x_blocks",
    )(tokens, gain, part, *grads)


def add_kernel(count, groups, *refs):
    for i, out_ref in enumerate(refs[-groups:]):
        total = refs[i * count][...].astype(f32)
        for ref in refs[i * count + 1 : (i + 1) * count]:
            total += ref[...].astype(f32)
        out_ref[...] = total.astype(out_ref.dtype)


def relay(sums, after):
    shape = sums[0][0].shape
    size = shape[0] * shape[1]
    return pl.pallas_call(
        functools.partial(add_kernel, len(sums[0]), len(sums)),
        in_specs=[pl.BlockSpec(memory_space=pltpu.VMEM)] * (len(sums) * len(sums[0]))
        + [pl.BlockSpec(memory_space=pl.ANY)] * len(after),
        out_shape=[jax.ShapeDtypeStruct(shape, bf16)] * len(sums),
        compiler_params=limit(16),
        cost_estimate=cost(2 * size, 12 * size),
        name="relay",
    )(*[a for group in sums for a in group], *after)


def finish_kernel(own_ref, even_ref, odd_ref, *refs):
    kept_ref, sent_ref = refs[-2:]
    half = kept_ref.shape[0]
    for part, out_ref in ((slice(half), kept_ref), (slice(half, 2 * half), sent_ref)):
        total = own_ref[part, :].astype(f32) + even_ref[part, :].astype(f32)
        out_ref[...] = (total + odd_ref[part, :].astype(f32)).astype(out_ref.dtype)


def finish(own, even, odd, after):
    height, width = own.shape
    return pl.pallas_call(
        finish_kernel,
        in_specs=[pl.BlockSpec(memory_space=pltpu.VMEM)] * 3
        + [pl.BlockSpec(memory_space=pl.ANY)] * len(after),
        out_shape=[
            jax.ShapeDtypeStruct((height // 2, width), f32),
            jax.ShapeDtypeStruct((height // 2, width), bf16),
        ],
        compiler_params=limit(16),
        cost_estimate=cost(2 * height * width, 9 * height * width),
        name="finish",
    )(own, even, odd, *after)


def adam_kernel(token_total, parts, owner_ref, *refs):
    kept_refs, got_refs, refs = refs[:parts], refs[parts : 2 * parts], refs[2 * parts :]
    master_ref, moment1_ref, moment2_ref = refs[:3]
    out_refs = refs[3:]
    step, width = kept_refs[0].shape
    dp = lax.axis_index("dp")
    owned = (owner_ref[...] == dp).astype(f32)
    count = jnp.sum(owned, axis=1, keepdims=True)
    index = pl.program_id(0) * step + lax.broadcasted_iota(jnp.int32, (step, 1), 0)
    occupied = (index.astype(f32) < count).astype(f32)
    for i, refs in enumerate((kept_refs, got_refs)):
        for part, ref in enumerate(refs):
            at = (((dp % 2) ^ i) * parts + part) * width
            cols = pl.ds(pl.multiple_of(at, width), width)
            slot_grad = ref[...].astype(f32) / token_total
            new_moment1 = (
                beta_one * moment1_ref[:, cols] + (1.0 - beta_one) * slot_grad
            ) * occupied
            new_moment2 = (
                beta_two * moment2_ref[:, cols] + (1.0 - beta_two) * slot_grad * slot_grad
            ) * occupied
            step_dir = new_moment1 / bias_one / (jnp.sqrt(new_moment2 / bias_two) + adam_eps)
            out_refs[0][:, cols] = (master_ref[:, cols] - learn_rate * step_dir) * occupied
            out_refs[1][:, cols] = new_moment1
            out_refs[2][:, cols] = new_moment2


def adam(owner, kept, got, states, token_total):
    slots, cols = states[0].shape
    width = kept[0].shape[-1]
    step = min(slots, 32)
    return pl.pallas_call(
        functools.partial(adam_kernel, token_total, len(kept)),
        grid=(slots // step,),
        in_specs=[pl.BlockSpec((1, owner.shape[0]), lambda i: (0, 0))]
        + [pl.BlockSpec((step, width), lambda i: (i, 0))] * (2 * len(kept))
        + [pl.BlockSpec((step, cols), lambda i: (i, 0))] * 3,
        out_specs=[pl.BlockSpec((step, cols), lambda i: (i, 0))] * 3,
        out_shape=[jax.ShapeDtypeStruct((slots, cols), f32)] * 3,
        compiler_params=limit(24),
        cost_estimate=cost(20 * slots * cols, 30 * slots * cols),
        name="adam",
    )(owner[None, :], *kept, *got, *states)


def on_device(groups, seqs, tokens, gain, w_t, grad_values, owner, master, moment1, moment2):
    planes = groups // 2
    chips = seqs
    parts = column_parts
    tokens, value_grad = tokens[0], grad_values[0]
    rows, model = tokens.shape
    feats = owner.shape[0]
    slots = master.shape[1]
    width = model // (2 * seqs)
    own_x = lax.axis_index("dp") % 2

    def permute(value, target):
        pairs = []
        for dp in range(groups):
            for seq in range(seqs):
                to = target(dp, seq)
                if to is not None:
                    pairs.append((dp * seqs + seq, to[0] * seqs + to[1]))
        return lax.ppermute(value, ("dp", "seq"), pairs)

    def to_chip(value, k):
        return permute(value, lambda dp, seq: (dp ^ (k & 1), seq ^ (k >> 1 << 1)))

    def to_core(value):
        return permute(value, lambda dp, seq: (dp, seq ^ 1))

    def to_x(value):
        return permute(value, lambda dp, seq: (dp ^ 1, seq))

    def to_plane(value, turn):
        return permute(value, lambda dp, seq: (dp ^ (2 * turn), seq))

    def busy(z, step, even):
        rightward = (z % 2 == 0) == even
        return z < step if rightward else planes - 1 - z < step

    def across(value, step, even):
        def target(dp, seq):
            z = dp // 2
            way = 1 if (z % 2 == 0) == even else -1
            return (dp + 2 * way, seq) if busy(z, step, even) else None

        return permute(value, target)

    w_keep = lax.dynamic_slice_in_dim(w_t, own_x * width, width, 1)
    w_got = to_x(lax.dynamic_slice_in_dim(w_t, (1 - own_x) * width, width, 1))
    gain_row = gain[None, :]
    sent = norm_blocks(tokens, gain_row, value_grad, chips, width, parts)
    near = [sent[0]] + [[to_chip(p, k) for p in sent[k]] for k in range(1, chips)]
    far = [[to_core(p) for p in piece] for piece in near]
    selected = select_rows(owner, groups, slots)

    w_plane = join(w_keep, w_got, (sent[0][0], selected))
    w_own = [w_plane] + [to_plane(w_plane, turn) for turn in range(1, planes)]
    weights = w_own + [to_core(w) for w in w_own]

    plan = [
        (step, even)
        for step in range(1, planes)
        for even in (True, False)
        if any(busy(z, step, even) for z in range(planes))
    ]
    kept, got = [], []
    first = [piece[0] for piece in near + far]
    for part in range(parts):
        pieces = [piece[part] for piece in near + far]
        after = weights if part == parts - 1 else []
        outs = weight_blocks(selected, first, pieces, planes, plan, after)
        ready = dict(zip(plan, outs))
        if part == parts - 1:
            back = back_blocks(near, weights, planes, feats, [outs[0]])
            home = [back[0]] + [to_chip(back[k], k) for k in range(1, chips)]
        held = {}
        for step in range(1, planes):
            here = [even for even in (True, False) if (step, even) in ready]
            send = [ready[step, even] for even in here]
            if held:
                sums = [[ready[step, even], held[not even]] for even in here if (not even) in held]
                sums = list(relay(sums, [back[0]] if step == 2 else home[-1:])) if sums else []
                send = []
                for even in here:
                    send.append(sums.pop(0) if (not even) in held else ready[step, even])
            held = {even: across(value, step, even) for even, value in zip(here, send)}
        keep, send = finish(outs[-1], held[True], held[False], home[1:])
        kept.append(keep)
        got.append(to_x(send))

    grad_x, values = grad_x_blocks(tokens, gain_row, back[-1], home)

    states = adam(owner, kept, got, (master[0], moment1[0], moment2[0]), rows * seqs * groups)
    return (values[None], grad_x[None], *(s[None] for s in states))


def solution(mesh):
    placed = (
        P("dp", "seq", None),
        P(),
        P("dp", "seq"),
        P("dp", "seq", None),
        P(),
        P("dp", None, "seq"),
        P("dp", None, "seq"),
        P("dp", None, "seq"),
    )
    return jax.shard_map(
        functools.partial(on_device, mesh.shape["dp"], mesh.shape["seq"]),
        mesh=mesh,
        in_specs=placed,
        out_specs=(
            P("dp", "seq", None),
            P("dp", "seq", None),
            P("dp", None, "seq"),
            P("dp", None, "seq"),
            P("dp", None, "seq"),
        ),
        check_vma=False,
    )
```

```python
import functools

import jax
import jax.numpy as jnp
from jax import lax
from jax.experimental import pallas as pl
from jax.experimental.pallas import tpu as pltpu
from jax.sharding import PartitionSpec as P

beta_one = 0.9
beta_two = 0.95
learn_rate = 0.001
adam_eps = 1e-08
bias_one = 1.0 - 0.9**10
bias_two = 1.0 - 0.95**10
norm_eps = 1e-05
column_parts = 1

bf16 = jnp.bfloat16
f32 = jnp.float32


def cost(flops, moved):
    return pl.CostEstimate(flops=flops, bytes_accessed=moved, transcendentals=0)


def limit(mib):
    return pltpu.CompilerParams(vmem_limit_bytes=mib * 1024 * 1024)


def column_block(k, j, width, part=0, parts=1):
    seq = lax.axis_index("seq") ^ (k >> 1 << 1) ^ j
    x = (lax.axis_index("dp") % 2) ^ (k & 1)
    return pl.ds(pl.multiple_of(((seq * 2 + x) * parts + part) * width, width), width)


def norm_kernel(parts, tok_ref, far_ref, gain_ref, *refs):
    out_refs = [refs[i : i + parts] for i in range(0, len(refs), parts)]
    chips = len(out_refs)
    width = out_refs[0][0].shape[-1]
    for i, ref in enumerate((tok_ref, far_ref)):
        tok = ref[...].astype(f32)
        inv_rms = lax.rsqrt(jnp.mean(tok * tok, axis=-1, keepdims=True) + norm_eps)
        for k in (*range(1, chips), 0):
            for part in range(parts):
                cols = column_block(k, 0, width, part, parts)
                scaled = ref[:, cols].astype(f32) * inv_rms
                out_refs[k][part][i] = (scaled * gain_ref[:, cols]).astype(bf16)


def norm_blocks(tokens, far, gain, chips, width, parts):
    rows, model = tokens.shape
    step = min(rows, 32)
    outs = pl.pallas_call(
        functools.partial(norm_kernel, parts),
        grid=(rows // step,),
        in_specs=[
            pl.BlockSpec((step, model), lambda i: (i, 0)),
            pl.BlockSpec((step, model), lambda i: (i, 0)),
            pl.BlockSpec((1, model), lambda i: (0, 0)),
        ],
        out_specs=[pl.BlockSpec((2, step, width // parts), lambda i: (0, i, 0))] * (chips * parts),
        out_shape=[jax.ShapeDtypeStruct((2, rows, width // parts), bf16)] * (chips * parts),
        compiler_params=limit(24),
        cost_estimate=cost(8 * rows * model, 6 * rows * model),
        name="norm_blocks",
    )(tokens, far, gain)
    return [outs[i : i + parts] for i in range(0, len(outs), parts)]


def pack_kernel(w_ref, grad_ref, keep_ref, send_ref):
    share, width = keep_ref.shape
    rows, feats = grad_ref.shape
    own_x = lax.axis_index("dp") % 2
    keep_ref[...] = w_ref[:, pl.ds(pl.multiple_of(own_x * width, width), width)]
    send_ref[:share, :] = w_ref[:, pl.ds(pl.multiple_of((1 - own_x) * width, width), width)]
    pieces = feats // width if feats > width else 1
    for at in range(0, rows * pieces, rows):
        send_ref[share + at : share + at + rows, : feats // pieces] = grad_ref[
            :, at // rows * width : at // rows * width + feats // pieces
        ]


def pack(w_t, grads, width):
    share, (rows, feats) = w_t.shape[0], grads.shape
    pieces = max(feats // width, 1)
    return pl.pallas_call(
        pack_kernel,
        out_shape=[
            jax.ShapeDtypeStruct((share, width), bf16),
            jax.ShapeDtypeStruct((share + pieces * rows, width), bf16),
        ],
        compiler_params=limit(16),
        cost_estimate=cost(0, 8 * rows * feats),
        name="pack",
    )(w_t, grads)


def unpack_kernel(keep_ref, got_ref, *refs):
    plane_ref, grads_ref = refs[-2:]
    chips = grads_ref.shape[0] // refs[0].shape[0]
    share, width = keep_ref.shape
    rows, feats = refs[0].shape
    plane_ref[:share, :] = keep_ref[...]
    plane_ref[share:, :] = got_ref[:share, :]
    for k in range(chips):
        at = slice(k * rows, (k + 1) * rows)
        if k != 1:
            grads_ref[at, :] = refs[k - (k > 1)][...]
            continue
        pieces = feats // width if feats > width else 1
        lanes = feats // pieces
        for i in range(pieces):
            part = got_ref[share + i * rows : share + (i + 1) * rows, :lanes]
            grads_ref[at, i * lanes : (i + 1) * lanes] = part


def unpack(keep, got, grads, after):
    share, width = keep.shape
    rows, feats = grads[0].shape
    return pl.pallas_call(
        unpack_kernel,
        in_specs=[pl.BlockSpec(memory_space=pltpu.VMEM)] * (2 + len(grads))
        + [pl.BlockSpec(memory_space=pl.ANY)] * len(after),
        out_shape=[
            jax.ShapeDtypeStruct((2 * share, width), bf16),
            jax.ShapeDtypeStruct(((len(grads) + 1) * rows, feats), bf16),
        ],
        compiler_params=limit(16),
        cost_estimate=cost(0, 0),
        name="unpack",
    )(keep, got, *grads, *after)


def select_kernel(groups, slots, owner_ref, *refs):
    out_ref = refs[-1]
    feats = owner_ref.shape[1]
    owner = owner_ref[...]
    lower = lax.broadcasted_iota(jnp.int32, (feats, feats), 0) < lax.broadcasted_iota(
        jnp.int32, (feats, feats), 1
    )
    owned = (lax.broadcasted_iota(jnp.int32, (groups, feats), 0) == owner).astype(f32)
    before = jnp.dot(
        owned.astype(bf16), lower.astype(f32).astype(bf16), preferred_element_type=f32
    )
    place = jnp.sum(owned * before, axis=0, keepdims=True).astype(jnp.int32)
    own_x = lax.axis_index("dp") % 2
    slot = (owner ^ own_x) * slots + place
    step = 256
    for at in range(0, out_ref.shape[0], step):
        index = at + lax.broadcasted_iota(jnp.int32, (step, feats), 0)
        out_ref[at : at + step, :] = (index == slot).astype(f32).astype(bf16)


def select_rows(owner, groups, slots, after):
    feats = owner.shape[1]
    return pl.pallas_call(
        functools.partial(select_kernel, groups, slots),
        in_specs=[pl.BlockSpec(memory_space=pltpu.VMEM)]
        + [pl.BlockSpec(memory_space=pl.ANY)] * len(after),
        out_shape=jax.ShapeDtypeStruct((groups * slots, feats), bf16),
        compiler_params=limit(24),
        cost_estimate=cost(4 * groups * slots * feats, 2 * groups * slots * feats),
        name="select_rows",
    )(owner, *after)


def weight_kernel(planes, chips, plan, *refs):
    sel_ref, refs = refs[0], refs[1:]
    grad_refs, refs = refs[:2], refs[2:]
    pieces, refs = refs[:chips], refs[chips:]
    out_refs, (held, base) = refs[-len(plan) - 3 : -2], refs[-2:]
    rows = pieces[0].shape[1]
    feats = sel_ref.shape[1]
    block = sel_ref.shape[0] // planes
    z = lax.axis_index("dp") // 2
    for k in range(chips):
        for i in range(2):
            held[i, k * rows : (k + 1) * rows, :] = pieces[k][i]
    for at in range(0, feats, 256):
        total = None
        for i in range(2):
            term = lax.dot_general(
                grad_refs[i][:, at : at + 256],
                held[i],
                (((0,), (0,)), ((), ())),
                preferred_element_type=f32,
            )
            total = term if total is None else total + term
        base[at : at + 256, :] = total.astype(bf16)

    def chosen(plane):
        at = pl.multiple_of(plane * block, block)
        return jnp.dot(sel_ref[pl.ds(at, block), :], base[...], preferred_element_type=f32)

    for (step, even), out_ref in zip(plan, out_refs):
        ahead = planes - step
        plane = jnp.where((z % 2 == 0) == even, z + ahead, z - ahead)

        @pl.when((plane >= 0) & (plane < planes))
        def _():
            out_ref[...] = chosen(plane).astype(bf16)

    out_refs[-1][...] = chosen(z).astype(bf16)


def weight_blocks(selected, grads, pieces, planes, plan, after):
    chips = len(pieces)
    slots_all, feats = selected.shape
    _, rows, width = pieces[0].shape
    total = 2 * chips * rows
    block = slots_all // planes
    return pl.pallas_call(
        functools.partial(weight_kernel, planes, chips, plan),
        in_specs=[pl.BlockSpec(memory_space=pltpu.VMEM)] * (3 + chips)
        + [pl.BlockSpec(memory_space=pl.ANY)] * len(after),
        out_shape=[jax.ShapeDtypeStruct((block, width), bf16)] * (len(plan) + 1),
        scratch_shapes=[
            pltpu.VMEM((2, total // 2, width), bf16),
            pltpu.VMEM((feats, width), bf16),
        ],
        compiler_params=limit(40),
        cost_estimate=cost(2 * (slots_all + total) * feats * width, 4 * total * width),
        name="weight_blocks",
    )(selected, *grads, *pieces, *after)


def gather_weight(piece_refs, held):
    dp = lax.axis_index("dp")
    own_x, own_z = dp % 2, dp // 2
    for turn, ref in enumerate(piece_refs):
        share = ref.shape[0] // 2
        for i in range(2):
            at = pl.multiple_of(((own_z ^ turn) * 2 + (own_x ^ i)) * share, share)
            held[pl.ds(at, share), :] = ref[i * share : (i + 1) * share, :]


def back_kernel(planes, chips, parts, grads_ref, far_ref, *refs):
    piece_refs, refs = refs[: chips * parts], refs[chips * parts :]
    (*far_refs, far_value_ref, out_ref, value_ref), held = refs[-6:-1], refs[-1]
    rows = grads_ref.shape[0] // chips
    feats, width = held.shape
    part_width = width // parts
    gather_weight(refs[:planes], held)
    for core in (1, 0):
        for k in range(chips):
            at = slice(k * rows, (k + 1) * rows)
            from_ref = far_ref if core else grads_ref
            block = jnp.dot(from_ref[at, :], held[...], preferred_element_type=f32).astype(bf16)
            if core:
                half = chips // 2
                far_refs[k // half][k % half * rows : (k % half + 1) * rows, :] = block
            else:
                out_ref[at, :] = block
            total = None
            for part in range(parts):
                term = lax.dot_general(
                    piece_refs[k * parts + part][core],
                    held[:, part * part_width : (part + 1) * part_width],
                    (((1,), (1,)), ((), ())),
                    preferred_element_type=f32,
                )
                total = term if total is None else total + term
            (far_value_ref if core else value_ref)[at, :] = total.astype(bf16)


def back_blocks(grads, grads_far, pieces, weights, after):
    chips, parts = len(pieces), len(pieces[0])
    rows, feats = grads.shape[0] // chips, grads.shape[1]
    width = weights[0].shape[-1]
    half = jax.ShapeDtypeStruct((chips // 2 * rows, width), bf16)
    value = jax.ShapeDtypeStruct((chips * rows, feats), bf16)
    outs = pl.pallas_call(
        functools.partial(back_kernel, len(weights), chips, parts),
        in_specs=[pl.BlockSpec(memory_space=pltpu.VMEM)] * (2 + chips * parts + len(weights))
        + [pl.BlockSpec(memory_space=pl.ANY)] * len(after),
        out_shape=[half, half, value, jax.ShapeDtypeStruct((chips * rows, width), bf16), value],
        scratch_shapes=[pltpu.VMEM((feats, width), bf16)],
        compiler_params=limit(40),
        name="back_blocks",
    )(grads, grads_far, *[p for piece in pieces for p in piece], *weights, *after)
    return outs[:3], outs[3:]


def home_kernel(own_ref, own_value_ref, got_a_ref, got_b_ref, got_value_ref, *out_refs):
    chips = len(out_refs) - 1
    rows = out_refs[0].shape[0]
    width = out_refs[0].shape[1] // 2
    half = chips // 2
    for k in range(chips):
        at = slice(k * rows, (k + 1) * rows)
        got_ref = got_b_ref if k // half else got_a_ref
        out_refs[k][:, :width] = own_ref[at, :]
        out_refs[k][:, width : 2 * width] = got_ref[k % half * rows : (k % half + 1) * rows, :]
        values = own_value_ref[at, :].astype(f32) + got_value_ref[at, :].astype(f32)
        if k == 0:
            out_refs[-1][...] = values
        else:
            out_refs[k][:, 2 * width :] = values.astype(bf16)


def home_blocks(own, got, chips):
    rows, width = own[0].shape[0] // chips, own[0].shape[1]
    feats = own[1].shape[1]
    return pl.pallas_call(
        home_kernel,
        out_shape=[
            jax.ShapeDtypeStruct((rows, 2 * width + (feats if k else 0)), bf16)
            for k in range(chips)
        ]
        + [jax.ShapeDtypeStruct((rows, feats), f32)],
        compiler_params=limit(24),
        name="home_blocks",
    )(*own, *got)


def grad_x_kernel(tok_ref, gain_ref, part_ref, *refs):
    grad_refs, out_ref, values_ref = refs[:-2], refs[-2], refs[-1]
    model = tok_ref.shape[-1]
    width = grad_refs[0].shape[-1] // 2
    values = part_ref[...]
    for grad_ref in grad_refs[1:]:
        values += grad_ref[:, 2 * width :].astype(f32)
    values_ref[...] = values.astype(bf16)
    tok = tok_ref[...].astype(f32)
    inv_rms = lax.rsqrt(jnp.mean(tok * tok, axis=-1, keepdims=True) + norm_eps)
    total = jnp.zeros((tok.shape[0], 1), f32)
    for k, grad_ref in enumerate(grad_refs):
        for j in range(2):
            cols = column_block(k, j, width)
            weighted = gain_ref[:, cols] * grad_ref[:, j * width : (j + 1) * width].astype(f32)
            scaled = tok_ref[:, cols].astype(f32) * inv_rms
            total += jnp.sum(weighted * scaled, axis=-1, keepdims=True)
    mean = total / model
    for k, grad_ref in enumerate(grad_refs):
        for j in range(2):
            cols = column_block(k, j, width)
            weighted = gain_ref[:, cols] * grad_ref[:, j * width : (j + 1) * width].astype(f32)
            scaled = tok_ref[:, cols].astype(f32) * inv_rms
            out_ref[:, cols] = (inv_rms * (weighted - scaled * mean)).astype(bf16)


def grad_x_blocks(tokens, gain, part, grads):
    rows, model = tokens.shape
    feats = part.shape[-1]
    step = min(rows, 32)
    return pl.pallas_call(
        grad_x_kernel,
        grid=(rows // step,),
        in_specs=[
            pl.BlockSpec((step, model), lambda i: (i, 0)),
            pl.BlockSpec((1, model), lambda i: (0, 0)),
            pl.BlockSpec((step, feats), lambda i: (i, 0)),
        ]
        + [pl.BlockSpec((step, g.shape[1]), lambda i: (i, 0)) for g in grads],
        out_specs=[
            pl.BlockSpec((step, model), lambda i: (i, 0)),
            pl.BlockSpec((step, feats), lambda i: (i, 0)),
        ],
        out_shape=[
            jax.ShapeDtypeStruct((rows, model), bf16),
            jax.ShapeDtypeStruct((rows, feats), bf16),
        ],
        compiler_params=limit(24),
        cost_estimate=cost(16 * rows * model, 6 * rows * model),
        name="grad_x_blocks",
    )(tokens, gain, part, *grads)


def add_kernel(count, groups, *refs):
    for i, out_ref in enumerate(refs[-groups:]):
        total = refs[i * count][...].astype(f32)
        for ref in refs[i * count + 1 : (i + 1) * count]:
            total += ref[...].astype(f32)
        out_ref[...] = total.astype(out_ref.dtype)


def relay(sums, after):
    shape = sums[0][0].shape
    size = shape[0] * shape[1]
    return pl.pallas_call(
        functools.partial(add_kernel, len(sums[0]), len(sums)),
        in_specs=[pl.BlockSpec(memory_space=pltpu.VMEM)] * (len(sums) * len(sums[0]))
        + [pl.BlockSpec(memory_space=pl.ANY)] * len(after),
        out_shape=[jax.ShapeDtypeStruct(shape, bf16)] * len(sums),
        compiler_params=limit(16),
        cost_estimate=cost(2 * size, 12 * size),
        name="relay",
    )(*[a for group in sums for a in group], *after)


def finish_kernel(own_ref, even_ref, odd_ref, *refs):
    kept_ref, sent_ref = refs[-2:]
    half = kept_ref.shape[0]
    for part, out_ref in ((slice(half), kept_ref), (slice(half, 2 * half), sent_ref)):
        total = own_ref[part, :].astype(f32) + even_ref[part, :].astype(f32)
        out_ref[...] = (total + odd_ref[part, :].astype(f32)).astype(out_ref.dtype)


def finish(own, even, odd, after):
    height, width = own.shape
    return pl.pallas_call(
        finish_kernel,
        in_specs=[pl.BlockSpec(memory_space=pltpu.VMEM)] * 3
        + [pl.BlockSpec(memory_space=pl.ANY)] * len(after),
        out_shape=[
            jax.ShapeDtypeStruct((height // 2, width), f32),
            jax.ShapeDtypeStruct((height // 2, width), bf16),
        ],
        compiler_params=limit(16),
        cost_estimate=cost(2 * height * width, 9 * height * width),
        name="finish",
    )(own, even, odd, *after)


def adam_kernel(token_total, parts, owner_ref, *refs):
    kept_refs, got_refs, refs = refs[:parts], refs[parts : 2 * parts], refs[2 * parts :]
    master_ref, moment1_ref, moment2_ref = refs[:3]
    out_refs = refs[3:]
    step, width = kept_refs[0].shape
    dp = lax.axis_index("dp")
    owned = (owner_ref[...] == dp).astype(f32)
    count = jnp.sum(owned, axis=1, keepdims=True)
    index = pl.program_id(0) * step + lax.broadcasted_iota(jnp.int32, (step, 1), 0)
    occupied = (index.astype(f32) < count).astype(f32)
    for i, refs in enumerate((kept_refs, got_refs)):
        for part, ref in enumerate(refs):
            at = (((dp % 2) ^ i) * parts + part) * width
            cols = pl.ds(pl.multiple_of(at, width), width)
            slot_grad = ref[...].astype(f32) / token_total
            new_moment1 = (
                beta_one * moment1_ref[:, cols] + (1.0 - beta_one) * slot_grad
            ) * occupied
            new_moment2 = (
                beta_two * moment2_ref[:, cols] + (1.0 - beta_two) * slot_grad * slot_grad
            ) * occupied
            step_dir = new_moment1 / bias_one / (jnp.sqrt(new_moment2 / bias_two) + adam_eps)
            out_refs[0][:, cols] = (master_ref[:, cols] - learn_rate * step_dir) * occupied
            out_refs[1][:, cols] = new_moment1
            out_refs[2][:, cols] = new_moment2


def adam(owner, kept, got, states, token_total):
    slots, cols = states[0].shape
    width = kept[0].shape[-1]
    step = min(slots, 32)
    return pl.pallas_call(
        functools.partial(adam_kernel, token_total, len(kept)),
        grid=(slots // step,),
        in_specs=[pl.BlockSpec(owner.shape, lambda i: (0, 0))]
        + [pl.BlockSpec((step, width), lambda i: (i, 0))] * (2 * len(kept))
        + [pl.BlockSpec((step, cols), lambda i: (i, 0))] * 3,
        out_specs=[pl.BlockSpec((step, cols), lambda i: (i, 0))] * 3,
        out_shape=[jax.ShapeDtypeStruct((slots, cols), f32)] * 3,
        compiler_params=limit(24),
        cost_estimate=cost(20 * slots * cols, 30 * slots * cols),
        name="adam",
    )(owner, *kept, *got, *states)


def on_device(groups, seqs, tokens, gain, w_t, grad_values, owner, master, moment1, moment2):
    planes = groups // 2
    chips = seqs
    parts = column_parts
    tokens, value_grad = tokens[0], grad_values[0]
    rows, model = tokens.shape
    feats = owner.shape[0]
    slots = master.shape[1]
    width = model // (2 * seqs)
    own_x = lax.axis_index("dp") % 2

    def permute(value, target):
        pairs = []
        for dp in range(groups):
            for seq in range(seqs):
                to = target(dp, seq)
                if to is not None:
                    pairs.append((dp * seqs + seq, to[0] * seqs + to[1]))
        return lax.ppermute(value, ("dp", "seq"), pairs)

    def to_chip(value, k):
        return permute(value, lambda dp, seq: (dp ^ (k & 1), seq ^ (k >> 1 << 1)))

    def to_core(value):
        return permute(value, lambda dp, seq: (dp, seq ^ 1))

    def to_x(value):
        return permute(value, lambda dp, seq: (dp ^ 1, seq))

    def to_plane(value, turn):
        return permute(value, lambda dp, seq: (dp ^ (2 * turn), seq))

    def busy(z, step, even):
        rightward = (z % 2 == 0) == even
        return z < step if rightward else planes - 1 - z < step

    def across(value, step, even):
        def target(dp, seq):
            z = dp // 2
            way = 1 if (z % 2 == 0) == even else -1
            return (dp + 2 * way, seq) if busy(z, step, even) else None

        return permute(value, target)

    tokens_far = to_core(tokens)
    w_keep, packed = pack(w_t, value_grad, width)
    packed = to_chip(packed, 1)
    grads = [to_chip(value_grad, k) for k in range(chips - 1, 1, -1)][::-1]

    gain_row, owner_row = gain[None, :], owner[None, :]
    sent = norm_blocks(tokens, tokens_far, gain_row, chips, width, parts)
    w_plane, grads = unpack(w_keep, packed, [value_grad] + grads, (sent[0][0],))
    pieces = [sent[0]] + [[to_chip(p, k) for p in sent[k]] for k in range(1, chips)]
    grads_far = to_core(grads)
    selected = select_rows(owner_row, groups, slots, (sent[0][0],))

    weights = [w_plane] + [to_plane(w_plane, turn) for turn in range(1, planes)]

    plan = [
        (step, even)
        for step in range(1, planes)
        for even in (True, False)
        if any(busy(z, step, even) for z in range(planes))
    ]
    kept, got = [], []
    for part in range(parts):
        outs = weight_blocks(
            selected,
            [grads, grads_far],
            [piece[part] for piece in pieces],
            planes,
            plan,
            weights if part == parts - 1 else [],
        )
        ready = dict(zip(plan, outs))
        if part == parts - 1:
            back_far, back_own = back_blocks(grads, grads_far, pieces, weights, [outs[0]])
            back = home_blocks(back_own, [to_core(b) for b in back_far], chips)
            home = [back[0]] + [to_chip(back[k], k) for k in range(1, chips)]
        held = {}
        for step in range(1, planes):
            here = [even for even in (True, False) if (step, even) in ready]
            send = [ready[step, even] for even in here]
            if held:
                sums = [[ready[step, even], held[not even]] for even in here if (not even) in held]
                sums = list(relay(sums, back_own[:1] if step == 2 else [back[0]])) if sums else []
                send = []
                for even in here:
                    send.append(sums.pop(0) if (not even) in held else ready[step, even])
            held = {even: across(value, step, even) for even, value in zip(here, send)}
        keep, send = finish(outs[-1], held[True], held[False], home[-1:])
        kept.append(keep)
        got.append(to_x(send))

    grad_x, values = grad_x_blocks(tokens, gain_row, back[-1], home)

    states = adam(owner_row, kept, got, (master[0], moment1[0], moment2[0]), rows * seqs * groups)
    return (values[None], grad_x[None], *(s[None] for s in states))


def solution(mesh):
    placed = (
        P("dp", "seq", None),
        P(),
        P("dp", "seq"),
        P("dp", "seq", None),
        P(),
        P("dp", None, "seq"),
        P("dp", None, "seq"),
        P("dp", None, "seq"),
    )
    return jax.shard_map(
        functools.partial(on_device, mesh.shape["dp"], mesh.shape["seq"]),
        mesh=mesh,
        in_specs=placed,
        out_specs=(
            P("dp", "seq", None),
            P("dp", "seq", None),
            P("dp", None, "seq"),
            P("dp", None, "seq"),
            P("dp", None, "seq"),
        ),
        check_vma=False,
    )
```

```python
import functools

import jax
import jax.numpy as jnp
from jax import lax
from jax.experimental import pallas as pl
from jax.experimental.pallas import tpu as pltpu
from jax.sharding import PartitionSpec as P

beta_one = 0.9
beta_two = 0.95
learn_rate = 0.001
adam_eps = 1e-08
bias_one = 1.0 - 0.9**10
bias_two = 1.0 - 0.95**10
norm_eps = 1e-05
column_parts = 1

bf16 = jnp.bfloat16
f32 = jnp.float32


def cost(flops, moved):
    return pl.CostEstimate(flops=flops, bytes_accessed=moved, transcendentals=0)


def limit(mib):
    return pltpu.CompilerParams(vmem_limit_bytes=mib * 1024 * 1024)


def column_block(k, j, width, part=0, parts=1):
    seq = lax.axis_index("seq") ^ (k >> 1 << 1) ^ j
    x = (lax.axis_index("dp") % 2) ^ (k & 1)
    return pl.ds(pl.multiple_of(((seq * 2 + x) * parts + part) * width, width), width)


def norm_kernel(parts, tok_ref, far_ref, gain_ref, *refs):
    out_refs = [refs[i : i + parts] for i in range(0, len(refs), parts)]
    chips = len(out_refs)
    width = out_refs[0][0].shape[-1]
    for i, ref in enumerate((tok_ref, far_ref)):
        tok = ref[...].astype(f32)
        inv_rms = lax.rsqrt(jnp.mean(tok * tok, axis=-1, keepdims=True) + norm_eps)
        for k in (*range(1, chips), 0):
            for part in range(parts):
                cols = column_block(k, 0, width, part, parts)
                scaled = ref[:, cols].astype(f32) * inv_rms
                out_refs[k][part][i] = (scaled * gain_ref[:, cols]).astype(bf16)


def norm_blocks(tokens, far, gain, chips, width, parts):
    rows, model = tokens.shape
    step = min(rows, 32)
    outs = pl.pallas_call(
        functools.partial(norm_kernel, parts),
        grid=(rows // step,),
        in_specs=[
            pl.BlockSpec((step, model), lambda i: (i, 0)),
            pl.BlockSpec((step, model), lambda i: (i, 0)),
            pl.BlockSpec((1, model), lambda i: (0, 0)),
        ],
        out_specs=[pl.BlockSpec((2, step, width // parts), lambda i: (0, i, 0))] * (chips * parts),
        out_shape=[jax.ShapeDtypeStruct((2, rows, width // parts), bf16)] * (chips * parts),
        compiler_params=limit(24),
        cost_estimate=cost(8 * rows * model, 6 * rows * model),
        name="norm_blocks",
    )(tokens, far, gain)
    return [outs[i : i + parts] for i in range(0, len(outs), parts)]


def late_kernel(a_ref, *refs):
    refs[-1][...] = a_ref[...]


def late(a, after):
    return pl.pallas_call(
        late_kernel,
        in_specs=[pl.BlockSpec(memory_space=pltpu.VMEM)]
        + [pl.BlockSpec(memory_space=pl.ANY)] * len(after),
        out_shape=jax.ShapeDtypeStruct(a.shape, a.dtype),
        compiler_params=limit(16),
        name="late",
    )(a, *after)


def halves_kernel(w_ref, keep_ref, send_ref):
    width = keep_ref.shape[1]
    own_x = lax.axis_index("dp") % 2
    keep_ref[...] = w_ref[:, pl.ds(pl.multiple_of(own_x * width, width), width)]
    send_ref[...] = w_ref[:, pl.ds(pl.multiple_of((1 - own_x) * width, width), width)]


def halves(w_t, width):
    return pl.pallas_call(
        halves_kernel,
        out_shape=[jax.ShapeDtypeStruct((w_t.shape[0], width), bf16)] * 2,
        compiler_params=limit(16),
        name="halves",
    )(w_t)


def unpack_kernel(keep_ref, got_ref, *refs):
    plane_ref, grads_ref = refs[-2:]
    share = keep_ref.shape[0]
    rows = refs[0].shape[0]
    plane_ref[:share, :] = keep_ref[...]
    plane_ref[share:, :] = got_ref[...]
    for k in range(grads_ref.shape[0] // rows):
        grads_ref[k * rows : (k + 1) * rows, :] = refs[k][...]


def unpack(keep, got, grads, after):
    share, width = keep.shape
    rows, feats = grads[0].shape
    return pl.pallas_call(
        unpack_kernel,
        in_specs=[pl.BlockSpec(memory_space=pltpu.VMEM)] * (2 + len(grads))
        + [pl.BlockSpec(memory_space=pl.ANY)] * len(after),
        out_shape=[
            jax.ShapeDtypeStruct((2 * share, width), bf16),
            jax.ShapeDtypeStruct((len(grads) * rows, feats), bf16),
        ],
        compiler_params=limit(16),
        name="unpack",
    )(keep, got, *grads, *after)


def select_kernel(groups, slots, owner_ref, *refs):
    out_ref = refs[-1]
    feats = owner_ref.shape[1]
    owner = owner_ref[...]
    lower = lax.broadcasted_iota(jnp.int32, (feats, feats), 0) < lax.broadcasted_iota(
        jnp.int32, (feats, feats), 1
    )
    owned = (lax.broadcasted_iota(jnp.int32, (groups, feats), 0) == owner).astype(f32)
    before = jnp.dot(
        owned.astype(bf16), lower.astype(f32).astype(bf16), preferred_element_type=f32
    )
    place = jnp.sum(owned * before, axis=0, keepdims=True).astype(jnp.int32)
    own_x = lax.axis_index("dp") % 2
    slot = (owner ^ own_x) * slots + place
    step = 256
    for at in range(0, out_ref.shape[0], step):
        index = at + lax.broadcasted_iota(jnp.int32, (step, feats), 0)
        out_ref[at : at + step, :] = (index == slot).astype(f32).astype(bf16)


def select_rows(owner, groups, slots, after):
    feats = owner.shape[1]
    return pl.pallas_call(
        functools.partial(select_kernel, groups, slots),
        in_specs=[pl.BlockSpec(memory_space=pltpu.VMEM)]
        + [pl.BlockSpec(memory_space=pl.ANY)] * len(after),
        out_shape=jax.ShapeDtypeStruct((groups * slots, feats), bf16),
        compiler_params=limit(24),
        cost_estimate=cost(4 * groups * slots * feats, 2 * groups * slots * feats),
        name="select_rows",
    )(owner, *after)


def weight_kernel(planes, chips, plan, *refs):
    sel_ref, refs = refs[0], refs[1:]
    grad_refs, refs = refs[:2], refs[2:]
    pieces, refs = refs[:chips], refs[chips:]
    out_refs, (held, base) = refs[-len(plan) - 3 : -2], refs[-2:]
    rows = pieces[0].shape[1]
    feats = sel_ref.shape[1]
    block = sel_ref.shape[0] // planes
    z = lax.axis_index("dp") // 2
    for k in range(chips):
        for i in range(2):
            held[i, k * rows : (k + 1) * rows, :] = pieces[k][i]
    for at in range(0, feats, 256):
        total = None
        for i in range(2):
            term = lax.dot_general(
                grad_refs[i][:, at : at + 256],
                held[i],
                (((0,), (0,)), ((), ())),
                preferred_element_type=f32,
            )
            total = term if total is None else total + term
        base[at : at + 256, :] = total.astype(bf16)

    def chosen(plane):
        at = pl.multiple_of(plane * block, block)
        return jnp.dot(sel_ref[pl.ds(at, block), :], base[...], preferred_element_type=f32)

    for (step, even), out_ref in zip(plan, out_refs):
        ahead = planes - step
        plane = jnp.where((z % 2 == 0) == even, z + ahead, z - ahead)

        @pl.when((plane >= 0) & (plane < planes))
        def _():
            out_ref[...] = chosen(plane).astype(bf16)

    out_refs[-1][...] = chosen(z).astype(bf16)


def weight_blocks(selected, grads, pieces, planes, plan, after):
    chips = len(pieces)
    slots_all, feats = selected.shape
    _, rows, width = pieces[0].shape
    total = 2 * chips * rows
    block = slots_all // planes
    return pl.pallas_call(
        functools.partial(weight_kernel, planes, chips, plan),
        in_specs=[pl.BlockSpec(memory_space=pltpu.VMEM)] * (3 + chips)
        + [pl.BlockSpec(memory_space=pl.ANY)] * len(after),
        out_shape=[jax.ShapeDtypeStruct((block, width), bf16)] * (len(plan) + 1),
        scratch_shapes=[
            pltpu.VMEM((2, total // 2, width), bf16),
            pltpu.VMEM((feats, width), bf16),
        ],
        compiler_params=limit(40),
        cost_estimate=cost(2 * (slots_all + total) * feats * width, 4 * total * width),
        name="weight_blocks",
    )(selected, *grads, *pieces, *after)


def gather_weight(piece_refs, held):
    dp = lax.axis_index("dp")
    own_x, own_z = dp % 2, dp // 2
    for turn, ref in enumerate(piece_refs):
        share = ref.shape[0] // 2
        for i in range(2):
            at = pl.multiple_of(((own_z ^ turn) * 2 + (own_x ^ i)) * share, share)
            held[pl.ds(at, share), :] = ref[i * share : (i + 1) * share, :]


def value_kernel(planes, chips, parts, *refs):
    piece_refs, refs = refs[: chips * parts], refs[chips * parts :]
    far_refs, out_ref, held = refs[-4:-2], refs[-2], refs[-1]
    rows = out_ref.shape[0] // chips
    half = chips // 2
    part_width = held.shape[1] // parts
    gather_weight(refs[:planes], held)
    for core in (1, 0):
        for k in range(chips):
            total = None
            for part in range(parts):
                term = lax.dot_general(
                    piece_refs[k * parts + part][core],
                    held[:, part * part_width : (part + 1) * part_width],
                    (((1,), (1,)), ((), ())),
                    preferred_element_type=f32,
                )
                total = term if total is None else total + term
            if core:
                at = k % half * rows
                far_refs[k // half][at : at + rows, :] = total.astype(bf16)
            else:
                out_ref[k * rows : (k + 1) * rows, :] = total


def value_parts(pieces, weights, feats, after):
    chips, parts = len(pieces), len(pieces[0])
    rows = pieces[0][0].shape[1]
    width = weights[0].shape[-1]
    return pl.pallas_call(
        functools.partial(value_kernel, len(weights), chips, parts),
        in_specs=[pl.BlockSpec(memory_space=pltpu.VMEM)] * (chips * parts + len(weights))
        + [pl.BlockSpec(memory_space=pl.ANY)] * len(after),
        out_shape=[jax.ShapeDtypeStruct((chips // 2 * rows, feats), bf16)] * 2
        + [jax.ShapeDtypeStruct((chips * rows, feats), f32)],
        scratch_shapes=[pltpu.VMEM((feats, width), bf16)],
        compiler_params=limit(40),
        name="value_parts",
    )(*[p for piece in pieces for p in piece], *weights, *after)


def back_kernel(planes, chips, grads_ref, value_ref, got_a_ref, got_b_ref, *refs):
    weight_refs, refs = refs[: 2 * planes], refs[2 * planes :]
    out_refs, own_ref, held = refs[-chips - 2 : -2], refs[-2], refs[-1]
    rows, feats = own_ref.shape
    width = held.shape[1]
    half = chips // 2
    for k in range(chips):
        got_ref = got_b_ref if k // half else got_a_ref
        total = value_ref[k * rows : (k + 1) * rows, :]
        total += got_ref[k % half * rows : (k % half + 1) * rows, :].astype(f32)
        if k == 0:
            own_ref[...] = total
        else:
            out_refs[k][:, 2 * width :] = total.astype(bf16)
    for j in range(2):
        gather_weight(weight_refs[j * planes : (j + 1) * planes], held)
        for k in range(chips):
            out_refs[k][:, j * width : (j + 1) * width] = jnp.dot(
                grads_ref[k * rows : (k + 1) * rows, :],
                held[...],
                preferred_element_type=f32,
            ).astype(bf16)


def back_blocks(grads, sums, weights, chips):
    rows, feats = grads.shape[0] // chips, grads.shape[1]
    width = weights[0].shape[-1]
    return pl.pallas_call(
        functools.partial(back_kernel, len(weights) // 2, chips),
        out_shape=[
            jax.ShapeDtypeStruct((rows, 2 * width + (feats if k else 0)), bf16)
            for k in range(chips)
        ]
        + [jax.ShapeDtypeStruct((rows, feats), f32)],
        scratch_shapes=[pltpu.VMEM((feats, width), bf16)],
        compiler_params=limit(40),
        name="back_blocks",
    )(grads, *sums, *weights)


def grad_x_kernel(tok_ref, gain_ref, part_ref, *refs):
    grad_refs, (out_ref, values_ref) = refs[:-2], refs[-2:]
    model = tok_ref.shape[-1]
    width = grad_refs[0].shape[-1] // 2
    values = part_ref[...]
    for grad_ref in grad_refs[1:]:
        values += grad_ref[:, 2 * width :].astype(f32)
    values_ref[...] = values.astype(bf16)
    tok = tok_ref[...].astype(f32)
    inv_rms = lax.rsqrt(jnp.mean(tok * tok, axis=-1, keepdims=True) + norm_eps)
    total = jnp.zeros((tok.shape[0], 1), f32)
    for k, grad_ref in enumerate(grad_refs):
        for j in range(2):
            cols = column_block(k, j, width)
            weighted = gain_ref[:, cols] * grad_ref[:, j * width : (j + 1) * width].astype(f32)
            scaled = tok_ref[:, cols].astype(f32) * inv_rms
            total += jnp.sum(weighted * scaled, axis=-1, keepdims=True)
    mean = total / model
    for k, grad_ref in enumerate(grad_refs):
        for j in range(2):
            cols = column_block(k, j, width)
            weighted = gain_ref[:, cols] * grad_ref[:, j * width : (j + 1) * width].astype(f32)
            scaled = tok_ref[:, cols].astype(f32) * inv_rms
            out_ref[:, cols] = (inv_rms * (weighted - scaled * mean)).astype(bf16)


def grad_x_blocks(tokens, gain, part, grads):
    rows, model = tokens.shape
    feats = part.shape[-1]
    step = min(rows, 32)
    return pl.pallas_call(
        grad_x_kernel,
        grid=(rows // step,),
        in_specs=[
            pl.BlockSpec((step, model), lambda i: (i, 0)),
            pl.BlockSpec((1, model), lambda i: (0, 0)),
            pl.BlockSpec((step, feats), lambda i: (i, 0)),
        ]
        + [pl.BlockSpec((step, g.shape[1]), lambda i: (i, 0)) for g in grads],
        out_specs=[
            pl.BlockSpec((step, model), lambda i: (i, 0)),
            pl.BlockSpec((step, feats), lambda i: (i, 0)),
        ],
        out_shape=[
            jax.ShapeDtypeStruct((rows, model), bf16),
            jax.ShapeDtypeStruct((rows, feats), bf16),
        ],
        compiler_params=limit(24),
        cost_estimate=cost(16 * rows * model, 6 * rows * model),
        name="grad_x_blocks",
    )(tokens, gain, part, *grads)


def add_kernel(count, groups, *refs):
    for i, out_ref in enumerate(refs[-groups:]):
        total = refs[i * count][...].astype(f32)
        for ref in refs[i * count + 1 : (i + 1) * count]:
            total += ref[...].astype(f32)
        out_ref[...] = total.astype(out_ref.dtype)


def relay(sums, after):
    shape = sums[0][0].shape
    size = shape[0] * shape[1]
    return pl.pallas_call(
        functools.partial(add_kernel, len(sums[0]), len(sums)),
        in_specs=[pl.BlockSpec(memory_space=pltpu.VMEM)] * (len(sums) * len(sums[0]))
        + [pl.BlockSpec(memory_space=pl.ANY)] * len(after),
        out_shape=[jax.ShapeDtypeStruct(shape, bf16)] * len(sums),
        compiler_params=limit(16),
        cost_estimate=cost(2 * size, 12 * size),
        name="relay",
    )(*[a for group in sums for a in group], *after)


def finish_kernel(own_ref, even_ref, odd_ref, *refs):
    kept_ref, sent_ref = refs[-2:]
    half = kept_ref.shape[0]
    for part, out_ref in ((slice(half), kept_ref), (slice(half, 2 * half), sent_ref)):
        total = own_ref[part, :].astype(f32) + even_ref[part, :].astype(f32)
        out_ref[...] = (total + odd_ref[part, :].astype(f32)).astype(out_ref.dtype)


def finish(own, even, odd, after):
    height, width = own.shape
    return pl.pallas_call(
        finish_kernel,
        in_specs=[pl.BlockSpec(memory_space=pltpu.VMEM)] * 3
        + [pl.BlockSpec(memory_space=pl.ANY)] * len(after),
        out_shape=[
            jax.ShapeDtypeStruct((height // 2, width), f32),
            jax.ShapeDtypeStruct((height // 2, width), bf16),
        ],
        compiler_params=limit(16),
        cost_estimate=cost(2 * height * width, 9 * height * width),
        name="finish",
    )(own, even, odd, *after)


def adam_kernel(token_total, parts, owner_ref, *refs):
    kept_refs, got_refs, refs = refs[:parts], refs[parts : 2 * parts], refs[2 * parts :]
    master_ref, moment1_ref, moment2_ref = refs[:3]
    out_refs = refs[3:]
    step, width = kept_refs[0].shape
    dp = lax.axis_index("dp")
    owned = (owner_ref[...] == dp).astype(f32)
    count = jnp.sum(owned, axis=1, keepdims=True)
    index = pl.program_id(0) * step + lax.broadcasted_iota(jnp.int32, (step, 1), 0)
    occupied = (index.astype(f32) < count).astype(f32)
    for i, refs in enumerate((kept_refs, got_refs)):
        for part, ref in enumerate(refs):
            at = (((dp % 2) ^ i) * parts + part) * width
            cols = pl.ds(pl.multiple_of(at, width), width)
            slot_grad = ref[...].astype(f32) / token_total
            new_moment1 = (
                beta_one * moment1_ref[:, cols] + (1.0 - beta_one) * slot_grad
            ) * occupied
            new_moment2 = (
                beta_two * moment2_ref[:, cols] + (1.0 - beta_two) * slot_grad * slot_grad
            ) * occupied
            step_dir = new_moment1 / bias_one / (jnp.sqrt(new_moment2 / bias_two) + adam_eps)
            out_refs[0][:, cols] = (master_ref[:, cols] - learn_rate * step_dir) * occupied
            out_refs[1][:, cols] = new_moment1
            out_refs[2][:, cols] = new_moment2


def adam(owner, kept, got, states, token_total):
    slots, cols = states[0].shape
    width = kept[0].shape[-1]
    step = min(slots, 32)
    return pl.pallas_call(
        functools.partial(adam_kernel, token_total, len(kept)),
        grid=(slots // step,),
        in_specs=[pl.BlockSpec(owner.shape, lambda i: (0, 0))]
        + [pl.BlockSpec((step, width), lambda i: (i, 0))] * (2 * len(kept))
        + [pl.BlockSpec((step, cols), lambda i: (i, 0))] * 3,
        out_specs=[pl.BlockSpec((step, cols), lambda i: (i, 0))] * 3,
        out_shape=[jax.ShapeDtypeStruct((slots, cols), f32)] * 3,
        compiler_params=limit(24),
        cost_estimate=cost(20 * slots * cols, 30 * slots * cols),
        name="adam",
    )(owner, *kept, *got, *states)


def on_device(groups, seqs, tokens, gain, w_t, grad_values, owner, master, moment1, moment2):
    planes = groups // 2
    chips = seqs
    parts = column_parts
    tokens, value_grad = tokens[0], grad_values[0]
    rows, model = tokens.shape
    feats = owner.shape[0]
    slots = master.shape[1]
    width = model // (2 * seqs)
    own_x = lax.axis_index("dp") % 2

    def permute(value, target):
        pairs = []
        for dp in range(groups):
            for seq in range(seqs):
                to = target(dp, seq)
                if to is not None:
                    pairs.append((dp * seqs + seq, to[0] * seqs + to[1]))
        return lax.ppermute(value, ("dp", "seq"), pairs)

    def to_chip(value, k):
        return permute(value, lambda dp, seq: (dp ^ (k & 1), seq ^ (k >> 1 << 1)))

    def to_core(value):
        return permute(value, lambda dp, seq: (dp, seq ^ 1))

    def to_x(value):
        return permute(value, lambda dp, seq: (dp ^ 1, seq))

    def to_plane(value, turn):
        return permute(value, lambda dp, seq: (dp ^ (2 * turn), seq))

    def busy(z, step, even):
        rightward = (z % 2 == 0) == even
        return z < step if rightward else planes - 1 - z < step

    def across(value, step, even):
        def target(dp, seq):
            z = dp // 2
            way = 1 if (z % 2 == 0) == even else -1
            return (dp + 2 * way, seq) if busy(z, step, even) else None

        return permute(value, target)

    tokens_far = to_core(tokens)
    grads = [value_grad] + [to_chip(value_grad, k) for k in range(chips - 1, 0, -1)][::-1]
    w_keep, w_send = halves(w_t, width)
    w_got = to_x(w_send)

    gain_row, owner_row = gain[None, :], owner[None, :]
    sent = norm_blocks(tokens, tokens_far, gain_row, chips, width, parts)
    w_plane, grads = unpack(w_keep, w_got, grads, (sent[0][0],))
    pieces = [sent[0]] + [[to_chip(p, k) for p in sent[k]] for k in range(1, chips)]
    selected = select_rows(owner_row, groups, slots, (sent[0][0],))

    weights = [w_plane]
    while len(weights) < planes:
        weights += [to_plane(w, len(weights)) for w in weights]
    weights_far = [to_core(w) for w in weights]
    grads_far = to_core(late(grads, weights[1:2]))

    plan = [
        (step, even)
        for step in range(1, planes)
        for even in (True, False)
        if any(busy(z, step, even) for z in range(planes))
    ]
    kept, got = [], []
    for part in range(parts):
        outs = weight_blocks(
            selected,
            [grads, grads_far],
            [piece[part] for piece in pieces],
            planes,
            plan,
            weights if part == parts - 1 else [],
        )
        ready = dict(zip(plan, outs))
        if part == parts - 1:
            *far_sums, near_sum = value_parts(pieces, weights, feats, outs[:1])
            sums = [near_sum] + [to_core(f) for f in far_sums]
            back = back_blocks(grads, sums, weights + weights_far, chips)
            home = [back[0]] + [to_chip(back[k], k) for k in range(1, chips)]
        held = {}
        for step in range(1, planes):
            here = [even for even in (True, False) if (step, even) in ready]
            send = [ready[step, even] for even in here]
            if held:
                sums = [[ready[step, even], held[not even]] for even in here if (not even) in held]
                if sums:
                    sums = list(relay(sums, back[:1] if step == 2 else home[-1:]))
                send = []
                for even in here:
                    send.append(sums.pop(0) if (not even) in held else ready[step, even])
            held = {even: across(value, step, even) for even, value in zip(here, send)}
        keep, send = finish(outs[-1], held[True], held[False], home[1:])
        kept.append(keep)
        got.append(to_x(send))

    grad_x, values = grad_x_blocks(tokens, gain_row, back[-1], home)

    states = adam(owner_row, kept, got, (master[0], moment1[0], moment2[0]), rows * seqs * groups)
    return (values[None], grad_x[None], *(s[None] for s in states))


def solution(mesh):
    placed = (
        P("dp", "seq", None),
        P(),
        P("dp", "seq"),
        P("dp", "seq", None),
        P(),
        P("dp", None, "seq"),
        P("dp", None, "seq"),
        P("dp", None, "seq"),
    )
    return jax.shard_map(
        functools.partial(on_device, mesh.shape["dp"], mesh.shape["seq"]),
        mesh=mesh,
        in_specs=placed,
        out_specs=(
            P("dp", "seq", None),
            P("dp", "seq", None),
            P("dp", None, "seq"),
            P("dp", None, "seq"),
            P("dp", None, "seq"),
        ),
        check_vma=False,
    )
```

```python
import functools

import jax
import jax.numpy as jnp
from jax import lax
from jax.experimental import pallas as pl
from jax.experimental.pallas import tpu as pltpu
from jax.sharding import PartitionSpec as P

beta_one = 0.9
beta_two = 0.95
learn_rate = 0.001
adam_eps = 1e-08
bias_one = 1.0 - 0.9**10
bias_two = 1.0 - 0.95**10
norm_eps = 1e-05
column_parts = 1

bf16 = jnp.bfloat16
f32 = jnp.float32


def cost(flops, moved):
    return pl.CostEstimate(flops=flops, bytes_accessed=moved, transcendentals=0)


def limit(mib):
    return pltpu.CompilerParams(vmem_limit_bytes=mib * 1024 * 1024)


def column_block(k, j, width, part=0, parts=1):
    seq = lax.axis_index("seq") ^ (k >> 1 << 1) ^ j
    x = (lax.axis_index("dp") % 2) ^ (k & 1)
    return pl.ds(pl.multiple_of(((seq * 2 + x) * parts + part) * width, width), width)


def norm_kernel(parts, tok_ref, far_ref, gain_ref, *refs):
    out_refs = [refs[i : i + parts] for i in range(0, len(refs), parts)]
    chips = len(out_refs)
    width = out_refs[0][0].shape[-1]
    for i, ref in enumerate((tok_ref, far_ref)):
        tok = ref[...].astype(f32)
        inv_rms = lax.rsqrt(jnp.mean(tok * tok, axis=-1, keepdims=True) + norm_eps)
        for k in (*range(1, chips), 0):
            for part in range(parts):
                cols = column_block(k, 0, width, part, parts)
                scaled = ref[:, cols].astype(f32) * inv_rms
                out_refs[k][part][i] = (scaled * gain_ref[:, cols]).astype(bf16)


def norm_blocks(tokens, far, gain, chips, width, parts):
    rows, model = tokens.shape
    step = min(rows, 32)
    outs = pl.pallas_call(
        functools.partial(norm_kernel, parts),
        grid=(rows // step,),
        in_specs=[
            pl.BlockSpec((step, model), lambda i: (i, 0)),
            pl.BlockSpec((step, model), lambda i: (i, 0)),
            pl.BlockSpec((1, model), lambda i: (0, 0)),
        ],
        out_specs=[pl.BlockSpec((2, step, width // parts), lambda i: (0, i, 0))] * (chips * parts),
        out_shape=[jax.ShapeDtypeStruct((2, rows, width // parts), bf16)] * (chips * parts),
        compiler_params=limit(24),
        cost_estimate=cost(8 * rows * model, 6 * rows * model),
        name="norm_blocks",
    )(tokens, far, gain)
    return [outs[i : i + parts] for i in range(0, len(outs), parts)]


def halves_kernel(w_ref, keep_ref, send_ref):
    width = keep_ref.shape[1]
    own_x = lax.axis_index("dp") % 2
    keep_ref[...] = w_ref[:, pl.ds(pl.multiple_of(own_x * width, width), width)]
    send_ref[...] = w_ref[:, pl.ds(pl.multiple_of((1 - own_x) * width, width), width)]


def halves(w_t, width):
    return pl.pallas_call(
        halves_kernel,
        out_shape=[jax.ShapeDtypeStruct((w_t.shape[0], width), bf16)] * 2,
        compiler_params=limit(16),
        name="halves",
    )(w_t)


def stack_kernel(count, *refs):
    out_refs = refs[-(len(refs) - count) :]
    rows = refs[0].shape[0]
    each = out_refs[0].shape[0] // rows
    for i, ref in enumerate(refs[:count]):
        out_refs[i // each][i % each * rows : (i % each + 1) * rows, :] = ref[...]


def stack(pieces, outs, after):
    count = len(pieces)
    rows, width = pieces[0].shape
    return pl.pallas_call(
        lambda *refs: stack_kernel(count, *refs[:count], *refs[count + len(after) :]),
        in_specs=[pl.BlockSpec(memory_space=pltpu.VMEM)] * count
        + [pl.BlockSpec(memory_space=pl.ANY)] * len(after),
        out_shape=[jax.ShapeDtypeStruct((count // outs * rows, width), bf16)] * outs,
        compiler_params=limit(16),
        name="stack",
    )(*pieces, *after)


def select_kernel(groups, slots, owner_ref, *refs):
    out_ref = refs[-1]
    feats = owner_ref.shape[1]
    owner = owner_ref[...]
    lower = lax.broadcasted_iota(jnp.int32, (feats, feats), 0) < lax.broadcasted_iota(
        jnp.int32, (feats, feats), 1
    )
    owned = (lax.broadcasted_iota(jnp.int32, (groups, feats), 0) == owner).astype(f32)
    before = jnp.dot(
        owned.astype(bf16), lower.astype(f32).astype(bf16), preferred_element_type=f32
    )
    place = jnp.sum(owned * before, axis=0, keepdims=True).astype(jnp.int32)
    own_x = lax.axis_index("dp") % 2
    slot = (owner ^ own_x) * slots + place
    step = 256
    for at in range(0, out_ref.shape[0], step):
        index = at + lax.broadcasted_iota(jnp.int32, (step, feats), 0)
        out_ref[at : at + step, :] = (index == slot).astype(f32).astype(bf16)


def select_rows(owner, groups, slots, after):
    feats = owner.shape[1]
    return pl.pallas_call(
        functools.partial(select_kernel, groups, slots),
        in_specs=[pl.BlockSpec(memory_space=pltpu.VMEM)]
        + [pl.BlockSpec(memory_space=pl.ANY)] * len(after),
        out_shape=jax.ShapeDtypeStruct((groups * slots, feats), bf16),
        compiler_params=limit(24),
        cost_estimate=cost(4 * groups * slots * feats, 2 * groups * slots * feats),
        name="select_rows",
    )(owner, *after)


def weight_kernel(planes, chips, plan, *refs):
    sel_ref, refs = refs[0], refs[1:]
    grad_refs, refs = refs[:4], refs[4:]
    pieces, refs = refs[:chips], refs[chips:]
    out_refs, (held, base) = refs[-len(plan) - 3 : -2], refs[-2:]
    rows = pieces[0].shape[1]
    feats = sel_ref.shape[1]
    block = sel_ref.shape[0] // planes
    half = chips // 2
    z = lax.axis_index("dp") // 2
    for k in range(chips):
        for i in range(2):
            at = k % half * rows
            held[2 * i + k // half, at : at + rows, :] = pieces[k][i]
    for at in range(0, feats, 256):
        total = None
        for i in range(4):
            term = lax.dot_general(
                grad_refs[i][:, at : at + 256],
                held[i],
                (((0,), (0,)), ((), ())),
                preferred_element_type=f32,
            )
            total = term if total is None else total + term
        base[at : at + 256, :] = total.astype(bf16)

    def chosen(plane):
        at = pl.multiple_of(plane * block, block)
        return jnp.dot(sel_ref[pl.ds(at, block), :], base[...], preferred_element_type=f32)

    for (step, even), out_ref in zip(plan, out_refs):
        ahead = planes - step
        plane = jnp.where((z % 2 == 0) == even, z + ahead, z - ahead)

        @pl.when((plane >= 0) & (plane < planes))
        def _():
            out_ref[...] = chosen(plane).astype(bf16)

    out_refs[-1][...] = chosen(z).astype(bf16)


def weight_blocks(selected, grads, pieces, planes, plan, after):
    chips = len(pieces)
    slots_all, feats = selected.shape
    _, rows, width = pieces[0].shape
    total = 2 * chips * rows
    block = slots_all // planes
    return pl.pallas_call(
        functools.partial(weight_kernel, planes, chips, plan),
        in_specs=[pl.BlockSpec(memory_space=pltpu.VMEM)] * (5 + chips)
        + [pl.BlockSpec(memory_space=pl.ANY)] * len(after),
        out_shape=[jax.ShapeDtypeStruct((block, width), bf16)] * (len(plan) + 1),
        scratch_shapes=[
            pltpu.VMEM((4, total // 4, width), bf16),
            pltpu.VMEM((feats, width), bf16),
        ],
        compiler_params=limit(40),
        cost_estimate=cost(2 * (slots_all + total) * feats * width, 4 * total * width),
        name="weight_blocks",
    )(selected, *grads, *pieces, *after)


def gather_weight(piece_refs, held):
    dp = lax.axis_index("dp")
    own_x, own_z = dp % 2, dp // 2
    for turn, ref in enumerate(piece_refs):
        share = ref.shape[0] // 2
        for i in range(2):
            at = pl.multiple_of(((own_z ^ turn) * 2 + (own_x ^ i)) * share, share)
            held[pl.ds(at, share), :] = ref[i * share : (i + 1) * share, :]


def value_kernel(planes, chips, parts, *refs):
    piece_refs, refs = refs[: chips * parts], refs[chips * parts :]
    far_refs, out_ref, held = refs[-4:-2], refs[-2], refs[-1]
    rows = out_ref.shape[0] // chips
    half = chips // 2
    part_width = held.shape[1] // parts
    gather_weight(refs[:planes], held)
    for core in (1, 0):
        for k in range(chips):
            total = None
            for part in range(parts):
                term = lax.dot_general(
                    piece_refs[k * parts + part][core],
                    held[:, part * part_width : (part + 1) * part_width],
                    (((1,), (1,)), ((), ())),
                    preferred_element_type=f32,
                )
                total = term if total is None else total + term
            if core:
                at = k % half * rows
                far_refs[k // half][at : at + rows, :] = total.astype(bf16)
            else:
                out_ref[k * rows : (k + 1) * rows, :] = total


def value_parts(pieces, weights, feats, after):
    chips, parts = len(pieces), len(pieces[0])
    rows = pieces[0][0].shape[1]
    width = weights[0].shape[-1]
    return pl.pallas_call(
        functools.partial(value_kernel, len(weights), chips, parts),
        in_specs=[pl.BlockSpec(memory_space=pltpu.VMEM)] * (chips * parts + len(weights))
        + [pl.BlockSpec(memory_space=pl.ANY)] * len(after),
        out_shape=[jax.ShapeDtypeStruct((chips // 2 * rows, feats), bf16)] * 2
        + [jax.ShapeDtypeStruct((chips * rows, feats), f32)],
        scratch_shapes=[pltpu.VMEM((feats, width), bf16)],
        compiler_params=limit(40),
        name="value_parts",
    )(*[p for piece in pieces for p in piece], *weights, *after)


def back_kernel(planes, chips, grads_a_ref, grads_b_ref, value_ref, got_a_ref, got_b_ref, *refs):
    weight_refs, refs = refs[: 2 * planes], refs[2 * planes :]
    out_refs, own_ref, held = refs[-chips - 2 : -2], refs[-2], refs[-1]
    rows, feats = own_ref.shape
    width = held.shape[1]
    half = chips // 2
    for k in range(chips):
        got_ref = got_b_ref if k // half else got_a_ref
        total = value_ref[k * rows : (k + 1) * rows, :]
        total += got_ref[k % half * rows : (k % half + 1) * rows, :].astype(f32)
        if k == 0:
            own_ref[...] = total
        else:
            out_refs[k][:, 2 * width :] = total.astype(bf16)
    for j in range(2):
        gather_weight(weight_refs[j * planes : (j + 1) * planes], held)
        for k in range(chips):
            grads_ref = grads_b_ref if k // half else grads_a_ref
            out_refs[k][:, j * width : (j + 1) * width] = jnp.dot(
                grads_ref[k % half * rows : (k % half + 1) * rows, :],
                held[...],
                preferred_element_type=f32,
            ).astype(bf16)


def back_blocks(grads, sums, weights, chips):
    rows, feats = 2 * grads[0].shape[0] // chips, grads[0].shape[1]
    width = weights[0].shape[-1]
    return pl.pallas_call(
        functools.partial(back_kernel, len(weights) // 2, chips),
        out_shape=[
            jax.ShapeDtypeStruct((rows, 2 * width + (feats if k else 0)), bf16)
            for k in range(chips)
        ]
        + [jax.ShapeDtypeStruct((rows, feats), f32)],
        scratch_shapes=[pltpu.VMEM((feats, width), bf16)],
        compiler_params=limit(40),
        name="back_blocks",
    )(*grads, *sums, *weights)


def grad_x_kernel(tok_ref, gain_ref, part_ref, *refs):
    grad_refs, (out_ref, values_ref) = refs[:-2], refs[-2:]
    model = tok_ref.shape[-1]
    width = grad_refs[0].shape[-1] // 2
    values = part_ref[...]
    for grad_ref in grad_refs[1:]:
        values += grad_ref[:, 2 * width :].astype(f32)
    values_ref[...] = values.astype(bf16)
    tok = tok_ref[...].astype(f32)
    inv_rms = lax.rsqrt(jnp.mean(tok * tok, axis=-1, keepdims=True) + norm_eps)
    total = jnp.zeros((tok.shape[0], 1), f32)
    for k, grad_ref in enumerate(grad_refs):
        for j in range(2):
            cols = column_block(k, j, width)
            weighted = gain_ref[:, cols] * grad_ref[:, j * width : (j + 1) * width].astype(f32)
            scaled = tok_ref[:, cols].astype(f32) * inv_rms
            total += jnp.sum(weighted * scaled, axis=-1, keepdims=True)
    mean = total / model
    for k, grad_ref in enumerate(grad_refs):
        for j in range(2):
            cols = column_block(k, j, width)
            weighted = gain_ref[:, cols] * grad_ref[:, j * width : (j + 1) * width].astype(f32)
            scaled = tok_ref[:, cols].astype(f32) * inv_rms
            out_ref[:, cols] = (inv_rms * (weighted - scaled * mean)).astype(bf16)


def grad_x_blocks(tokens, gain, part, grads):
    rows, model = tokens.shape
    feats = part.shape[-1]
    step = min(rows, 32)
    return pl.pallas_call(
        grad_x_kernel,
        grid=(rows // step,),
        in_specs=[
            pl.BlockSpec((step, model), lambda i: (i, 0)),
            pl.BlockSpec((1, model), lambda i: (0, 0)),
            pl.BlockSpec((step, feats), lambda i: (i, 0)),
        ]
        + [pl.BlockSpec((step, g.shape[1]), lambda i: (i, 0)) for g in grads],
        out_specs=[
            pl.BlockSpec((step, model), lambda i: (i, 0)),
            pl.BlockSpec((step, feats), lambda i: (i, 0)),
        ],
        out_shape=[
            jax.ShapeDtypeStruct((rows, model), bf16),
            jax.ShapeDtypeStruct((rows, feats), bf16),
        ],
        compiler_params=limit(24),
        cost_estimate=cost(16 * rows * model, 6 * rows * model),
        name="grad_x_blocks",
    )(tokens, gain, part, *grads)


def add_kernel(count, groups, *refs):
    for i, out_ref in enumerate(refs[-groups:]):
        total = refs[i * count][...].astype(f32)
        for ref in refs[i * count + 1 : (i + 1) * count]:
            total += ref[...].astype(f32)
        out_ref[...] = total.astype(out_ref.dtype)


def relay(sums, after):
    shape = sums[0][0].shape
    size = shape[0] * shape[1]
    return pl.pallas_call(
        functools.partial(add_kernel, len(sums[0]), len(sums)),
        in_specs=[pl.BlockSpec(memory_space=pltpu.VMEM)] * (len(sums) * len(sums[0]))
        + [pl.BlockSpec(memory_space=pl.ANY)] * len(after),
        out_shape=[jax.ShapeDtypeStruct(shape, bf16)] * len(sums),
        compiler_params=limit(16),
        cost_estimate=cost(2 * size, 12 * size),
        name="relay",
    )(*[a for group in sums for a in group], *after)


def finish_kernel(own_ref, even_ref, odd_ref, *refs):
    kept_ref, sent_ref = refs[-2:]
    half = kept_ref.shape[0]
    for part, out_ref in ((slice(half), kept_ref), (slice(half, 2 * half), sent_ref)):
        total = own_ref[part, :].astype(f32) + even_ref[part, :].astype(f32)
        out_ref[...] = (total + odd_ref[part, :].astype(f32)).astype(out_ref.dtype)


def finish(own, even, odd, after):
    height, width = own.shape
    return pl.pallas_call(
        finish_kernel,
        in_specs=[pl.BlockSpec(memory_space=pltpu.VMEM)] * 3
        + [pl.BlockSpec(memory_space=pl.ANY)] * len(after),
        out_shape=[
            jax.ShapeDtypeStruct((height // 2, width), f32),
            jax.ShapeDtypeStruct((height // 2, width), bf16),
        ],
        compiler_params=limit(16),
        cost_estimate=cost(2 * height * width, 9 * height * width),
        name="finish",
    )(own, even, odd, *after)


def adam_kernel(token_total, parts, owner_ref, *refs):
    kept_refs, got_refs, refs = refs[:parts], refs[parts : 2 * parts], refs[2 * parts :]
    master_ref, moment1_ref, moment2_ref = refs[:3]
    out_refs = refs[3:]
    step, width = kept_refs[0].shape
    dp = lax.axis_index("dp")
    owned = (owner_ref[...] == dp).astype(f32)
    count = jnp.sum(owned, axis=1, keepdims=True)
    index = pl.program_id(0) * step + lax.broadcasted_iota(jnp.int32, (step, 1), 0)
    occupied = (index.astype(f32) < count).astype(f32)
    for i, refs in enumerate((kept_refs, got_refs)):
        for part, ref in enumerate(refs):
            at = (((dp % 2) ^ i) * parts + part) * width
            cols = pl.ds(pl.multiple_of(at, width), width)
            slot_grad = ref[...].astype(f32) / token_total
            new_moment1 = (
                beta_one * moment1_ref[:, cols] + (1.0 - beta_one) * slot_grad
            ) * occupied
            new_moment2 = (
                beta_two * moment2_ref[:, cols] + (1.0 - beta_two) * slot_grad * slot_grad
            ) * occupied
            step_dir = new_moment1 / bias_one / (jnp.sqrt(new_moment2 / bias_two) + adam_eps)
            out_refs[0][:, cols] = (master_ref[:, cols] - learn_rate * step_dir) * occupied
            out_refs[1][:, cols] = new_moment1
            out_refs[2][:, cols] = new_moment2


def adam(owner, kept, got, states, token_total):
    slots, cols = states[0].shape
    width = kept[0].shape[-1]
    step = min(slots, 32)
    return pl.pallas_call(
        functools.partial(adam_kernel, token_total, len(kept)),
        grid=(slots // step,),
        in_specs=[pl.BlockSpec(owner.shape, lambda i: (0, 0))]
        + [pl.BlockSpec((step, width), lambda i: (i, 0))] * (2 * len(kept))
        + [pl.BlockSpec((step, cols), lambda i: (i, 0))] * 3,
        out_specs=[pl.BlockSpec((step, cols), lambda i: (i, 0))] * 3,
        out_shape=[jax.ShapeDtypeStruct((slots, cols), f32)] * 3,
        compiler_params=limit(24),
        cost_estimate=cost(20 * slots * cols, 30 * slots * cols),
        name="adam",
    )(owner, *kept, *got, *states)


def on_device(groups, seqs, tokens, gain, w_t, grad_values, owner, master, moment1, moment2):
    planes = groups // 2
    chips = seqs
    parts = column_parts
    tokens, value_grad = tokens[0], grad_values[0]
    rows, model = tokens.shape
    feats = owner.shape[0]
    slots = master.shape[1]
    width = model // (2 * seqs)
    own_x = lax.axis_index("dp") % 2

    def permute(value, target):
        pairs = []
        for dp in range(groups):
            for seq in range(seqs):
                to = target(dp, seq)
                if to is not None:
                    pairs.append((dp * seqs + seq, to[0] * seqs + to[1]))
        return lax.ppermute(value, ("dp", "seq"), pairs)

    def to_chip(value, k):
        return permute(value, lambda dp, seq: (dp ^ (k & 1), seq ^ (k >> 1 << 1)))

    def to_core(value):
        return permute(value, lambda dp, seq: (dp, seq ^ 1))

    def to_x(value):
        return permute(value, lambda dp, seq: (dp ^ 1, seq))

    def to_plane(value, turn):
        return permute(value, lambda dp, seq: (dp ^ (2 * turn), seq))

    def busy(z, step, even):
        rightward = (z % 2 == 0) == even
        return z < step if rightward else planes - 1 - z < step

    def across(value, step, even):
        def target(dp, seq):
            z = dp // 2
            way = 1 if (z % 2 == 0) == even else -1
            return (dp + 2 * way, seq) if busy(z, step, even) else None

        return permute(value, target)

    tokens_far = to_core(tokens)
    grads = [value_grad] + [to_chip(value_grad, k) for k in range(chips - 1, 0, -1)][::-1]
    w_keep, w_send = halves(w_t, width)
    w_got = to_x(w_send)

    gain_row, owner_row = gain[None, :], owner[None, :]
    sent = norm_blocks(tokens, tokens_far, gain_row, chips, width, parts)
    grads = stack(grads, 2, sent[0][:1])
    pieces = [sent[0]] + [[to_chip(p, k) for p in sent[k]] for k in range(1, chips)]
    grads_far = [to_core(g) for g in grads]
    selected = select_rows(owner_row, groups, slots, (sent[0][0],))

    weights = stack([w_keep, w_got], 1, grads[:1])
    turn = planes // 2
    while turn:
        weights = [w for value in weights for w in (value, to_plane(value, turn))]
        turn //= 2
    weights_far = [to_core(w) for w in weights]

    plan = [
        (step, even)
        for step in range(1, planes)
        for even in (True, False)
        if any(busy(z, step, even) for z in range(planes))
    ]
    kept, got = [], []
    for part in range(parts):
        outs = weight_blocks(
            selected,
            [*grads, *grads_far],
            [piece[part] for piece in pieces],
            planes,
            plan,
            weights[:1] if part == parts - 1 else [],
        )
        ready = dict(zip(plan, outs))
        if part == parts - 1:
            *far_sums, near_sum = value_parts(pieces, weights, feats, outs[:1])
            sums = [near_sum] + [to_core(f) for f in far_sums]
            back = back_blocks(grads, sums, weights + weights_far, chips)
            home = [back[0]] + [to_chip(back[k], k) for k in range(1, chips)]
        held = {}
        for step in range(1, planes):
            here = [even for even in (True, False) if (step, even) in ready]
            send = [ready[step, even] for even in here]
            if held:
                sums = [[ready[step, even], held[not even]] for even in here if (not even) in held]
                if sums:
                    sums = list(relay(sums, back[:1] if step == 2 else home[-1:]))
                send = []
                for even in here:
                    send.append(sums.pop(0) if (not even) in held else ready[step, even])
            held = {even: across(value, step, even) for even, value in zip(here, send)}
        keep, send = finish(outs[-1], held[True], held[False], home[1:])
        kept.append(keep)
        got.append(to_x(send))

    grad_x, values = grad_x_blocks(tokens, gain_row, back[-1], home)

    states = adam(owner_row, kept, got, (master[0], moment1[0], moment2[0]), rows * seqs * groups)
    return (values[None], grad_x[None], *(s[None] for s in states))


def solution(mesh):
    placed = (
        P("dp", "seq", None),
        P(),
        P("dp", "seq"),
        P("dp", "seq", None),
        P(),
        P("dp", None, "seq"),
        P("dp", None, "seq"),
        P("dp", None, "seq"),
    )
    return jax.shard_map(
        functools.partial(on_device, mesh.shape["dp"], mesh.shape["seq"]),
        mesh=mesh,
        in_specs=placed,
        out_specs=(
            P("dp", "seq", None),
            P("dp", "seq", None),
            P("dp", None, "seq"),
            P("dp", None, "seq"),
            P("dp", None, "seq"),
        ),
        check_vma=False,
    )
```

```python
import functools

import jax
import jax.numpy as jnp
from jax import lax
from jax.experimental import pallas as pl
from jax.experimental.pallas import tpu as pltpu
from jax.sharding import PartitionSpec as P

beta_one = 0.9
beta_two = 0.95
learn_rate = 0.001
adam_eps = 1e-08
bias_one = 1.0 - 0.9**10
bias_two = 1.0 - 0.95**10
norm_eps = 1e-05
column_parts = 1

bf16 = jnp.bfloat16
f32 = jnp.float32


def cost(flops, moved):
    return pl.CostEstimate(flops=flops, bytes_accessed=moved, transcendentals=0)


def limit(mib):
    return pltpu.CompilerParams(vmem_limit_bytes=mib * 1024 * 1024)


def column_block(k, j, width, part=0, parts=1):
    seq = lax.axis_index("seq") ^ (k >> 1 << 1) ^ j
    x = (lax.axis_index("dp") % 2) ^ (k & 1)
    return pl.ds(pl.multiple_of(((seq * 2 + x) * parts + part) * width, width), width)


def norm_kernel(parts, tok_ref, far_ref, gain_ref, *refs):
    out_refs = [refs[i : i + parts] for i in range(0, len(refs), parts)]
    chips = len(out_refs)
    width = out_refs[0][0].shape[-1]
    for i, ref in enumerate((tok_ref, far_ref)):
        tok = ref[...].astype(f32)
        inv_rms = lax.rsqrt(jnp.mean(tok * tok, axis=-1, keepdims=True) + norm_eps)
        for k in (*range(1, chips), 0):
            for part in range(parts):
                cols = column_block(k, 0, width, part, parts)
                scaled = ref[:, cols].astype(f32) * inv_rms
                out_refs[k][part][i] = (scaled * gain_ref[:, cols]).astype(bf16)


def norm_blocks(tokens, far, gain, chips, width, parts):
    rows, model = tokens.shape
    step = min(rows, 32)
    outs = pl.pallas_call(
        functools.partial(norm_kernel, parts),
        grid=(rows // step,),
        in_specs=[
            pl.BlockSpec((step, model), lambda i: (i, 0)),
            pl.BlockSpec((step, model), lambda i: (i, 0)),
            pl.BlockSpec((1, model), lambda i: (0, 0)),
        ],
        out_specs=[pl.BlockSpec((2, step, width // parts), lambda i: (0, i, 0))] * (chips * parts),
        out_shape=[jax.ShapeDtypeStruct((2, rows, width // parts), bf16)] * (chips * parts),
        compiler_params=limit(24),
        cost_estimate=cost(8 * rows * model, 6 * rows * model),
        name="norm_blocks",
    )(
        pltpu.with_memory_space_constraint(tokens, pltpu.HBM),
        far,
        pltpu.with_memory_space_constraint(gain, pltpu.HBM),
    )
    return [outs[i : i + parts] for i in range(0, len(outs), parts)]


def halves_kernel(w_ref, keep_ref, send_ref):
    width = keep_ref.shape[1]
    own_x = lax.axis_index("dp") % 2
    keep_ref[...] = w_ref[:, pl.ds(pl.multiple_of(own_x * width, width), width)]
    send_ref[...] = w_ref[:, pl.ds(pl.multiple_of((1 - own_x) * width, width), width)]


def halves(w_t, width):
    return pl.pallas_call(
        halves_kernel,
        out_shape=[jax.ShapeDtypeStruct((w_t.shape[0], width), bf16)] * 2,
        compiler_params=limit(16),
        name="halves",
    )(pltpu.with_memory_space_constraint(w_t, pltpu.HBM))


def stack_kernel(count, *refs):
    out_refs = refs[-(len(refs) - count) :]
    rows = refs[0].shape[0]
    each = out_refs[0].shape[0] // rows
    for i, ref in enumerate(refs[:count]):
        out_refs[i // each][i % each * rows : (i % each + 1) * rows, :] = ref[...]


def stack(pieces, outs, after):
    count = len(pieces)
    rows, width = pieces[0].shape
    return pl.pallas_call(
        lambda *refs: stack_kernel(count, *refs[:count], *refs[count + len(after) :]),
        in_specs=[pl.BlockSpec(memory_space=pltpu.VMEM)] * count
        + [pl.BlockSpec(memory_space=pl.ANY)] * len(after),
        out_shape=[jax.ShapeDtypeStruct((count // outs * rows, width), bf16)] * outs,
        compiler_params=limit(16),
        name="stack",
    )(*pieces, *after)


def select_kernel(groups, slots, owner_ref, *refs):
    out_ref = refs[-1]
    feats = owner_ref.shape[1]
    owner = owner_ref[...]
    lower = lax.broadcasted_iota(jnp.int32, (feats, feats), 0) < lax.broadcasted_iota(
        jnp.int32, (feats, feats), 1
    )
    owned = (lax.broadcasted_iota(jnp.int32, (groups, feats), 0) == owner).astype(f32)
    before = jnp.dot(
        owned.astype(bf16), lower.astype(f32).astype(bf16), preferred_element_type=f32
    )
    place = jnp.sum(owned * before, axis=0, keepdims=True).astype(jnp.int32)
    own_x = lax.axis_index("dp") % 2
    slot = (owner ^ own_x) * slots + place
    step = 256
    for at in range(0, out_ref.shape[0], step):
        index = at + lax.broadcasted_iota(jnp.int32, (step, feats), 0)
        out_ref[at : at + step, :] = (index == slot).astype(f32).astype(bf16)


def select_rows(owner, groups, slots, after):
    feats = owner.shape[1]
    return pl.pallas_call(
        functools.partial(select_kernel, groups, slots),
        in_specs=[pl.BlockSpec(memory_space=pltpu.VMEM)]
        + [pl.BlockSpec(memory_space=pl.ANY)] * len(after),
        out_shape=jax.ShapeDtypeStruct((groups * slots, feats), bf16),
        compiler_params=limit(24),
        cost_estimate=cost(4 * groups * slots * feats, 2 * groups * slots * feats),
        name="select_rows",
    )(owner, *after)


def weight_kernel(planes, chips, plan, *refs):
    sel_ref, refs = refs[0], refs[1:]
    grad_refs, refs = refs[:4], refs[4:]
    pieces, refs = refs[:chips], refs[chips:]
    out_refs, (held, base) = refs[-len(plan) - 3 : -2], refs[-2:]
    rows = pieces[0].shape[1]
    feats = sel_ref.shape[1]
    block = sel_ref.shape[0] // planes
    half = chips // 2
    z = lax.axis_index("dp") // 2
    for k in range(chips):
        for i in range(2):
            at = k % half * rows
            held[2 * i + k // half, at : at + rows, :] = pieces[k][i]
    for at in range(0, feats, 256):
        total = None
        for i in range(4):
            term = lax.dot_general(
                grad_refs[i][:, at : at + 256],
                held[i],
                (((0,), (0,)), ((), ())),
                preferred_element_type=f32,
            )
            total = term if total is None else total + term
        base[at : at + 256, :] = total.astype(bf16)

    def chosen(plane):
        at = pl.multiple_of(plane * block, block)
        return jnp.dot(sel_ref[pl.ds(at, block), :], base[...], preferred_element_type=f32)

    for (step, even), out_ref in zip(plan, out_refs):
        ahead = planes - step
        plane = jnp.where((z % 2 == 0) == even, z + ahead, z - ahead)

        @pl.when((plane >= 0) & (plane < planes))
        def _():
            out_ref[...] = chosen(plane).astype(bf16)

    out_refs[-1][...] = chosen(z).astype(bf16)


def weight_blocks(selected, grads, pieces, planes, plan, after):
    chips = len(pieces)
    slots_all, feats = selected.shape
    _, rows, width = pieces[0].shape
    total = 2 * chips * rows
    block = slots_all // planes
    return pl.pallas_call(
        functools.partial(weight_kernel, planes, chips, plan),
        in_specs=[pl.BlockSpec(memory_space=pltpu.VMEM)] * (5 + chips)
        + [pl.BlockSpec(memory_space=pl.ANY)] * len(after),
        out_shape=[jax.ShapeDtypeStruct((block, width), bf16)] * (len(plan) + 1),
        scratch_shapes=[
            pltpu.VMEM((4, total // 4, width), bf16),
            pltpu.VMEM((feats, width), bf16),
        ],
        compiler_params=limit(40),
        cost_estimate=cost(2 * (slots_all + total) * feats * width, 4 * total * width),
        name="weight_blocks",
    )(selected, *grads, *pieces, *after)


def gather_weight(piece_refs, held):
    dp = lax.axis_index("dp")
    own_x, own_z = dp % 2, dp // 2
    for turn, ref in enumerate(piece_refs):
        share = ref.shape[0] // 2
        for i in range(2):
            at = pl.multiple_of(((own_z ^ turn) * 2 + (own_x ^ i)) * share, share)
            held[pl.ds(at, share), :] = ref[i * share : (i + 1) * share, :]


def value_kernel(planes, chips, parts, *refs):
    piece_refs, refs = refs[: chips * parts], refs[chips * parts :]
    far_refs, out_ref, held = refs[-4:-2], refs[-2], refs[-1]
    rows = out_ref.shape[0] // chips
    half = chips // 2
    part_width = held.shape[1] // parts
    gather_weight(refs[:planes], held)
    for core in (1, 0):
        for k in range(chips):
            total = None
            for part in range(parts):
                term = lax.dot_general(
                    piece_refs[k * parts + part][core],
                    held[:, part * part_width : (part + 1) * part_width],
                    (((1,), (1,)), ((), ())),
                    preferred_element_type=f32,
                )
                total = term if total is None else total + term
            if core:
                at = k % half * rows
                far_refs[k // half][at : at + rows, :] = total.astype(bf16)
            else:
                out_ref[k * rows : (k + 1) * rows, :] = total


def value_parts(pieces, weights, feats, after):
    chips, parts = len(pieces), len(pieces[0])
    rows = pieces[0][0].shape[1]
    width = weights[0].shape[-1]
    return pl.pallas_call(
        functools.partial(value_kernel, len(weights), chips, parts),
        in_specs=[pl.BlockSpec(memory_space=pltpu.VMEM)] * (chips * parts + len(weights))
        + [pl.BlockSpec(memory_space=pl.ANY)] * len(after),
        out_shape=[jax.ShapeDtypeStruct((chips // 2 * rows, feats), bf16)] * 2
        + [jax.ShapeDtypeStruct((chips * rows, feats), f32)],
        scratch_shapes=[pltpu.VMEM((feats, width), bf16)],
        compiler_params=limit(40),
        name="value_parts",
    )(*[p for piece in pieces for p in piece], *weights, *after)


def back_kernel(planes, chips, grads_a_ref, grads_b_ref, value_ref, got_a_ref, got_b_ref, *refs):
    weight_refs, refs = refs[: 2 * planes], refs[2 * planes :]
    out_refs, own_ref, held = refs[-chips - 2 : -2], refs[-2], refs[-1]
    rows, feats = own_ref.shape
    width = held.shape[1]
    half = chips // 2
    for k in range(chips):
        got_ref = got_b_ref if k // half else got_a_ref
        total = value_ref[k * rows : (k + 1) * rows, :]
        total += got_ref[k % half * rows : (k % half + 1) * rows, :].astype(f32)
        if k == 0:
            own_ref[...] = total
        else:
            out_refs[k][:, 2 * width :] = total.astype(bf16)
    for j in range(2):
        gather_weight(weight_refs[j * planes : (j + 1) * planes], held)
        for k in range(chips):
            grads_ref = grads_b_ref if k // half else grads_a_ref
            out_refs[k][:, j * width : (j + 1) * width] = jnp.dot(
                grads_ref[k % half * rows : (k % half + 1) * rows, :],
                held[...],
                preferred_element_type=f32,
            ).astype(bf16)


def back_blocks(grads, sums, weights, chips):
    rows, feats = 2 * grads[0].shape[0] // chips, grads[0].shape[1]
    width = weights[0].shape[-1]
    return pl.pallas_call(
        functools.partial(back_kernel, len(weights) // 2, chips),
        out_shape=[
            jax.ShapeDtypeStruct((rows, 2 * width + (feats if k else 0)), bf16)
            for k in range(chips)
        ]
        + [jax.ShapeDtypeStruct((rows, feats), f32)],
        scratch_shapes=[pltpu.VMEM((feats, width), bf16)],
        compiler_params=limit(40),
        name="back_blocks",
    )(*grads, *sums, *weights)


def grad_x_kernel(tok_ref, gain_ref, part_ref, *refs):
    grad_refs, (out_ref, values_ref) = refs[:-2], refs[-2:]
    model = tok_ref.shape[-1]
    width = grad_refs[0].shape[-1] // 2
    values = part_ref[...]
    for grad_ref in grad_refs[1:]:
        values += grad_ref[:, 2 * width :].astype(f32)
    values_ref[...] = values.astype(bf16)
    tok = tok_ref[...].astype(f32)
    inv_rms = lax.rsqrt(jnp.mean(tok * tok, axis=-1, keepdims=True) + norm_eps)
    total = jnp.zeros((tok.shape[0], 1), f32)
    for k, grad_ref in enumerate(grad_refs):
        for j in range(2):
            cols = column_block(k, j, width)
            weighted = gain_ref[:, cols] * grad_ref[:, j * width : (j + 1) * width].astype(f32)
            scaled = tok_ref[:, cols].astype(f32) * inv_rms
            total += jnp.sum(weighted * scaled, axis=-1, keepdims=True)
    mean = total / model
    for k, grad_ref in enumerate(grad_refs):
        for j in range(2):
            cols = column_block(k, j, width)
            weighted = gain_ref[:, cols] * grad_ref[:, j * width : (j + 1) * width].astype(f32)
            scaled = tok_ref[:, cols].astype(f32) * inv_rms
            out_ref[:, cols] = (inv_rms * (weighted - scaled * mean)).astype(bf16)


def grad_x_blocks(tokens, gain, part, grads):
    rows, model = tokens.shape
    feats = part.shape[-1]
    step = min(rows, 32)
    return pl.pallas_call(
        grad_x_kernel,
        grid=(rows // step,),
        in_specs=[
            pl.BlockSpec((step, model), lambda i: (i, 0)),
            pl.BlockSpec((1, model), lambda i: (0, 0)),
            pl.BlockSpec((step, feats), lambda i: (i, 0)),
        ]
        + [pl.BlockSpec((step, g.shape[1]), lambda i: (i, 0)) for g in grads],
        out_specs=[
            pl.BlockSpec((step, model), lambda i: (i, 0)),
            pl.BlockSpec((step, feats), lambda i: (i, 0)),
        ],
        out_shape=[
            jax.ShapeDtypeStruct((rows, model), bf16),
            jax.ShapeDtypeStruct((rows, feats), bf16),
        ],
        compiler_params=limit(24),
        cost_estimate=cost(16 * rows * model, 6 * rows * model),
        name="grad_x_blocks",
    )(tokens, gain, part, *grads)


def add_kernel(count, groups, *refs):
    for i, out_ref in enumerate(refs[-groups:]):
        total = refs[i * count][...].astype(f32)
        for ref in refs[i * count + 1 : (i + 1) * count]:
            total += ref[...].astype(f32)
        out_ref[...] = total.astype(out_ref.dtype)


def relay(sums, after):
    shape = sums[0][0].shape
    size = shape[0] * shape[1]
    return pl.pallas_call(
        functools.partial(add_kernel, len(sums[0]), len(sums)),
        in_specs=[pl.BlockSpec(memory_space=pltpu.VMEM)] * (len(sums) * len(sums[0]))
        + [pl.BlockSpec(memory_space=pl.ANY)] * len(after),
        out_shape=[jax.ShapeDtypeStruct(shape, bf16)] * len(sums),
        compiler_params=limit(16),
        cost_estimate=cost(2 * size, 12 * size),
        name="relay",
    )(*[a for group in sums for a in group], *after)


def finish_kernel(own_ref, even_ref, odd_ref, *refs):
    kept_ref, sent_ref = refs[-2:]
    half = kept_ref.shape[0]
    for part, out_ref in ((slice(half), kept_ref), (slice(half, 2 * half), sent_ref)):
        total = own_ref[part, :].astype(f32) + even_ref[part, :].astype(f32)
        out_ref[...] = (total + odd_ref[part, :].astype(f32)).astype(out_ref.dtype)


def finish(own, even, odd, after):
    height, width = own.shape
    return pl.pallas_call(
        finish_kernel,
        in_specs=[pl.BlockSpec(memory_space=pltpu.VMEM)] * 3
        + [pl.BlockSpec(memory_space=pl.ANY)] * len(after),
        out_shape=[
            jax.ShapeDtypeStruct((height // 2, width), f32),
            jax.ShapeDtypeStruct((height // 2, width), bf16),
        ],
        compiler_params=limit(16),
        cost_estimate=cost(2 * height * width, 9 * height * width),
        name="finish",
    )(own, even, odd, *after)


def adam_kernel(token_total, parts, at_ref, owner_ref, *refs):
    grad_refs, refs = refs[:parts], refs[parts:]
    master_ref, moment1_ref, moment2_ref = refs[:3]
    out_refs = refs[-3:]
    step, width = grad_refs[0].shape
    owned = (owner_ref[...] == lax.axis_index("dp")).astype(f32)
    count = jnp.sum(owned, axis=1, keepdims=True)
    index = pl.program_id(0) * step + lax.broadcasted_iota(jnp.int32, (step, 1), 0)
    occupied = (index.astype(f32) < count).astype(f32)
    for part, ref in enumerate(grad_refs):
        cols = slice(part * width, (part + 1) * width)
        slot_grad = ref[...].astype(f32) / token_total
        new_moment1 = (beta_one * moment1_ref[:, cols] + (1.0 - beta_one) * slot_grad) * occupied
        new_moment2 = (
            beta_two * moment2_ref[:, cols] + (1.0 - beta_two) * slot_grad * slot_grad
        ) * occupied
        step_dir = new_moment1 / bias_one / (jnp.sqrt(new_moment2 / bias_two) + adam_eps)
        out_refs[0][:, cols] = (master_ref[:, cols] - learn_rate * step_dir) * occupied
        out_refs[1][:, cols] = new_moment1
        out_refs[2][:, cols] = new_moment2


def adam(at, owner, grads, states, token_total, into, after):
    slots, cols = states[0].shape
    parts = len(grads)
    width = grads[0].shape[-1]
    step = min(slots, 32)
    half = pl.BlockSpec((step, cols // 2), lambda i, at: (i, at[0]))
    return pl.pallas_call(
        functools.partial(adam_kernel, token_total, parts),
        grid_spec=pltpu.PrefetchScalarGridSpec(
            num_scalar_prefetch=1,
            grid=(slots // step,),
            in_specs=[pl.BlockSpec(owner.shape, lambda i, at: (0, 0))]
            + [pl.BlockSpec((step, width), lambda i, at: (i, 0))] * parts
            + [half] * 3
            + [pl.BlockSpec(memory_space=pl.ANY)] * (len(into) + len(after)),
            out_specs=[half] * 3,
        ),
        out_shape=[jax.ShapeDtypeStruct((slots, cols), f32)] * 3,
        input_output_aliases={5 + parts + i: i for i in range(len(into))},
        compiler_params=limit(24),
        name="adam",
    )(at, owner, *grads, *states, *into, *after)


def on_device(groups, seqs, tokens, gain, w_t, grad_values, owner, master, moment1, moment2):
    planes = groups // 2
    chips = seqs
    parts = column_parts
    tokens, value_grad = tokens[0], grad_values[0]
    rows, model = tokens.shape
    feats = owner.shape[0]
    slots = master.shape[1]
    width = model // (2 * seqs)
    own_x = lax.axis_index("dp") % 2

    def permute(value, target):
        pairs = []
        for dp in range(groups):
            for seq in range(seqs):
                to = target(dp, seq)
                if to is not None:
                    pairs.append((dp * seqs + seq, to[0] * seqs + to[1]))
        return lax.ppermute(value, ("dp", "seq"), pairs)

    def to_chip(value, k):
        return permute(value, lambda dp, seq: (dp ^ (k & 1), seq ^ (k >> 1 << 1)))

    def to_core(value):
        return permute(value, lambda dp, seq: (dp, seq ^ 1))

    def to_x(value):
        return permute(value, lambda dp, seq: (dp ^ 1, seq))

    def to_plane(value, turn):
        return permute(value, lambda dp, seq: (dp ^ (2 * turn), seq))

    def busy(z, step, even):
        rightward = (z % 2 == 0) == even
        return z < step if rightward else planes - 1 - z < step

    def across(value, step, even):
        def target(dp, seq):
            z = dp // 2
            way = 1 if (z % 2 == 0) == even else -1
            return (dp + 2 * way, seq) if busy(z, step, even) else None

        return permute(value, target)

    tokens_far = to_core(tokens)
    grads = [value_grad] + [to_chip(value_grad, k) for k in range(chips - 1, 0, -1)][::-1]

    w_keep, w_send = halves(w_t, width)
    w_got = to_x(w_send)

    gain_row, owner_row = gain[None, :], owner[None, :]
    sent = norm_blocks(tokens, tokens_far, gain_row, chips, width, parts)
    grads = stack(grads, 2, sent[0][:1])
    pieces = [sent[0]] + [[to_chip(p, k) for p in sent[k]] for k in range(1, chips)]
    grads_far = [to_core(g) for g in grads]
    selected = select_rows(owner_row, groups, slots, (sent[0][0],))

    weights = stack([w_keep, w_got], 1, grads_far[:1])
    turn = planes // 2
    while turn:
        weights = [w for value in weights for w in (value, to_plane(value, turn))]
        turn //= 2
    weights_far = [to_core(w) for w in weights]

    plan = [
        (step, even)
        for step in range(1, planes)
        for even in (True, False)
        if any(busy(z, step, even) for z in range(planes))
    ]
    kept, got = [], []
    for part in range(parts):
        outs = weight_blocks(
            selected,
            [*grads, *grads_far],
            [piece[part] for piece in pieces],
            planes,
            plan,
            weights if part == parts - 1 else [],
        )
        ready = dict(zip(plan, outs))
        if part == parts - 1:
            *far_sums, near_sum = value_parts(pieces, weights, feats, outs[:1])
            sums = [near_sum] + [to_core(f) for f in far_sums]
            back = back_blocks(grads, sums, weights + weights_far, chips)
            home = [back[0]] + [to_chip(back[k], k) for k in range(1, chips)]
        held = {}
        for step in range(1, planes):
            here = [even for even in (True, False) if (step, even) in ready]
            send = [ready[step, even] for even in here]
            if held:
                sums = [[ready[step, even], held[not even]] for even in here if (not even) in held]
                if sums:
                    sums = list(relay(sums, back[:1] if step == 2 else home[-1:]))
                send = []
                for even in here:
                    send.append(sums.pop(0) if (not even) in held else ready[step, even])
            held = {even: across(value, step, even) for even, value in zip(here, send)}
        keep, send = finish(outs[-1], held[True], held[False], home[1:])
        kept.append(keep)
        got.append(to_x(send))

    grad_x, values = grad_x_blocks(tokens, gain_row, back[-1], home)

    states = (master[0], moment1[0], moment2[0])
    total = rows * seqs * groups
    at = own_x.astype(jnp.int32)[None]
    new = adam(at, owner_row, kept, states, total, (), (grad_x,))
    new = adam(1 - at, owner_row, got, states, total, new, ())
    return (values[None], grad_x[None], *(n[None] for n in new))


def solution(mesh):
    placed = (
        P("dp", "seq", None),
        P(),
        P("dp", "seq"),
        P("dp", "seq", None),
        P(),
        P("dp", None, "seq"),
        P("dp", None, "seq"),
        P("dp", None, "seq"),
    )
    return jax.shard_map(
        functools.partial(on_device, mesh.shape["dp"], mesh.shape["seq"]),
        mesh=mesh,
        in_specs=placed,
        out_specs=(
            P("dp", "seq", None),
            P("dp", "seq", None),
            P("dp", None, "seq"),
            P("dp", None, "seq"),
            P("dp", None, "seq"),
        ),
        check_vma=False,
    )
```

```python
import functools

import jax
import jax.numpy as jnp
from jax import lax
from jax.experimental import pallas as pl
from jax.experimental.pallas import tpu as pltpu
from jax.sharding import PartitionSpec as P

beta_one = 0.9
beta_two = 0.95
learn_rate = 0.001
adam_eps = 1e-08
bias_one = 1.0 - 0.9**10
bias_two = 1.0 - 0.95**10
norm_eps = 1e-05
column_parts = 1

bf16 = jnp.bfloat16
f32 = jnp.float32


def cost(flops, moved):
    return pl.CostEstimate(flops=flops, bytes_accessed=moved, transcendentals=0)


def limit(mib):
    return pltpu.CompilerParams(vmem_limit_bytes=mib * 1024 * 1024)


def column_block(k, j, width, part=0, parts=1):
    seq = lax.axis_index("seq") ^ (k >> 1 << 1) ^ j
    x = (lax.axis_index("dp") % 2) ^ (k & 1)
    return pl.ds(pl.multiple_of(((seq * 2 + x) * parts + part) * width, width), width)


def norm_kernel(parts, tok_ref, far_ref, gain_ref, *refs):
    out_refs = [refs[i : i + parts] for i in range(0, len(refs), parts)]
    chips = len(out_refs)
    width = out_refs[0][0].shape[-1]
    for i, ref in enumerate((tok_ref, far_ref)):
        tok = ref[...].astype(f32)
        inv_rms = lax.rsqrt(jnp.mean(tok * tok, axis=-1, keepdims=True) + norm_eps)
        for k in (*range(1, chips), 0):
            for part in range(parts):
                cols = column_block(k, 0, width, part, parts)
                scaled = ref[:, cols].astype(f32) * inv_rms
                out_refs[k][part][i] = (scaled * gain_ref[:, cols]).astype(bf16)


def norm_blocks(tokens, far, gain, chips, width, parts):
    rows, model = tokens.shape
    step = min(rows, 32)
    outs = pl.pallas_call(
        functools.partial(norm_kernel, parts),
        grid=(rows // step,),
        in_specs=[
            pl.BlockSpec((step, model), lambda i: (i, 0)),
            pl.BlockSpec((step, model), lambda i: (i, 0)),
            pl.BlockSpec((1, model), lambda i: (0, 0)),
        ],
        out_specs=[pl.BlockSpec((2, step, width // parts), lambda i: (0, i, 0))] * (chips * parts),
        out_shape=[jax.ShapeDtypeStruct((2, rows, width // parts), bf16)] * (chips * parts),
        compiler_params=limit(24),
        cost_estimate=cost(8 * rows * model, 6 * rows * model),
        name="norm_blocks",
    )(
        pltpu.with_memory_space_constraint(tokens, pltpu.HBM),
        far,
        pltpu.with_memory_space_constraint(gain, pltpu.HBM),
    )
    return [outs[i : i + parts] for i in range(0, len(outs), parts)]


def halves_kernel(w_ref, keep_ref, send_ref):
    width = keep_ref.shape[1]
    own_x = lax.axis_index("dp") % 2
    keep_ref[...] = w_ref[:, pl.ds(pl.multiple_of(own_x * width, width), width)]
    send_ref[...] = w_ref[:, pl.ds(pl.multiple_of((1 - own_x) * width, width), width)]


def halves(w_t, width):
    return pl.pallas_call(
        halves_kernel,
        out_shape=[jax.ShapeDtypeStruct((w_t.shape[0], width), bf16)] * 2,
        compiler_params=limit(16),
        name="halves",
    )(pltpu.with_memory_space_constraint(w_t, pltpu.HBM))


def stack_kernel(count, *refs):
    out_refs = refs[-(len(refs) - count) :]
    rows = refs[0].shape[0]
    if len(out_refs) == 3:
        stack_kernel(count, *refs[:count], out_refs[2])
        out_refs = out_refs[:2]
    each = out_refs[0].shape[0] // rows
    for i, ref in enumerate(refs[:count]):
        out_refs[i // each][i % each * rows : (i % each + 1) * rows, :] = ref[...]


def stack(pieces, outs, after):
    count = len(pieces)
    rows, width = pieces[0].shape
    return pl.pallas_call(
        lambda *refs: stack_kernel(count, *refs[:count], *refs[count + len(after) :]),
        in_specs=[pl.BlockSpec(memory_space=pltpu.VMEM)] * count
        + [pl.BlockSpec(memory_space=pl.ANY)] * len(after),
        out_shape=[jax.ShapeDtypeStruct((count // outs * rows, width), bf16)] * outs
        + [jax.ShapeDtypeStruct((count * rows, width), bf16)] * (outs > 1),
        compiler_params=limit(16),
        name="stack",
    )(*pieces, *after)


def select_kernel(groups, slots, owner_ref, *refs):
    out_ref = refs[-1]
    feats = owner_ref.shape[1]
    owner = owner_ref[...]
    lower = lax.broadcasted_iota(jnp.int32, (feats, feats), 0) < lax.broadcasted_iota(
        jnp.int32, (feats, feats), 1
    )
    owned = (lax.broadcasted_iota(jnp.int32, (groups, feats), 0) == owner).astype(f32)
    before = jnp.dot(
        owned.astype(bf16), lower.astype(f32).astype(bf16), preferred_element_type=f32
    )
    place = jnp.sum(owned * before, axis=0, keepdims=True).astype(jnp.int32)
    own_x = lax.axis_index("dp") % 2
    slot = (owner ^ own_x) * slots + place
    step = 256
    for at in range(0, out_ref.shape[0], step):
        index = at + lax.broadcasted_iota(jnp.int32, (step, feats), 0)
        out_ref[at : at + step, :] = (index == slot).astype(f32).astype(bf16)


def select_rows(owner, groups, slots, after):
    feats = owner.shape[1]
    return pl.pallas_call(
        functools.partial(select_kernel, groups, slots),
        in_specs=[pl.BlockSpec(memory_space=pltpu.VMEM)]
        + [pl.BlockSpec(memory_space=pl.ANY)] * len(after),
        out_shape=jax.ShapeDtypeStruct((groups * slots, feats), bf16),
        compiler_params=limit(24),
        cost_estimate=cost(4 * groups * slots * feats, 2 * groups * slots * feats),
        name="select_rows",
    )(owner, *after)


def weight_kernel(planes, chips, plan, *refs):
    sel_ref, refs = refs[0], refs[1:]
    grad_refs, refs = [*refs[:2], refs[2].at[: refs[0].shape[0]], refs[2].at[refs[0].shape[0] :]], refs[3:]
    pieces, refs = refs[:chips], refs[chips:]
    out_refs, (held, base) = refs[-len(plan) - 3 : -2], refs[-2:]
    rows = pieces[0].shape[1]
    feats = sel_ref.shape[1]
    block = sel_ref.shape[0] // planes
    half = chips // 2
    z = lax.axis_index("dp") // 2
    for k in range(chips):
        for i in range(2):
            at = k % half * rows
            held[2 * i + k // half, at : at + rows, :] = pieces[k][i]
    for at in range(0, feats, 256):
        total = None
        for i in range(4):
            term = lax.dot_general(
                grad_refs[i][:, at : at + 256],
                held[i],
                (((0,), (0,)), ((), ())),
                preferred_element_type=f32,
            )
            total = term if total is None else total + term
        base[at : at + 256, :] = total.astype(bf16)

    def chosen(plane):
        at = pl.multiple_of(plane * block, block)
        return jnp.dot(sel_ref[pl.ds(at, block), :], base[...], preferred_element_type=f32)

    for (step, even), out_ref in zip(plan, out_refs):
        ahead = planes - step
        plane = jnp.where((z % 2 == 0) == even, z + ahead, z - ahead)

        @pl.when((plane >= 0) & (plane < planes))
        def _():
            out_ref[...] = chosen(plane).astype(bf16)

    out_refs[-1][...] = chosen(z).astype(bf16)


def weight_blocks(selected, grads, pieces, planes, plan, after):
    chips = len(pieces)
    slots_all, feats = selected.shape
    _, rows, width = pieces[0].shape
    total = 2 * chips * rows
    block = slots_all // planes
    return pl.pallas_call(
        functools.partial(weight_kernel, planes, chips, plan),
        in_specs=[pl.BlockSpec(memory_space=pltpu.VMEM)] * (4 + chips)
        + [pl.BlockSpec(memory_space=pl.ANY)] * len(after),
        out_shape=[jax.ShapeDtypeStruct((block, width), bf16)] * (len(plan) + 1),
        scratch_shapes=[
            pltpu.VMEM((4, total // 4, width), bf16),
            pltpu.VMEM((feats, width), bf16),
        ],
        compiler_params=limit(40),
        cost_estimate=cost(2 * (slots_all + total) * feats * width, 4 * total * width),
        name="weight_blocks",
    )(selected, *grads, *pieces, *after)


def gather_weight(piece_refs, held):
    dp = lax.axis_index("dp")
    own_x, own_z = dp % 2, dp // 2
    for turn, ref in enumerate(piece_refs):
        share = ref.shape[0] // 2
        for i in range(2):
            at = pl.multiple_of(((own_z ^ turn) * 2 + (own_x ^ i)) * share, share)
            held[pl.ds(at, share), :] = ref[i * share : (i + 1) * share, :]


def value_kernel(planes, chips, parts, *refs):
    piece_refs, refs = refs[: chips * parts], refs[chips * parts :]
    far_refs, out_ref, held = refs[-4:-2], refs[-2], refs[-1]
    rows = out_ref.shape[0] // chips
    half = chips // 2
    part_width = held.shape[1] // parts
    gather_weight(refs[:planes], held)
    for k in range(chips):
        total = None
        for part in range(parts):
            piece = piece_refs[k * parts + part][...]
            term = lax.dot_general(
                piece.reshape(2 * rows, part_width),
                held[:, part * part_width : (part + 1) * part_width],
                (((1,), (1,)), ((), ())),
                preferred_element_type=f32,
            )
            total = term if total is None else total + term
        out_ref[k * rows : (k + 1) * rows, :] = total[:rows]
        at = k % half * rows
        far_refs[k // half][at : at + rows, :] = total[rows:].astype(bf16)


def value_parts(pieces, weights, feats, after):
    chips, parts = len(pieces), len(pieces[0])
    rows = pieces[0][0].shape[1]
    width = weights[0].shape[-1]
    return pl.pallas_call(
        functools.partial(value_kernel, len(weights), chips, parts),
        in_specs=[pl.BlockSpec(memory_space=pltpu.VMEM)] * (chips * parts + len(weights))
        + [pl.BlockSpec(memory_space=pl.ANY)] * len(after),
        out_shape=[jax.ShapeDtypeStruct((chips // 2 * rows, feats), bf16)] * 2
        + [jax.ShapeDtypeStruct((chips * rows, feats), f32)],
        scratch_shapes=[pltpu.VMEM((feats, width), bf16)],
        compiler_params=limit(40),
        name="value_parts",
    )(*[p for piece in pieces for p in piece], *weights, *after)


def back_kernel(planes, chips, grads_a_ref, grads_b_ref, value_ref, got_a_ref, got_b_ref, *refs):
    weight_refs, refs = refs[: 2 * planes], refs[2 * planes :]
    out_refs, own_ref, held = refs[-chips - 2 : -2], refs[-2], refs[-1]
    rows, feats = own_ref.shape
    width = held.shape[1]
    half = chips // 2
    for k in range(chips):
        got_ref = got_b_ref if k // half else got_a_ref
        total = value_ref[k * rows : (k + 1) * rows, :]
        total += got_ref[k % half * rows : (k % half + 1) * rows, :].astype(f32)
        if k == 0:
            own_ref[...] = total
        else:
            out_refs[k][:, 2 * width :] = total.astype(bf16)
    for j in range(2):
        gather_weight(weight_refs[j * planes : (j + 1) * planes], held)
        for i, grads_ref in enumerate((grads_a_ref, grads_b_ref)):
            block = jnp.dot(grads_ref[...], held[...], preferred_element_type=f32).astype(bf16)
            for k in range(half):
                out_refs[i * half + k][:, j * width : (j + 1) * width] = block[
                    k * rows : (k + 1) * rows, :
                ]


def back_blocks(grads, sums, weights, chips):
    rows, feats = 2 * grads[0].shape[0] // chips, grads[0].shape[1]
    width = weights[0].shape[-1]
    return pl.pallas_call(
        functools.partial(back_kernel, len(weights) // 2, chips),
        out_shape=[
            jax.ShapeDtypeStruct((rows, 2 * width + (feats if k else 0)), bf16)
            for k in range(chips)
        ]
        + [jax.ShapeDtypeStruct((rows, feats), f32)],
        scratch_shapes=[pltpu.VMEM((feats, width), bf16)],
        compiler_params=limit(40),
        name="back_blocks",
    )(*grads, *sums, *weights)


def grad_x_kernel(tok_ref, gain_ref, part_ref, *refs):
    grad_refs, (out_ref, values_ref) = refs[:-2], refs[-2:]
    model = tok_ref.shape[-1]
    width = grad_refs[0].shape[-1] // 2
    values = part_ref[...]
    for grad_ref in grad_refs[1:]:
        values += grad_ref[:, 2 * width :].astype(f32)
    values_ref[...] = values.astype(bf16)
    tok = tok_ref[...].astype(f32)
    inv_rms = lax.rsqrt(jnp.mean(tok * tok, axis=-1, keepdims=True) + norm_eps)
    total = jnp.zeros((tok.shape[0], 1), f32)
    for k, grad_ref in enumerate(grad_refs):
        for j in range(2):
            cols = column_block(k, j, width)
            weighted = gain_ref[:, cols] * grad_ref[:, j * width : (j + 1) * width].astype(f32)
            scaled = tok_ref[:, cols].astype(f32) * inv_rms
            total += jnp.sum(weighted * scaled, axis=-1, keepdims=True)
    mean = total / model
    for k, grad_ref in enumerate(grad_refs):
        for j in range(2):
            cols = column_block(k, j, width)
            weighted = gain_ref[:, cols] * grad_ref[:, j * width : (j + 1) * width].astype(f32)
            scaled = tok_ref[:, cols].astype(f32) * inv_rms
            out_ref[:, cols] = (inv_rms * (weighted - scaled * mean)).astype(bf16)


def grad_x_blocks(tokens, gain, part, grads):
    rows, model = tokens.shape
    feats = part.shape[-1]
    step = min(rows, 32)
    return pl.pallas_call(
        grad_x_kernel,
        grid=(rows // step,),
        in_specs=[
            pl.BlockSpec((step, model), lambda i: (i, 0)),
            pl.BlockSpec((1, model), lambda i: (0, 0)),
            pl.BlockSpec((step, feats), lambda i: (i, 0)),
        ]
        + [pl.BlockSpec((step, g.shape[1]), lambda i: (i, 0)) for g in grads],
        out_specs=[
            pl.BlockSpec((step, model), lambda i: (i, 0)),
            pl.BlockSpec((step, feats), lambda i: (i, 0)),
        ],
        out_shape=[
            jax.ShapeDtypeStruct((rows, model), bf16),
            jax.ShapeDtypeStruct((rows, feats), bf16),
        ],
        compiler_params=limit(24),
        cost_estimate=cost(16 * rows * model, 6 * rows * model),
        name="grad_x_blocks",
    )(tokens, gain, part, *grads)


def add_kernel(count, groups, *refs):
    for i, out_ref in enumerate(refs[-groups:]):
        total = refs[i * count][...].astype(f32)
        for ref in refs[i * count + 1 : (i + 1) * count]:
            total += ref[...].astype(f32)
        out_ref[...] = total.astype(out_ref.dtype)


def relay(sums, after):
    shape = sums[0][0].shape
    size = shape[0] * shape[1]
    return pl.pallas_call(
        functools.partial(add_kernel, len(sums[0]), len(sums)),
        in_specs=[pl.BlockSpec(memory_space=pltpu.VMEM)] * (len(sums) * len(sums[0]))
        + [pl.BlockSpec(memory_space=pl.ANY)] * len(after),
        out_shape=[jax.ShapeDtypeStruct(shape, bf16)] * len(sums),
        compiler_params=limit(16),
        cost_estimate=cost(2 * size, 12 * size),
        name="relay",
    )(*[a for group in sums for a in group], *after)


def finish_kernel(own_ref, even_ref, odd_ref, *refs):
    kept_ref, sent_ref = refs[-2:]
    half = kept_ref.shape[0]
    for part, out_ref in ((slice(half), kept_ref), (slice(half, 2 * half), sent_ref)):
        total = own_ref[part, :].astype(f32) + even_ref[part, :].astype(f32)
        out_ref[...] = (total + odd_ref[part, :].astype(f32)).astype(out_ref.dtype)


def finish(own, even, odd, after):
    height, width = own.shape
    return pl.pallas_call(
        finish_kernel,
        in_specs=[pl.BlockSpec(memory_space=pltpu.VMEM)] * 3
        + [pl.BlockSpec(memory_space=pl.ANY)] * len(after),
        out_shape=[
            jax.ShapeDtypeStruct((height // 2, width), f32),
            jax.ShapeDtypeStruct((height // 2, width), bf16),
        ],
        compiler_params=limit(16),
        cost_estimate=cost(2 * height * width, 9 * height * width),
        name="finish",
    )(own, even, odd, *after)


def adam_kernel(token_total, parts, owner_ref, *refs):
    kept_refs, got_refs, refs = refs[:parts], refs[parts : 2 * parts], refs[2 * parts :]
    master_ref, moment1_ref, moment2_ref = refs[:3]
    out_refs = refs[3:]
    step, width = kept_refs[0].shape
    dp = lax.axis_index("dp")
    owned = (owner_ref[...] == dp).astype(f32)
    count = jnp.sum(owned, axis=1, keepdims=True)
    index = pl.program_id(0) * step + lax.broadcasted_iota(jnp.int32, (step, 1), 0)
    occupied = (index.astype(f32) < count).astype(f32)
    for i, refs in enumerate((kept_refs, got_refs)):
        for part, ref in enumerate(refs):
            at = (((dp % 2) ^ i) * parts + part) * width
            cols = pl.ds(pl.multiple_of(at, width), width)
            slot_grad = ref[...].astype(f32) / token_total
            new_moment1 = (
                beta_one * moment1_ref[:, cols] + (1.0 - beta_one) * slot_grad
            ) * occupied
            new_moment2 = (
                beta_two * moment2_ref[:, cols] + (1.0 - beta_two) * slot_grad * slot_grad
            ) * occupied
            step_dir = new_moment1 / bias_one / (jnp.sqrt(new_moment2 / bias_two) + adam_eps)
            out_refs[0][:, cols] = (master_ref[:, cols] - learn_rate * step_dir) * occupied
            out_refs[1][:, cols] = new_moment1
            out_refs[2][:, cols] = new_moment2


def adam(owner, kept, got, states, token_total):
    slots, cols = states[0].shape
    width = kept[0].shape[-1]
    step = min(slots, 32)
    return pl.pallas_call(
        functools.partial(adam_kernel, token_total, len(kept)),
        grid=(slots // step,),
        in_specs=[pl.BlockSpec(owner.shape, lambda i: (0, 0))]
        + [pl.BlockSpec((step, width), lambda i: (i, 0))] * (2 * len(kept))
        + [pl.BlockSpec((step, cols), lambda i: (i, 0))] * 3,
        out_specs=[pl.BlockSpec((step, cols), lambda i: (i, 0))] * 3,
        out_shape=[jax.ShapeDtypeStruct((slots, cols), f32)] * 3,
        compiler_params=limit(24),
        cost_estimate=cost(20 * slots * cols, 30 * slots * cols),
        name="adam",
    )(owner, *kept, *got, *states)


def on_device(groups, seqs, tokens, gain, w_t, grad_values, owner, master, moment1, moment2):
    planes = groups // 2
    chips = seqs
    parts = column_parts
    tokens, value_grad = tokens[0], grad_values[0]
    rows, model = tokens.shape
    feats = owner.shape[0]
    slots = master.shape[1]
    width = model // (2 * seqs)
    own_x = lax.axis_index("dp") % 2

    def permute(value, target):
        pairs = []
        for dp in range(groups):
            for seq in range(seqs):
                to = target(dp, seq)
                if to is not None:
                    pairs.append((dp * seqs + seq, to[0] * seqs + to[1]))
        return lax.ppermute(value, ("dp", "seq"), pairs)

    def to_chip(value, k):
        return permute(value, lambda dp, seq: (dp ^ (k & 1), seq ^ (k >> 1 << 1)))

    def to_core(value):
        return permute(value, lambda dp, seq: (dp, seq ^ 1))

    def to_x(value):
        return permute(value, lambda dp, seq: (dp ^ 1, seq))

    def to_plane(value, turn):
        return permute(value, lambda dp, seq: (dp ^ (2 * turn), seq))

    def busy(z, step, even):
        rightward = (z % 2 == 0) == even
        return z < step if rightward else planes - 1 - z < step

    def across(value, step, even):
        def target(dp, seq):
            z = dp // 2
            way = 1 if (z % 2 == 0) == even else -1
            return (dp + 2 * way, seq) if busy(z, step, even) else None

        return permute(value, target)

    tokens_far = to_core(tokens)
    grads = [value_grad] + [to_chip(value_grad, k) for k in range(chips - 1, 0, -1)][::-1]

    w_keep, w_send = halves(w_t, width)
    w_got = to_x(w_send)

    gain_row, owner_row = gain[None, :], owner[None, :]
    sent = norm_blocks(tokens, tokens_far, gain_row, chips, width, parts)
    grads = stack(grads, 2, [sent[0][0], w_keep])
    pieces = [sent[0]] + [[to_chip(p, k) for p in sent[k]] for k in range(1, chips)]
    grads_far = [to_core(grads[-1])]
    grads = grads[:2]
    selected = select_rows(owner_row, groups, slots, (sent[0][0],))

    weights = stack([w_keep, w_got], 1, grads_far[:1])
    turn = planes // 2
    while turn:
        weights = [w for value in weights for w in (value, to_plane(value, turn))]
        turn //= 2
    weights_far = [to_core(w) for w in weights]

    plan = [
        (step, even)
        for step in range(1, planes)
        for even in (True, False)
        if any(busy(z, step, even) for z in range(planes))
    ]
    outs = []
    for part in range(parts):
        outs.append(
            weight_blocks(
                selected,
                [*grads, *grads_far],
                [piece[part] for piece in pieces],
                planes,
                plan,
                weights if part == parts - 1 else [],
            )
        )

    *far_sums, near_sum = value_parts(pieces, weights, feats, outs[-1][:1])
    sums = [near_sum] + [to_core(f) for f in far_sums]
    back = back_blocks(grads, sums, weights + weights_far, chips)
    home = [back[0]] + [to_chip(back[k], k) for k in range(1, chips)]

    kept, got = [], []
    for part in range(parts):
        ready, held = dict(zip(plan, outs[part])), {}
        final = part == parts - 1
        for step in range(1, planes):
            here = [even for even in (True, False) if (step, even) in ready]
            sums = [[ready[step, even], held[not even]] for even in here if (not even) in held]
            if sums:
                after = (back[:1] if step == 2 else home[-1:]) if final else []
                sums = list(relay(sums, after))
            send = [
                sums.pop(0) if (not even) in held else ready[step, even] for even in here
            ]
            held = {even: across(value, step, even) for even, value in zip(here, send)}
        after = home[1:] if final else []
        keep, send = finish(outs[part][-1], held[True], held[False], after)
        kept.append(keep)
        got.append(to_x(send))
    grad_x, values = grad_x_blocks(tokens, gain_row, back[-1], home)

    states = adam(owner_row, kept, got, (master[0], moment1[0], moment2[0]), rows * seqs * groups)
    return (values[None], grad_x[None], *(s[None] for s in states))


def solution(mesh):
    placed = (
        P("dp", "seq", None),
        P(),
        P("dp", "seq"),
        P("dp", "seq", None),
        P(),
        P("dp", None, "seq"),
        P("dp", None, "seq"),
        P("dp", None, "seq"),
    )
    return jax.shard_map(
        functools.partial(on_device, mesh.shape["dp"], mesh.shape["seq"]),
        mesh=mesh,
        in_specs=placed,
        out_specs=(
            P("dp", "seq", None),
            P("dp", "seq", None),
            P("dp", None, "seq"),
            P("dp", None, "seq"),
            P("dp", None, "seq"),
        ),
        check_vma=False,
    )
```

```python
import functools

import jax
import jax.numpy as jnp
from jax import lax
from jax.experimental import pallas as pl
from jax.experimental.pallas import tpu as pltpu
from jax.sharding import PartitionSpec as P

beta_one = 0.9
beta_two = 0.95
learn_rate = 0.001
adam_eps = 1e-08
bias_one = 1.0 - 0.9**10
bias_two = 1.0 - 0.95**10
norm_eps = 1e-05
column_parts = 1

bf16 = jnp.bfloat16
f32 = jnp.float32


def cost(flops, moved):
    return pl.CostEstimate(flops=flops, bytes_accessed=moved, transcendentals=0)


def limit(mib):
    return pltpu.CompilerParams(vmem_limit_bytes=mib * 1024 * 1024)


def column_block(k, j, width, part=0, parts=1):
    seq = lax.axis_index("seq") ^ (k >> 1 << 1) ^ j
    x = (lax.axis_index("dp") % 2) ^ (k & 1)
    return pl.ds(pl.multiple_of(((seq * 2 + x) * parts + part) * width, width), width)


def norm_kernel(parts, tok_ref, far_ref, gain_ref, *refs):
    out_refs = [refs[i : i + parts] for i in range(0, len(refs), parts)]
    chips = len(out_refs)
    width = out_refs[0][0].shape[-1]
    for i, ref in enumerate((tok_ref, far_ref)):
        tok = ref[...].astype(f32)
        inv_rms = lax.rsqrt(jnp.mean(tok * tok, axis=-1, keepdims=True) + norm_eps)
        for k in (*range(1, chips), 0):
            for part in range(parts):
                cols = column_block(k, 0, width, part, parts)
                scaled = ref[:, cols].astype(f32) * inv_rms
                out_refs[k][part][i] = (scaled * gain_ref[:, cols]).astype(bf16)


def norm_blocks(tokens, far, gain, chips, width, parts):
    rows, model = tokens.shape
    step = min(rows, 32)
    outs = pl.pallas_call(
        functools.partial(norm_kernel, parts),
        grid=(rows // step,),
        in_specs=[
            pl.BlockSpec((step, model), lambda i: (i, 0)),
            pl.BlockSpec((step, model), lambda i: (i, 0)),
            pl.BlockSpec((1, model), lambda i: (0, 0)),
        ],
        out_specs=[pl.BlockSpec((2, step, width // parts), lambda i: (0, i, 0))] * (chips * parts),
        out_shape=[jax.ShapeDtypeStruct((2, rows, width // parts), bf16)] * (chips * parts),
        compiler_params=limit(24),
        cost_estimate=cost(8 * rows * model, 6 * rows * model),
        name="norm_blocks",
    )(
        pltpu.with_memory_space_constraint(tokens, pltpu.HBM),
        far,
        pltpu.with_memory_space_constraint(gain, pltpu.HBM),
    )
    return [outs[i : i + parts] for i in range(0, len(outs), parts)]


def halves_kernel(w_ref, keep_ref, send_ref):
    width = keep_ref.shape[1]
    own_x = lax.axis_index("dp") % 2
    keep_ref[...] = w_ref[:, pl.ds(pl.multiple_of(own_x * width, width), width)]
    send_ref[...] = w_ref[:, pl.ds(pl.multiple_of((1 - own_x) * width, width), width)]


def halves(w_t, width):
    return pl.pallas_call(
        halves_kernel,
        out_shape=[jax.ShapeDtypeStruct((w_t.shape[0], width), bf16)] * 2,
        compiler_params=limit(16),
        name="halves",
    )(pltpu.with_memory_space_constraint(w_t, pltpu.HBM))


def stack_kernel(count, *refs):
    out_refs = refs[-(len(refs) - count) :]
    rows = refs[0].shape[0]
    if len(out_refs) == 3:
        stack_kernel(count, *refs[:count], out_refs[2])
        out_refs = out_refs[:2]
    each = out_refs[0].shape[0] // rows
    for i, ref in enumerate(refs[:count]):
        out_refs[i // each][i % each * rows : (i % each + 1) * rows, :] = ref[...]


def stack(pieces, outs, after):
    count = len(pieces)
    rows, width = pieces[0].shape
    return pl.pallas_call(
        lambda *refs: stack_kernel(count, *refs[:count], *refs[count + len(after) :]),
        in_specs=[pl.BlockSpec(memory_space=pltpu.VMEM)] * count
        + [pl.BlockSpec(memory_space=pl.ANY)] * len(after),
        out_shape=[jax.ShapeDtypeStruct((count // outs * rows, width), bf16)] * outs
        + [jax.ShapeDtypeStruct((count * rows, width), bf16)] * (outs > 1),
        compiler_params=limit(16),
        name="stack",
    )(*pieces, *after)


def select_kernel(groups, slots, owner_ref, *refs):
    out_ref = refs[-1]
    feats = owner_ref.shape[1]
    owner = owner_ref[...]
    lower = lax.broadcasted_iota(jnp.int32, (feats, feats), 0) < lax.broadcasted_iota(
        jnp.int32, (feats, feats), 1
    )
    owned = (lax.broadcasted_iota(jnp.int32, (groups, feats), 0) == owner).astype(f32)
    before = jnp.dot(
        owned.astype(bf16), lower.astype(f32).astype(bf16), preferred_element_type=f32
    )
    place = jnp.sum(owned * before, axis=0, keepdims=True).astype(jnp.int32)
    own_x = lax.axis_index("dp") % 2
    slot = (owner ^ own_x) * slots + place
    step = 256
    for at in range(0, out_ref.shape[0], step):
        index = at + lax.broadcasted_iota(jnp.int32, (step, feats), 0)
        out_ref[at : at + step, :] = (index == slot).astype(f32).astype(bf16)


def select_rows(owner, groups, slots, after):
    feats = owner.shape[1]
    return pl.pallas_call(
        functools.partial(select_kernel, groups, slots),
        in_specs=[pl.BlockSpec(memory_space=pltpu.VMEM)]
        + [pl.BlockSpec(memory_space=pl.ANY)] * len(after),
        out_shape=jax.ShapeDtypeStruct((groups * slots, feats), bf16),
        compiler_params=limit(24),
        cost_estimate=cost(4 * groups * slots * feats, 2 * groups * slots * feats),
        name="select_rows",
    )(owner, *after)


def weight_kernel(planes, chips, plan, *refs):
    sel_ref, refs = refs[0], refs[1:]
    grad_refs, refs = [*refs[:2], refs[2].at[: refs[0].shape[0]], refs[2].at[refs[0].shape[0] :]], refs[3:]
    pieces, refs = refs[:chips], refs[chips:]
    out_refs, (held, base) = refs[-len(plan) - 3 : -2], refs[-2:]
    rows = pieces[0].shape[1]
    feats = sel_ref.shape[1]
    block = sel_ref.shape[0] // planes
    half = chips // 2
    z = lax.axis_index("dp") // 2
    for k in range(chips):
        for i in range(2):
            at = k % half * rows
            held[2 * i + k // half, at : at + rows, :] = pieces[k][i]
    for at in range(0, feats, 256):
        total = None
        for i in range(4):
            term = lax.dot_general(
                grad_refs[i][:, at : at + 256],
                held[i],
                (((0,), (0,)), ((), ())),
                preferred_element_type=f32,
            )
            total = term if total is None else total + term
        base[at : at + 256, :] = total.astype(bf16)

    def chosen(plane):
        at = pl.multiple_of(plane * block, block)
        return jnp.dot(sel_ref[pl.ds(at, block), :], base[...], preferred_element_type=f32)

    for (step, even), out_ref in zip(plan, out_refs):
        ahead = planes - step
        plane = jnp.where((z % 2 == 0) == even, z + ahead, z - ahead)

        @pl.when((plane >= 0) & (plane < planes))
        def _():
            out_ref[...] = chosen(plane).astype(bf16)

    out_refs[-1][...] = chosen(z).astype(bf16)


def weight_blocks(selected, grads, pieces, planes, plan, after):
    chips = len(pieces)
    slots_all, feats = selected.shape
    _, rows, width = pieces[0].shape
    total = 2 * chips * rows
    block = slots_all // planes
    return pl.pallas_call(
        functools.partial(weight_kernel, planes, chips, plan),
        in_specs=[pl.BlockSpec(memory_space=pltpu.VMEM)] * (4 + chips)
        + [pl.BlockSpec(memory_space=pl.ANY)] * len(after),
        out_shape=[jax.ShapeDtypeStruct((block, width), bf16)] * (len(plan) + 1),
        scratch_shapes=[
            pltpu.VMEM((4, total // 4, width), bf16),
            pltpu.VMEM((feats, width), bf16),
        ],
        compiler_params=limit(40),
        cost_estimate=cost(2 * (slots_all + total) * feats * width, 4 * total * width),
        name="weight_blocks",
    )(selected, *grads, *pieces, *after)


def gather_weight(piece_refs, held):
    dp = lax.axis_index("dp")
    own_x, own_z = dp % 2, dp // 2
    for turn, ref in enumerate(piece_refs):
        share = ref.shape[0] // 2
        for i in range(2):
            at = pl.multiple_of(((own_z ^ turn) * 2 + (own_x ^ i)) * share, share)
            held[pl.ds(at, share), :] = ref[i * share : (i + 1) * share, :]


def value_kernel(planes, chips, parts, *refs):
    piece_refs, refs = refs[: chips * parts], refs[chips * parts :]
    far_refs, out_ref, held = refs[-4:-2], refs[-2], refs[-1]
    rows = out_ref.shape[0] // chips
    half = chips // 2
    part_width = held.shape[1] // parts
    gather_weight(refs[:planes], held)
    for k in range(chips):
        total = None
        for part in range(parts):
            piece = piece_refs[k * parts + part][...]
            term = lax.dot_general(
                piece.reshape(2 * rows, part_width),
                held[:, part * part_width : (part + 1) * part_width],
                (((1,), (1,)), ((), ())),
                preferred_element_type=f32,
            )
            total = term if total is None else total + term
        out_ref[k * rows : (k + 1) * rows, :] = total[:rows]
        at = k % half * rows
        far_refs[k // half][at : at + rows, :] = total[rows:].astype(bf16)


def value_parts(pieces, weights, feats, after):
    chips, parts = len(pieces), len(pieces[0])
    rows = pieces[0][0].shape[1]
    width = weights[0].shape[-1]
    return pl.pallas_call(
        functools.partial(value_kernel, len(weights), chips, parts),
        in_specs=[pl.BlockSpec(memory_space=pltpu.VMEM)] * (chips * parts + len(weights))
        + [pl.BlockSpec(memory_space=pl.ANY)] * len(after),
        out_shape=[jax.ShapeDtypeStruct((chips // 2 * rows, feats), bf16)] * 2
        + [jax.ShapeDtypeStruct((chips * rows, feats), f32)],
        scratch_shapes=[pltpu.VMEM((feats, width), bf16)],
        compiler_params=limit(40),
        name="value_parts",
    )(*[p for piece in pieces for p in piece], *weights, *after)


def back_kernel(planes, chips, grads_a_ref, grads_b_ref, value_ref, got_a_ref, got_b_ref, *refs):
    weight_refs, refs = refs[: 2 * planes], refs[2 * planes :]
    out_refs, own_ref, held = refs[-chips - 2 : -2], refs[-2], refs[-1]
    rows, feats = own_ref.shape
    width = held.shape[1]
    half = chips // 2
    for k in range(chips):
        got_ref = got_b_ref if k // half else got_a_ref
        total = value_ref[k * rows : (k + 1) * rows, :]
        total += got_ref[k % half * rows : (k % half + 1) * rows, :].astype(f32)
        if k == 0:
            own_ref[...] = total
        else:
            out_refs[k][:, 2 * width :] = total.astype(bf16)
    for j in range(2):
        gather_weight(weight_refs[j * planes : (j + 1) * planes], held)
        for i, grads_ref in enumerate((grads_a_ref, grads_b_ref)):
            block = jnp.dot(grads_ref[...], held[...], preferred_element_type=f32).astype(bf16)
            for k in range(half):
                out_refs[i * half + k][:, j * width : (j + 1) * width] = block[
                    k * rows : (k + 1) * rows, :
                ]


def back_blocks(grads, sums, weights, chips, after):
    rows, feats = 2 * grads[0].shape[0] // chips, grads[0].shape[1]
    width = weights[0].shape[-1]
    return pl.pallas_call(
        functools.partial(back_kernel, len(weights) // 2, chips),
        in_specs=[pl.BlockSpec(memory_space=pltpu.VMEM)] * (len(grads) + len(sums) + len(weights))
        + [pl.BlockSpec(memory_space=pl.ANY)] * len(after),
        out_shape=[
            jax.ShapeDtypeStruct((rows, 2 * width + (feats if k else 0)), bf16)
            for k in range(chips)
        ]
        + [jax.ShapeDtypeStruct((rows, feats), f32)],
        scratch_shapes=[pltpu.VMEM((feats, width), bf16)],
        compiler_params=limit(40),
        name="back_blocks",
    )(*grads, *sums, *weights, *after)


def grad_x_kernel(tok_ref, gain_ref, part_ref, *refs):
    grad_refs, (out_ref, values_ref) = refs[:-2], refs[-2:]
    model = tok_ref.shape[-1]
    width = grad_refs[0].shape[-1] // 2
    values = part_ref[...]
    for grad_ref in grad_refs[1:]:
        values += grad_ref[:, 2 * width :].astype(f32)
    values_ref[...] = values.astype(bf16)
    tok = tok_ref[...].astype(f32)
    inv_rms = lax.rsqrt(jnp.mean(tok * tok, axis=-1, keepdims=True) + norm_eps)
    total = jnp.zeros((tok.shape[0], 1), f32)
    for k, grad_ref in enumerate(grad_refs):
        for j in range(2):
            cols = column_block(k, j, width)
            weighted = gain_ref[:, cols] * grad_ref[:, j * width : (j + 1) * width].astype(f32)
            scaled = tok_ref[:, cols].astype(f32) * inv_rms
            total += jnp.sum(weighted * scaled, axis=-1, keepdims=True)
    mean = total / model
    for k, grad_ref in enumerate(grad_refs):
        for j in range(2):
            cols = column_block(k, j, width)
            weighted = gain_ref[:, cols] * grad_ref[:, j * width : (j + 1) * width].astype(f32)
            scaled = tok_ref[:, cols].astype(f32) * inv_rms
            out_ref[:, cols] = (inv_rms * (weighted - scaled * mean)).astype(bf16)


def grad_x_blocks(tokens, gain, part, grads):
    rows, model = tokens.shape
    feats = part.shape[-1]
    step = min(rows, 32)
    return pl.pallas_call(
        grad_x_kernel,
        grid=(rows // step,),
        in_specs=[
            pl.BlockSpec((step, model), lambda i: (i, 0)),
            pl.BlockSpec((1, model), lambda i: (0, 0)),
            pl.BlockSpec((step, feats), lambda i: (i, 0)),
        ]
        + [pl.BlockSpec((step, g.shape[1]), lambda i: (i, 0)) for g in grads],
        out_specs=[
            pl.BlockSpec((step, model), lambda i: (i, 0)),
            pl.BlockSpec((step, feats), lambda i: (i, 0)),
        ],
        out_shape=[
            jax.ShapeDtypeStruct((rows, model), bf16),
            jax.ShapeDtypeStruct((rows, feats), bf16),
        ],
        compiler_params=limit(24),
        cost_estimate=cost(16 * rows * model, 6 * rows * model),
        name="grad_x_blocks",
    )(tokens, gain, part, *grads)


def add_kernel(halves_of, *refs):
    outs = refs[-len(halves_of) :]
    at = 0
    for half_of, out_ref in zip(halves_of, outs):
        rows = out_ref.shape[0]
        total = None
        for half in half_of:
            first = (half or 0) * rows
            term = refs[at][first : first + rows, :].astype(f32)
            total = term if total is None else total + term
            at += 1
        out_ref[...] = total.astype(out_ref.dtype)


def relay(sums, after):
    arrays = [array for group in sums for array, _ in group]
    rows, width = sums[0][0][0].shape
    shape = (rows if sums[0][0][1] is None else rows // 2, width)
    return pl.pallas_call(
        functools.partial(add_kernel, [[half for _, half in group] for group in sums]),
        in_specs=[pl.BlockSpec(memory_space=pltpu.VMEM)] * len(arrays)
        + [pl.BlockSpec(memory_space=pl.ANY)] * len(after),
        out_shape=[jax.ShapeDtypeStruct(shape, bf16)] * len(sums),
        compiler_params=limit(16),
        name="relay",
    )(*arrays, *after)


def adam_kernel(token_total, count, owner_ref, *refs):
    part_refs, got_ref, refs = refs[:count], refs[count], refs[count + 1 :]
    master_ref, moment1_ref, moment2_ref = refs[:3]
    out_refs = refs[3:]
    step, width = got_ref.shape
    dp = lax.axis_index("dp")
    owned = (owner_ref[...] == dp).astype(f32)
    count = jnp.sum(owned, axis=1, keepdims=True)
    index = pl.program_id(0) * step + lax.broadcasted_iota(jnp.int32, (step, 1), 0)
    occupied = (index.astype(f32) < count).astype(f32)
    for i, refs in enumerate((part_refs, (got_ref,))):
        total = refs[0][...].astype(f32)
        for ref in refs[1:]:
            total += ref[...].astype(f32)
        cols = pl.ds(pl.multiple_of(((dp % 2) ^ i) * width, width), width)
        slot_grad = total / token_total
        new_moment1 = (beta_one * moment1_ref[:, cols] + (1.0 - beta_one) * slot_grad) * occupied
        new_moment2 = (
            beta_two * moment2_ref[:, cols] + (1.0 - beta_two) * slot_grad * slot_grad
        ) * occupied
        step_dir = new_moment1 / bias_one / (jnp.sqrt(new_moment2 / bias_two) + adam_eps)
        out_refs[0][:, cols] = (master_ref[:, cols] - learn_rate * step_dir) * occupied
        out_refs[1][:, cols] = new_moment1
        out_refs[2][:, cols] = new_moment2


def adam(owner, parts, got, states, token_total):
    slots, cols = states[0].shape
    width = got.shape[-1]
    step = min(slots, 32)
    return pl.pallas_call(
        functools.partial(adam_kernel, token_total, len(parts)),
        grid=(slots // step,),
        in_specs=[pl.BlockSpec(owner.shape, lambda i: (0, 0))]
        + [pl.BlockSpec((step, width), lambda i: (i, 0))] * (len(parts) + 1)
        + [pl.BlockSpec((step, cols), lambda i: (i, 0))] * 3,
        out_specs=[pl.BlockSpec((step, cols), lambda i: (i, 0))] * 3,
        out_shape=[jax.ShapeDtypeStruct((slots, cols), f32)] * 3,
        compiler_params=limit(24),
        cost_estimate=cost(20 * slots * cols, 30 * slots * cols),
        name="adam",
    )(owner, *parts, got, *states)


def on_device(groups, seqs, tokens, gain, w_t, grad_values, owner, master, moment1, moment2):
    planes = groups // 2
    chips = seqs
    parts = column_parts
    tokens, value_grad = tokens[0], grad_values[0]
    rows, model = tokens.shape
    feats = owner.shape[0]
    slots = master.shape[1]
    width = model // (2 * seqs)
    own_x = lax.axis_index("dp") % 2

    def permute(value, target):
        pairs = []
        for dp in range(groups):
            for seq in range(seqs):
                to = target(dp, seq)
                if to is not None:
                    pairs.append((dp * seqs + seq, to[0] * seqs + to[1]))
        return lax.ppermute(value, ("dp", "seq"), pairs)

    def to_chip(value, k):
        return permute(value, lambda dp, seq: (dp ^ (k & 1), seq ^ (k >> 1 << 1)))

    def to_core(value):
        return permute(value, lambda dp, seq: (dp, seq ^ 1))

    def to_x(value):
        return permute(value, lambda dp, seq: (dp ^ 1, seq))

    def to_plane(value, turn):
        return permute(value, lambda dp, seq: (dp ^ (2 * turn), seq))

    def busy(z, step, even):
        rightward = (z % 2 == 0) == even
        return z < step if rightward else planes - 1 - z < step

    def across(value, step, even):
        def target(dp, seq):
            z = dp // 2
            way = 1 if (z % 2 == 0) == even else -1
            return (dp + 2 * way, seq) if busy(z, step, even) else None

        return permute(value, target)

    tokens_far = to_core(tokens)
    grads = [value_grad] + [to_chip(value_grad, k) for k in range(chips - 1, 0, -1)][::-1]

    w_keep, w_send = halves(w_t, width)
    w_got = to_x(w_send)

    gain_row, owner_row = gain[None, :], owner[None, :]
    sent = norm_blocks(tokens, tokens_far, gain_row, chips, width, parts)
    grads = stack(grads, 2, [sent[0][0], w_keep])
    pieces = [sent[0]] + [[to_chip(p, k) for p in sent[k]] for k in range(1, chips)]
    grads_far = [to_core(grads[-1])]
    grads = grads[:2]
    selected = select_rows(owner_row, groups, slots, (sent[0][0],))

    weights = stack([w_keep, w_got], 1, grads_far[:1])
    turn = planes // 2
    while turn:
        weights = [w for value in weights for w in (value, to_plane(value, turn))]
        turn //= 2
    weights_far = [to_core(w) for w in weights]

    plan = [
        (step, even)
        for step in range(1, planes)
        for even in (True, False)
        if any(busy(z, step, even) for z in range(planes))
    ]
    outs = weight_blocks(
        selected, [*grads, *grads_far], [piece[0] for piece in pieces], planes, plan, weights
    )
    ready = dict(zip(plan, outs))
    got = {even: across(ready[1, even], 1, even) for even in (True, False) if (1, even) in ready}
    held = [{even: (value, chunk) for even, value in got.items()} for chunk in range(2)]

    def advance(step, chunks, after):
        here = [even for even in (True, False) if (step, even) in ready]
        adds = [even for even in here if (not even) in held[0]]
        keys = [(chunk, even) for chunk in chunks for even in adds]
        sums = relay(
            [[(ready[step, even], chunk), held[chunk][not even]] for chunk, even in keys], after
        )
        new = [{}, {}]
        for (chunk, even), value in zip(keys, sums):
            new[chunk][even] = (across(value, step, even), None)
        for even in here:
            if even not in adds:
                whole = across(ready[step, even], step, even)
                for chunk in chunks:
                    new[chunk][even] = (whole, chunk)
        for chunk in chunks:
            held[chunk] = new[chunk]
        return sums

    *far_sums, near_sum = value_parts(pieces, weights, feats, outs[:1])
    sums = [near_sum] + [to_core(f) for f in far_sums]
    back = back_blocks(grads, sums, weights + weights_far, chips, [])
    home = [back[0]] + [to_chip(back[k], k) for k in range(1, chips)]
    advance(2, (1, 0), [])
    for step in range(3, planes):
        advance(step, (1,), [])
        advance(step, (0,), [])
    other = relay([[(outs[-1], 1), *held[1].values()]], home[-1:])
    got = to_x(other[0])
    grad_x, values = grad_x_blocks(tokens, gain_row, back[-1], home)
    mine = [outs[-1][:slots]] + [value for value, _ in held[0].values()]
    total = rows * seqs * groups
    states = (master[0], moment1[0], moment2[0])
    states = adam(owner_row, mine, got, states, total)
    return (values[None], grad_x[None], *(s[None] for s in states))


def solution(mesh):
    placed = (
        P("dp", "seq", None),
        P(),
        P("dp", "seq"),
        P("dp", "seq", None),
        P(),
        P("dp", None, "seq"),
        P("dp", None, "seq"),
        P("dp", None, "seq"),
    )
    return jax.shard_map(
        functools.partial(on_device, mesh.shape["dp"], mesh.shape["seq"]),
        mesh=mesh,
        in_specs=placed,
        out_specs=(
            P("dp", "seq", None),
            P("dp", "seq", None),
            P("dp", None, "seq"),
            P("dp", None, "seq"),
            P("dp", None, "seq"),
        ),
        check_vma=False,
    )
```

```python
import functools

import jax
import jax.numpy as jnp
from jax import lax
from jax.experimental import pallas as pl
from jax.experimental.pallas import tpu as pltpu
from jax.sharding import PartitionSpec as P

beta_one = 0.9
beta_two = 0.95
learn_rate = 0.001
adam_eps = 1e-08
bias_one = 1.0 - 0.9**10
bias_two = 1.0 - 0.95**10
norm_eps = 1e-05
column_parts = 1

bf16 = jnp.bfloat16
f32 = jnp.float32


def cost(flops, moved):
    return pl.CostEstimate(flops=flops, bytes_accessed=moved, transcendentals=0)


def limit(mib):
    return pltpu.CompilerParams(vmem_limit_bytes=mib * 1024 * 1024)


def column_block(k, j, width, part=0, parts=1):
    seq = lax.axis_index("seq") ^ (k >> 1 << 1) ^ j
    x = (lax.axis_index("dp") % 2) ^ (k & 1)
    return pl.ds(pl.multiple_of(((seq * 2 + x) * parts + part) * width, width), width)


def norm_kernel(parts, tok_ref, far_ref, gain_ref, after_ref, *refs):
    out_refs = [refs[i : i + parts] for i in range(0, len(refs), parts)]
    chips = len(out_refs)
    width = out_refs[0][0].shape[-1]
    for i, ref in enumerate((tok_ref, far_ref)):
        tok = ref[...].astype(f32)
        inv_rms = lax.rsqrt(jnp.mean(tok * tok, axis=-1, keepdims=True) + norm_eps)
        for k in (*range(1, chips), 0):
            for part in range(parts):
                cols = column_block(k, 0, width, part, parts)
                scaled = ref[:, cols].astype(f32) * inv_rms
                out_refs[k][part][i] = (scaled * gain_ref[:, cols]).astype(bf16)


def norm_blocks(tokens, far, gain, chips, width, parts, after):
    rows, model = tokens.shape
    step = min(rows, 32)
    outs = pl.pallas_call(
        functools.partial(norm_kernel, parts),
        grid=(rows // step,),
        in_specs=[
            pl.BlockSpec((step, model), lambda i: (i, 0)),
            pl.BlockSpec((step, model), lambda i: (i, 0)),
            pl.BlockSpec((1, model), lambda i: (0, 0)),
            pl.BlockSpec(memory_space=pl.ANY),
        ],
        out_specs=[pl.BlockSpec((2, step, width // parts), lambda i: (0, i, 0))] * (chips * parts),
        out_shape=[jax.ShapeDtypeStruct((2, rows, width // parts), bf16)] * (chips * parts),
        compiler_params=limit(24),
        cost_estimate=cost(8 * rows * model, 6 * rows * model),
        name="norm_blocks",
    )(
        pltpu.with_memory_space_constraint(tokens, pltpu.HBM),
        far,
        pltpu.with_memory_space_constraint(gain, pltpu.HBM),
        after,
    )
    return [outs[i : i + parts] for i in range(0, len(outs), parts)]


def halves_kernel(w_ref, keep_ref, send_ref):
    width = keep_ref.shape[1]
    own_x = lax.axis_index("dp") % 2
    keep_ref[...] = w_ref[:, pl.ds(pl.multiple_of(own_x * width, width), width)]
    send_ref[...] = w_ref[:, pl.ds(pl.multiple_of((1 - own_x) * width, width), width)]


def halves(w_t, width):
    return pl.pallas_call(
        halves_kernel,
        out_shape=[jax.ShapeDtypeStruct((w_t.shape[0], width), bf16)] * 2,
        compiler_params=limit(16),
        name="halves",
    )(pltpu.with_memory_space_constraint(w_t, pltpu.HBM))


def stack_kernel(count, *refs):
    out_refs = refs[-(len(refs) - count) :]
    rows = refs[0].shape[0]
    if len(out_refs) == 3:
        stack_kernel(count, *refs[:count], out_refs[2])
        out_refs = out_refs[:2]
    each = out_refs[0].shape[0] // rows
    for i, ref in enumerate(refs[:count]):
        out_refs[i // each][i % each * rows : (i % each + 1) * rows, :] = ref[...]


def stack(pieces, outs, after):
    count = len(pieces)
    rows, width = pieces[0].shape
    return pl.pallas_call(
        lambda *refs: stack_kernel(count, *refs[:count], *refs[count + len(after) :]),
        in_specs=[pl.BlockSpec(memory_space=pltpu.VMEM)] * count
        + [pl.BlockSpec(memory_space=pl.ANY)] * len(after),
        out_shape=[jax.ShapeDtypeStruct((count // outs * rows, width), bf16)] * outs
        + [jax.ShapeDtypeStruct((count * rows, width), bf16)] * (outs > 1),
        compiler_params=limit(16),
        name="stack",
    )(*pieces, *after)


def select_kernel(groups, slots, owner_ref, *refs):
    out_ref = refs[-1]
    feats = owner_ref.shape[1]
    owner = owner_ref[...]
    lower = lax.broadcasted_iota(jnp.int32, (feats, feats), 0) < lax.broadcasted_iota(
        jnp.int32, (feats, feats), 1
    )
    owned = (lax.broadcasted_iota(jnp.int32, (groups, feats), 0) == owner).astype(f32)
    before = jnp.dot(
        owned.astype(bf16), lower.astype(f32).astype(bf16), preferred_element_type=f32
    )
    place = jnp.sum(owned * before, axis=0, keepdims=True).astype(jnp.int32)
    own_x = lax.axis_index("dp") % 2
    slot = (owner ^ own_x) * slots + place
    step = 256
    for at in range(0, out_ref.shape[0], step):
        index = at + lax.broadcasted_iota(jnp.int32, (step, feats), 0)
        out_ref[at : at + step, :] = (index == slot).astype(f32).astype(bf16)


def select_rows(owner, groups, slots, after):
    feats = owner.shape[1]
    return pl.pallas_call(
        functools.partial(select_kernel, groups, slots),
        in_specs=[pl.BlockSpec(memory_space=pltpu.VMEM)]
        + [pl.BlockSpec(memory_space=pl.ANY)] * len(after),
        out_shape=jax.ShapeDtypeStruct((groups * slots, feats), bf16),
        compiler_params=limit(24),
        cost_estimate=cost(4 * groups * slots * feats, 2 * groups * slots * feats),
        name="select_rows",
    )(owner, *after)


def chip_term(k, chips, grad_refs, piece_ref, joined, at):
    _, rows, width = piece_ref.shape
    near = grad_refs[k * 2 // chips]
    first = k % (chips // 2) * rows
    joined[:rows, :] = near[first : first + rows, at : at + 256]
    joined[rows:, :] = grad_refs[2][k * rows : (k + 1) * rows, at : at + 256]
    return lax.dot_general(
        joined[...],
        piece_ref[...].reshape(2 * rows, width),
        (((0,), (0,)), ((), ())),
        preferred_element_type=f32,
    )


def early_kernel(chips, *refs):
    grad_refs, piece_refs, (base_ref, joined) = refs[:3], refs[3:-2], refs[-2:]
    for at in range(0, base_ref.shape[0], 256):
        total = None
        for k, piece_ref in enumerate(piece_refs):
            term = chip_term(k, chips, grad_refs, piece_ref, joined, at)
            total = term if total is None else total + term
        base_ref[at : at + 256, :] = total


def early_weight(grads, pieces):
    _, rows, width = pieces[0].shape
    feats = grads[0].shape[1]
    return pl.pallas_call(
        functools.partial(early_kernel, len(pieces) + 1),
        out_shape=jax.ShapeDtypeStruct((feats, width), f32),
        scratch_shapes=[pltpu.VMEM((2 * rows, 256), bf16)],
        compiler_params=limit(24),
        name="early_weight",
    )(*grads, *pieces)


def weight_kernel(planes, chips, plan, sel_ref, base_ref, *refs):
    grad_refs, piece_ref = refs[:3], refs[3]
    out_refs, (base, joined) = refs[-len(plan) - 3 : -2], refs[-2:]
    block = sel_ref.shape[0] // planes
    z = lax.axis_index("dp") // 2
    for at in range(0, base.shape[0], 256):
        term = chip_term(chips - 1, chips, grad_refs, piece_ref, joined, at)
        base[at : at + 256, :] = (base_ref[at : at + 256, :] + term).astype(bf16)

    def chosen(plane):
        at = pl.multiple_of(plane * block, block)
        return jnp.dot(sel_ref[pl.ds(at, block), :], base[...], preferred_element_type=f32)

    for (step, even), out_ref in zip(plan, out_refs):
        ahead = planes - step
        plane = jnp.where((z % 2 == 0) == even, z + ahead, z - ahead)

        @pl.when((plane >= 0) & (plane < planes))
        def _():
            out_ref[...] = chosen(plane).astype(bf16)

    out_refs[-1][...] = chosen(z).astype(bf16)


def weight_blocks(selected, early, grads, piece, chips, planes, plan, after):
    slots_all, feats = selected.shape
    _, rows, width = piece.shape
    block = slots_all // planes
    return pl.pallas_call(
        functools.partial(weight_kernel, planes, chips, plan),
        in_specs=[pl.BlockSpec(memory_space=pltpu.VMEM)] * 6
        + [pl.BlockSpec(memory_space=pl.ANY)] * len(after),
        out_shape=[jax.ShapeDtypeStruct((block, width), bf16)] * (len(plan) + 1),
        scratch_shapes=[pltpu.VMEM((feats, width), bf16), pltpu.VMEM((2 * rows, 256), bf16)],
        compiler_params=limit(24),
        name="weight_blocks",
    )(selected, early, *grads, piece, *after)


def gather_weight(piece_refs, held):
    dp = lax.axis_index("dp")
    own_x, own_z = dp % 2, dp // 2
    for turn, ref in enumerate(piece_refs):
        share = ref.shape[0] // 2
        for i in range(2):
            at = pl.multiple_of(((own_z ^ turn) * 2 + (own_x ^ i)) * share, share)
            held[pl.ds(at, share), :] = ref[i * share : (i + 1) * share, :]


def value_kernel(planes, chips, parts, *refs):
    piece_refs, refs = refs[: chips * parts], refs[chips * parts :]
    far_refs, out_ref, held = refs[-4:-2], refs[-2], refs[-1]
    rows = out_ref.shape[0] // chips
    half = chips // 2
    part_width = held.shape[1] // parts
    gather_weight(refs[:planes], held)
    for k in range(chips):
        total = None
        for part in range(parts):
            piece = piece_refs[k * parts + part][...]
            term = lax.dot_general(
                piece.reshape(2 * rows, part_width),
                held[:, part * part_width : (part + 1) * part_width],
                (((1,), (1,)), ((), ())),
                preferred_element_type=f32,
            )
            total = term if total is None else total + term
        out_ref[k * rows : (k + 1) * rows, :] = total[:rows]
        at = k % half * rows
        far_refs[k // half][at : at + rows, :] = total[rows:].astype(bf16)


def value_parts(pieces, weights, feats, after):
    chips, parts = len(pieces), len(pieces[0])
    rows = pieces[0][0].shape[1]
    width = weights[0].shape[-1]
    return pl.pallas_call(
        functools.partial(value_kernel, len(weights), chips, parts),
        in_specs=[pl.BlockSpec(memory_space=pltpu.VMEM)] * (chips * parts + len(weights))
        + [pl.BlockSpec(memory_space=pl.ANY)] * len(after),
        out_shape=[jax.ShapeDtypeStruct((chips // 2 * rows, feats), bf16)] * 2
        + [jax.ShapeDtypeStruct((chips * rows, feats), f32)],
        scratch_shapes=[pltpu.VMEM((feats, width), bf16)],
        compiler_params=limit(40),
        name="value_parts",
    )(*[p for piece in pieces for p in piece], *weights, *after)


def back_kernel(planes, chips, grads_a_ref, grads_b_ref, value_ref, got_a_ref, got_b_ref, *refs):
    weight_refs, refs = refs[: 2 * planes], refs[2 * planes :]
    out_refs, own_ref, held = refs[-chips - 2 : -2], refs[-2], refs[-1]
    rows, feats = own_ref.shape
    width = held.shape[1]
    half = chips // 2
    for k in range(chips):
        got_ref = got_b_ref if k // half else got_a_ref
        total = value_ref[k * rows : (k + 1) * rows, :]
        total += got_ref[k % half * rows : (k % half + 1) * rows, :].astype(f32)
        if k == 0:
            own_ref[...] = total
        else:
            out_refs[k][:, 2 * width :] = total.astype(bf16)
    for j in range(2):
        gather_weight(weight_refs[j * planes : (j + 1) * planes], held)
        for i, grads_ref in enumerate((grads_a_ref, grads_b_ref)):
            block = jnp.dot(grads_ref[...], held[...], preferred_element_type=f32).astype(bf16)
            for k in range(half):
                out_refs[i * half + k][:, j * width : (j + 1) * width] = block[
                    k * rows : (k + 1) * rows, :
                ]


def back_blocks(grads, sums, weights, chips, after):
    rows, feats = 2 * grads[0].shape[0] // chips, grads[0].shape[1]
    width = weights[0].shape[-1]
    return pl.pallas_call(
        functools.partial(back_kernel, len(weights) // 2, chips),
        in_specs=[pl.BlockSpec(memory_space=pltpu.VMEM)] * (len(grads) + len(sums) + len(weights))
        + [pl.BlockSpec(memory_space=pl.ANY)] * len(after),
        out_shape=[
            jax.ShapeDtypeStruct((rows, 2 * width + (feats if k else 0)), bf16)
            for k in range(chips)
        ]
        + [jax.ShapeDtypeStruct((rows, feats), f32)],
        scratch_shapes=[pltpu.VMEM((feats, width), bf16)],
        compiler_params=limit(40),
        name="back_blocks",
    )(*grads, *sums, *weights, *after)


def grad_x_kernel(tok_ref, gain_ref, part_ref, *refs):
    grad_refs, (out_ref, values_ref) = refs[:-2], refs[-2:]
    model = tok_ref.shape[-1]
    width = grad_refs[0].shape[-1] // 2
    values = part_ref[...]
    for grad_ref in grad_refs[1:]:
        values += grad_ref[:, 2 * width :].astype(f32)
    values_ref[...] = values.astype(bf16)
    tok = tok_ref[...].astype(f32)
    inv_rms = lax.rsqrt(jnp.mean(tok * tok, axis=-1, keepdims=True) + norm_eps)
    total = jnp.zeros((tok.shape[0], 1), f32)
    for k, grad_ref in enumerate(grad_refs):
        for j in range(2):
            cols = column_block(k, j, width)
            weighted = gain_ref[:, cols] * grad_ref[:, j * width : (j + 1) * width].astype(f32)
            scaled = tok_ref[:, cols].astype(f32) * inv_rms
            total += jnp.sum(weighted * scaled, axis=-1, keepdims=True)
    mean = total / model
    for k, grad_ref in enumerate(grad_refs):
        for j in range(2):
            cols = column_block(k, j, width)
            weighted = gain_ref[:, cols] * grad_ref[:, j * width : (j + 1) * width].astype(f32)
            scaled = tok_ref[:, cols].astype(f32) * inv_rms
            out_ref[:, cols] = (inv_rms * (weighted - scaled * mean)).astype(bf16)


def grad_x_blocks(tokens, gain, part, grads):
    rows, model = tokens.shape
    feats = part.shape[-1]
    step = min(rows, 32)
    return pl.pallas_call(
        grad_x_kernel,
        grid=(rows // step,),
        in_specs=[
            pl.BlockSpec((step, model), lambda i: (i, 0)),
            pl.BlockSpec((1, model), lambda i: (0, 0)),
            pl.BlockSpec((step, feats), lambda i: (i, 0)),
        ]
        + [pl.BlockSpec((step, g.shape[1]), lambda i: (i, 0)) for g in grads],
        out_specs=[
            pl.BlockSpec((step, model), lambda i: (i, 0)),
            pl.BlockSpec((step, feats), lambda i: (i, 0)),
        ],
        out_shape=[
            jax.ShapeDtypeStruct((rows, model), bf16),
            jax.ShapeDtypeStruct((rows, feats), bf16),
        ],
        compiler_params=limit(24),
        cost_estimate=cost(16 * rows * model, 6 * rows * model),
        name="grad_x_blocks",
    )(tokens, gain, part, *grads)


def add_kernel(halves_of, *refs):
    outs = refs[-len(halves_of) :]
    at = 0
    for half_of, out_ref in zip(halves_of, outs):
        rows = out_ref.shape[0]
        total = None
        for half in half_of:
            first = (half or 0) * rows
            term = refs[at][first : first + rows, :].astype(f32)
            total = term if total is None else total + term
            at += 1
        out_ref[...] = total.astype(out_ref.dtype)


def relay(sums, after):
    arrays = [array for group in sums for array, _ in group]
    rows, width = sums[0][0][0].shape
    shape = (rows if sums[0][0][1] is None else rows // 2, width)
    return pl.pallas_call(
        functools.partial(add_kernel, [[half for _, half in group] for group in sums]),
        in_specs=[pl.BlockSpec(memory_space=pltpu.VMEM)] * len(arrays)
        + [pl.BlockSpec(memory_space=pl.ANY)] * len(after),
        out_shape=[jax.ShapeDtypeStruct(shape, bf16)] * len(sums),
        compiler_params=limit(16),
        name="relay",
    )(*arrays, *after)


def adam_kernel(token_total, count, owner_ref, *refs):
    part_refs, got_ref, refs = refs[:count], refs[count], refs[count + 1 :]
    master_ref, moment1_ref, moment2_ref = refs[:3]
    out_refs = refs[3:]
    step, width = got_ref.shape
    dp = lax.axis_index("dp")
    owned = (owner_ref[...] == dp).astype(f32)
    count = jnp.sum(owned, axis=1, keepdims=True)
    index = pl.program_id(0) * step + lax.broadcasted_iota(jnp.int32, (step, 1), 0)
    occupied = (index.astype(f32) < count).astype(f32)
    for i, refs in enumerate((part_refs, (got_ref,))):
        total = refs[0][...].astype(f32)
        for ref in refs[1:]:
            total += ref[...].astype(f32)
        cols = pl.ds(pl.multiple_of(((dp % 2) ^ i) * width, width), width)
        slot_grad = total / token_total
        new_moment1 = (beta_one * moment1_ref[:, cols] + (1.0 - beta_one) * slot_grad) * occupied
        new_moment2 = (
            beta_two * moment2_ref[:, cols] + (1.0 - beta_two) * slot_grad * slot_grad
        ) * occupied
        step_dir = new_moment1 / bias_one / (jnp.sqrt(new_moment2 / bias_two) + adam_eps)
        out_refs[0][:, cols] = (master_ref[:, cols] - learn_rate * step_dir) * occupied
        out_refs[1][:, cols] = new_moment1
        out_refs[2][:, cols] = new_moment2


def adam(owner, parts, got, states, token_total):
    slots, cols = states[0].shape
    width = got.shape[-1]
    step = min(slots, 32)
    return pl.pallas_call(
        functools.partial(adam_kernel, token_total, len(parts)),
        grid=(slots // step,),
        in_specs=[pl.BlockSpec(owner.shape, lambda i: (0, 0))]
        + [pl.BlockSpec((step, width), lambda i: (i, 0))] * (len(parts) + 1)
        + [pl.BlockSpec((step, cols), lambda i: (i, 0))] * 3,
        out_specs=[pl.BlockSpec((step, cols), lambda i: (i, 0))] * 3,
        out_shape=[jax.ShapeDtypeStruct((slots, cols), f32)] * 3,
        compiler_params=limit(24),
        cost_estimate=cost(20 * slots * cols, 30 * slots * cols),
        name="adam",
    )(owner, *parts, got, *states)


def on_device(groups, seqs, tokens, gain, w_t, grad_values, owner, master, moment1, moment2):
    planes = groups // 2
    chips = seqs
    parts = column_parts
    tokens, value_grad = tokens[0], grad_values[0]
    rows, model = tokens.shape
    feats = owner.shape[0]
    slots = master.shape[1]
    width = model // (2 * seqs)
    own_x = lax.axis_index("dp") % 2

    def permute(value, target):
        pairs = []
        for dp in range(groups):
            for seq in range(seqs):
                to = target(dp, seq)
                if to is not None:
                    pairs.append((dp * seqs + seq, to[0] * seqs + to[1]))
        return lax.ppermute(value, ("dp", "seq"), pairs)

    def to_chip(value, k):
        return permute(value, lambda dp, seq: (dp ^ (k & 1), seq ^ (k >> 1 << 1)))

    def to_core(value):
        return permute(value, lambda dp, seq: (dp, seq ^ 1))

    def to_x(value):
        return permute(value, lambda dp, seq: (dp ^ 1, seq))

    def to_plane(value, turn):
        return permute(value, lambda dp, seq: (dp ^ (2 * turn), seq))

    def busy(z, step, even):
        rightward = (z % 2 == 0) == even
        return z < step if rightward else planes - 1 - z < step

    def across(value, step, even):
        def target(dp, seq):
            z = dp // 2
            way = 1 if (z % 2 == 0) == even else -1
            return (dp + 2 * way, seq) if busy(z, step, even) else None

        return permute(value, target)

    tokens_far = to_core(tokens)
    grads = [value_grad] + [to_chip(value_grad, k) for k in range(chips - 1, 0, -1)][::-1]

    w_keep, w_send = halves(w_t, width)
    w_got = to_x(w_send)

    gain_row, owner_row = gain[None, :], owner[None, :]
    sent = norm_blocks(tokens, tokens_far, gain_row, chips, width, parts, w_keep)
    grads = stack(grads, 2, [sent[0][0], w_keep])
    pieces = [sent[0]] + [[to_chip(p, k) for p in sent[k]] for k in range(1, chips)]
    grads_far = [to_core(grads[-1])]
    grads = grads[:2]
    selected = select_rows(owner_row, groups, slots, (sent[0][0],))

    weights = stack([w_keep, w_got], 1, grads_far[:1])
    turn = planes // 2
    while turn:
        weights = [w for value in weights for w in (value, to_plane(value, turn))]
        turn //= 2
    weights_far = [to_core(w) for w in weights]

    plan = [
        (step, even)
        for step in range(1, planes)
        for even in (True, False)
        if any(busy(z, step, even) for z in range(planes))
    ]
    every = [*grads, *grads_far]
    early = early_weight(every, [piece[0] for piece in pieces[:-1]])
    outs = weight_blocks(selected, early, every, pieces[-1][0], chips, planes, plan, weights)
    ready = dict(zip(plan, outs))
    got = {even: across(ready[1, even], 1, even) for even in (True, False) if (1, even) in ready}
    held = [{even: (value, chunk) for even, value in got.items()} for chunk in range(2)]

    def advance(step, chunks, after):
        here = [even for even in (True, False) if (step, even) in ready]
        adds = [even for even in here if (not even) in held[0]]
        keys = [(chunk, even) for chunk in chunks for even in adds]
        sums = relay(
            [[(ready[step, even], chunk), held[chunk][not even]] for chunk, even in keys], after
        )
        new = [{}, {}]
        for (chunk, even), value in zip(keys, sums):
            new[chunk][even] = (across(value, step, even), None)
        for even in here:
            if even not in adds:
                whole = across(ready[step, even], step, even)
                for chunk in chunks:
                    new[chunk][even] = (whole, chunk)
        for chunk in chunks:
            held[chunk] = new[chunk]
        return sums

    *far_sums, near_sum = value_parts(pieces, weights, feats, outs[:1])
    sums = [near_sum] + [to_core(f) for f in far_sums]
    back = back_blocks(grads, sums, weights + weights_far, chips, [])
    home = [back[0]] + [to_chip(back[k], k) for k in range(1, chips)]
    advance(2, (1, 0), [])
    for step in range(3, planes):
        advance(step, (1,), [])
        advance(step, (0,), [])
    other = relay([[(outs[-1], 1), *held[1].values()]], home[-1:])
    got = to_x(other[0])
    grad_x, values = grad_x_blocks(tokens, gain_row, back[-1], home)
    mine = [outs[-1][:slots]] + [value for value, _ in held[0].values()]
    total = rows * seqs * groups
    states = (master[0], moment1[0], moment2[0])
    states = adam(owner_row, mine, got, states, total)
    return (values[None], grad_x[None], *(s[None] for s in states))


def solution(mesh):
    placed = (
        P("dp", "seq", None),
        P(),
        P("dp", "seq"),
        P("dp", "seq", None),
        P(),
        P("dp", None, "seq"),
        P("dp", None, "seq"),
        P("dp", None, "seq"),
    )
    return jax.shard_map(
        functools.partial(on_device, mesh.shape["dp"], mesh.shape["seq"]),
        mesh=mesh,
        in_specs=placed,
        out_specs=(
            P("dp", "seq", None),
            P("dp", "seq", None),
            P("dp", None, "seq"),
            P("dp", None, "seq"),
            P("dp", None, "seq"),
        ),
        check_vma=False,
    )
```

```python
import functools

import jax
import jax.numpy as jnp
from jax import lax
from jax.experimental import pallas as pl
from jax.experimental.pallas import tpu as pltpu
from jax.sharding import PartitionSpec as P

beta_one = 0.9
beta_two = 0.95
learn_rate = 0.001
adam_eps = 1e-08
bias_one = 1.0 - 0.9**10
bias_two = 1.0 - 0.95**10
norm_eps = 1e-05
column_parts = 1

bf16 = jnp.bfloat16
f32 = jnp.float32


def cost(flops, moved):
    return pl.CostEstimate(flops=flops, bytes_accessed=moved, transcendentals=0)


def limit(mib):
    return pltpu.CompilerParams(vmem_limit_bytes=mib * 1024 * 1024)


def column_block(k, j, width, part=0, parts=1):
    seq = lax.axis_index("seq") ^ (k >> 1 << 1) ^ j
    x = (lax.axis_index("dp") % 2) ^ (k & 1)
    return pl.ds(pl.multiple_of(((seq * 2 + x) * parts + part) * width, width), width)


def norm_kernel(parts, tok_ref, far_ref, gain_ref, after_ref, *refs):
    out_refs = [refs[i : i + parts] for i in range(0, len(refs), parts)]
    chips = len(out_refs)
    width = out_refs[0][0].shape[-1]
    for i, ref in enumerate((tok_ref, far_ref)):
        tok = ref[...].astype(f32)
        inv_rms = lax.rsqrt(jnp.mean(tok * tok, axis=-1, keepdims=True) + norm_eps)
        for k in (*range(1, chips), 0):
            for part in range(parts):
                cols = column_block(k, 0, width, part, parts)
                scaled = ref[:, cols].astype(f32) * inv_rms
                out_refs[k][part][i] = (scaled * gain_ref[:, cols]).astype(bf16)


def norm_blocks(tokens, far, gain, chips, width, parts, after):
    rows, model = tokens.shape
    step = min(rows, 32)
    outs = pl.pallas_call(
        functools.partial(norm_kernel, parts),
        grid=(rows // step,),
        in_specs=[
            pl.BlockSpec((step, model), lambda i: (i, 0)),
            pl.BlockSpec((step, model), lambda i: (i, 0)),
            pl.BlockSpec((1, model), lambda i: (0, 0)),
            pl.BlockSpec(memory_space=pl.ANY),
        ],
        out_specs=[pl.BlockSpec((2, step, width // parts), lambda i: (0, i, 0))] * (chips * parts),
        out_shape=[jax.ShapeDtypeStruct((2, rows, width // parts), bf16)] * (chips * parts),
        compiler_params=limit(24),
        cost_estimate=cost(8 * rows * model, 6 * rows * model),
        name="norm_blocks",
    )(
        pltpu.with_memory_space_constraint(tokens, pltpu.HBM),
        far,
        pltpu.with_memory_space_constraint(gain, pltpu.HBM),
        after,
    )
    return [outs[i : i + parts] for i in range(0, len(outs), parts)]


def halves_kernel(w_ref, keep_ref, send_ref):
    width = keep_ref.shape[1]
    own_x = lax.axis_index("dp") % 2
    keep_ref[...] = w_ref[:, pl.ds(pl.multiple_of(own_x * width, width), width)]
    send_ref[...] = w_ref[:, pl.ds(pl.multiple_of((1 - own_x) * width, width), width)]


def halves(w_t, width):
    return pl.pallas_call(
        halves_kernel,
        out_shape=[jax.ShapeDtypeStruct((w_t.shape[0], width), bf16)] * 2,
        compiler_params=limit(16),
        name="halves",
    )(pltpu.with_memory_space_constraint(w_t, pltpu.HBM))


def stack_kernel(count, *refs):
    out_refs = refs[-(len(refs) - count) :]
    rows = refs[0].shape[0]
    if len(out_refs) == 3:
        stack_kernel(count, *refs[:count], out_refs[2])
        out_refs = out_refs[:2]
    each = out_refs[0].shape[0] // rows
    for i, ref in enumerate(refs[:count]):
        out_refs[i // each][i % each * rows : (i % each + 1) * rows, :] = ref[...]


def stack(pieces, outs, after):
    count = len(pieces)
    rows, width = pieces[0].shape
    return pl.pallas_call(
        lambda *refs: stack_kernel(count, *refs[:count], *refs[count + len(after) :]),
        in_specs=[pl.BlockSpec(memory_space=pltpu.VMEM)] * count
        + [pl.BlockSpec(memory_space=pl.ANY)] * len(after),
        out_shape=[jax.ShapeDtypeStruct((count // outs * rows, width), bf16)] * outs
        + [jax.ShapeDtypeStruct((count * rows, width), bf16)] * (outs > 1),
        compiler_params=limit(16),
        name="stack",
    )(*pieces, *after)


def select_kernel(groups, slots, owner_ref, *refs):
    out_ref = refs[-1]
    feats = owner_ref.shape[1]
    owner = owner_ref[...]
    lower = lax.broadcasted_iota(jnp.int32, (feats, feats), 0) < lax.broadcasted_iota(
        jnp.int32, (feats, feats), 1
    )
    owned = (lax.broadcasted_iota(jnp.int32, (groups, feats), 0) == owner).astype(f32)
    before = jnp.dot(
        owned.astype(bf16), lower.astype(f32).astype(bf16), preferred_element_type=f32
    )
    place = jnp.sum(owned * before, axis=0, keepdims=True).astype(jnp.int32)
    own_x = lax.axis_index("dp") % 2
    slot = (owner ^ own_x) * slots + place
    step = 256
    for at in range(0, out_ref.shape[0], step):
        index = at + lax.broadcasted_iota(jnp.int32, (step, feats), 0)
        out_ref[at : at + step, :] = (index == slot).astype(f32).astype(bf16)


def select_rows(owner, groups, slots, after):
    feats = owner.shape[1]
    return pl.pallas_call(
        functools.partial(select_kernel, groups, slots),
        in_specs=[pl.BlockSpec(memory_space=pltpu.VMEM)]
        + [pl.BlockSpec(memory_space=pl.ANY)] * len(after),
        out_shape=jax.ShapeDtypeStruct((groups * slots, feats), bf16),
        compiler_params=limit(24),
        cost_estimate=cost(4 * groups * slots * feats, 2 * groups * slots * feats),
        name="select_rows",
    )(owner, *after)


def chip_term(k, chips, grad_refs, piece_ref, joined, at):
    _, rows, width = piece_ref.shape
    near = grad_refs[k * 2 // chips]
    first = k % (chips // 2) * rows
    joined[:rows, :] = near[first : first + rows, at : at + 256]
    joined[rows:, :] = grad_refs[2][k * rows : (k + 1) * rows, at : at + 256]
    return lax.dot_general(
        joined[...],
        piece_ref[...].reshape(2 * rows, width),
        (((0,), (0,)), ((), ())),
        preferred_element_type=f32,
    )


def early_kernel(chips, *refs):
    grad_refs, piece_refs, (base_ref, joined) = refs[:3], refs[3:-2], refs[-2:]
    for at in range(0, base_ref.shape[0], 256):
        total = None
        for k, piece_ref in enumerate(piece_refs):
            term = chip_term(k, chips, grad_refs, piece_ref, joined, at)
            total = term if total is None else total + term
        base_ref[at : at + 256, :] = total


def early_weight(grads, pieces):
    _, rows, width = pieces[0].shape
    feats = grads[0].shape[1]
    return pl.pallas_call(
        functools.partial(early_kernel, len(pieces) + 1),
        out_shape=jax.ShapeDtypeStruct((feats, width), f32),
        scratch_shapes=[pltpu.VMEM((2 * rows, 256), bf16)],
        compiler_params=limit(24),
        name="early_weight",
    )(*grads, *pieces)


def slot_blocks(planes, plan, sel_ref, base_ref, out_refs):
    block = sel_ref.shape[0] // planes
    z = lax.axis_index("dp") // 2

    def chosen(plane):
        at = pl.multiple_of(plane * block, block)
        rows = jnp.dot(sel_ref[pl.ds(at, block), :], base_ref[...], preferred_element_type=f32)
        return rows.astype(bf16)

    for (step, even), out_ref in zip(plan, out_refs):
        ahead = planes - step
        plane = jnp.where((z % 2 == 0) == even, z + ahead, z - ahead)

        @pl.when((plane >= 0) & (plane < planes))
        def _():
            out_ref[...] = chosen(plane)

    if len(out_refs) > len(plan):
        out_refs[-1][...] = chosen(z)


def weight_kernel(planes, chips, plan, sel_ref, early_ref, *refs):
    grad_refs, piece_ref = refs[:3], refs[3]
    base_ref, out_refs, joined = refs[-len(plan) - 2], refs[-len(plan) - 1 : -1], refs[-1]
    for at in range(0, base_ref.shape[0], 256):
        term = chip_term(chips - 1, chips, grad_refs, piece_ref, joined, at)
        base_ref[at : at + 256, :] = (early_ref[at : at + 256, :] + term).astype(bf16)
    slot_blocks(planes, plan, sel_ref, base_ref, out_refs)


def weight_blocks(selected, early, grads, piece, chips, planes, plan, after):
    slots_all, feats = selected.shape
    _, rows, width = piece.shape
    block = slots_all // planes
    return pl.pallas_call(
        functools.partial(weight_kernel, planes, chips, plan),
        in_specs=[pl.BlockSpec(memory_space=pltpu.VMEM)] * 6
        + [pl.BlockSpec(memory_space=pl.ANY)] * len(after),
        out_shape=[jax.ShapeDtypeStruct((feats, width), bf16)]
        + [jax.ShapeDtypeStruct((block, width), bf16)] * len(plan),
        scratch_shapes=[pltpu.VMEM((2 * rows, 256), bf16)],
        compiler_params=limit(24),
        name="weight_blocks",
    )(selected, early, *grads, piece, *after)


def later_kernel(planes, plan, sel_ref, base_ref, *refs):
    slot_blocks(planes, plan, sel_ref, base_ref, refs[-len(plan) - 1 :])


def later_blocks(selected, base, planes, plan, after):
    block, width = selected.shape[0] // planes, base.shape[1]
    return pl.pallas_call(
        functools.partial(later_kernel, planes, plan),
        in_specs=[pl.BlockSpec(memory_space=pltpu.VMEM)] * 2
        + [pl.BlockSpec(memory_space=pl.ANY)] * len(after),
        out_shape=[jax.ShapeDtypeStruct((block, width), bf16)] * (len(plan) + 1),
        compiler_params=limit(24),
        name="later_blocks",
    )(selected, base, *after)


def gather_weight(piece_refs, held):
    dp = lax.axis_index("dp")
    own_x, own_z = dp % 2, dp // 2
    for turn, ref in enumerate(piece_refs):
        share = ref.shape[0] // 2
        for i in range(2):
            at = pl.multiple_of(((own_z ^ turn) * 2 + (own_x ^ i)) * share, share)
            held[pl.ds(at, share), :] = ref[i * share : (i + 1) * share, :]


def value_kernel(planes, chips, parts, *refs):
    piece_refs, refs = refs[: chips * parts], refs[chips * parts :]
    far_refs, out_ref, held = refs[-4:-2], refs[-2], refs[-1]
    rows = out_ref.shape[0] // chips
    half = chips // 2
    part_width = held.shape[1] // parts
    gather_weight(refs[:planes], held)
    for k in range(chips):
        total = None
        for part in range(parts):
            piece = piece_refs[k * parts + part][...]
            term = lax.dot_general(
                piece.reshape(2 * rows, part_width),
                held[:, part * part_width : (part + 1) * part_width],
                (((1,), (1,)), ((), ())),
                preferred_element_type=f32,
            )
            total = term if total is None else total + term
        out_ref[k * rows : (k + 1) * rows, :] = total[:rows]
        at = k % half * rows
        far_refs[k // half][at : at + rows, :] = total[rows:].astype(bf16)


def value_parts(pieces, weights, feats, after):
    chips, parts = len(pieces), len(pieces[0])
    rows = pieces[0][0].shape[1]
    width = weights[0].shape[-1]
    return pl.pallas_call(
        functools.partial(value_kernel, len(weights), chips, parts),
        in_specs=[pl.BlockSpec(memory_space=pltpu.VMEM)] * (chips * parts + len(weights))
        + [pl.BlockSpec(memory_space=pl.ANY)] * len(after),
        out_shape=[jax.ShapeDtypeStruct((chips // 2 * rows, feats), bf16)] * 2
        + [jax.ShapeDtypeStruct((chips * rows, feats), f32)],
        scratch_shapes=[pltpu.VMEM((feats, width), bf16)],
        compiler_params=limit(40),
        name="value_parts",
    )(*[p for piece in pieces for p in piece], *weights, *after)


def back_kernel(planes, chips, grads_a_ref, grads_b_ref, value_ref, got_a_ref, got_b_ref, *refs):
    weight_refs, refs = refs[: 2 * planes], refs[2 * planes :]
    out_refs, own_ref, held = refs[-chips - 2 : -2], refs[-2], refs[-1]
    rows, feats = own_ref.shape
    width = held.shape[1]
    half = chips // 2
    for k in range(chips):
        got_ref = got_b_ref if k // half else got_a_ref
        total = value_ref[k * rows : (k + 1) * rows, :]
        total += got_ref[k % half * rows : (k % half + 1) * rows, :].astype(f32)
        if k == 0:
            own_ref[...] = total
        else:
            out_refs[k][:, 2 * width :] = total.astype(bf16)
    for j in range(2):
        gather_weight(weight_refs[j * planes : (j + 1) * planes], held)
        for i, grads_ref in enumerate((grads_a_ref, grads_b_ref)):
            block = jnp.dot(grads_ref[...], held[...], preferred_element_type=f32).astype(bf16)
            for k in range(half):
                out_refs[i * half + k][:, j * width : (j + 1) * width] = block[
                    k * rows : (k + 1) * rows, :
                ]


def back_blocks(grads, sums, weights, chips, after):
    rows, feats = 2 * grads[0].shape[0] // chips, grads[0].shape[1]
    width = weights[0].shape[-1]
    return pl.pallas_call(
        functools.partial(back_kernel, len(weights) // 2, chips),
        in_specs=[pl.BlockSpec(memory_space=pltpu.VMEM)] * (len(grads) + len(sums) + len(weights))
        + [pl.BlockSpec(memory_space=pl.ANY)] * len(after),
        out_shape=[
            jax.ShapeDtypeStruct((rows, 2 * width + (feats if k else 0)), bf16)
            for k in range(chips)
        ]
        + [jax.ShapeDtypeStruct((rows, feats), f32)],
        scratch_shapes=[pltpu.VMEM((feats, width), bf16)],
        compiler_params=limit(40),
        name="back_blocks",
    )(*grads, *sums, *weights, *after)


def grad_x_kernel(tok_ref, gain_ref, part_ref, *refs):
    grad_refs, (out_ref, values_ref) = refs[:-2], refs[-2:]
    model = tok_ref.shape[-1]
    width = grad_refs[0].shape[-1] // 2
    values = part_ref[...]
    for grad_ref in grad_refs[1:]:
        values += grad_ref[:, 2 * width :].astype(f32)
    values_ref[...] = values.astype(bf16)
    tok = tok_ref[...].astype(f32)
    inv_rms = lax.rsqrt(jnp.mean(tok * tok, axis=-1, keepdims=True) + norm_eps)
    total = jnp.zeros((tok.shape[0], 1), f32)
    for k, grad_ref in enumerate(grad_refs):
        for j in range(2):
            cols = column_block(k, j, width)
            weighted = gain_ref[:, cols] * grad_ref[:, j * width : (j + 1) * width].astype(f32)
            scaled = tok_ref[:, cols].astype(f32) * inv_rms
            total += jnp.sum(weighted * scaled, axis=-1, keepdims=True)
    mean = total / model
    for k, grad_ref in enumerate(grad_refs):
        for j in range(2):
            cols = column_block(k, j, width)
            weighted = gain_ref[:, cols] * grad_ref[:, j * width : (j + 1) * width].astype(f32)
            scaled = tok_ref[:, cols].astype(f32) * inv_rms
            out_ref[:, cols] = (inv_rms * (weighted - scaled * mean)).astype(bf16)


def grad_x_blocks(tokens, gain, part, grads):
    rows, model = tokens.shape
    feats = part.shape[-1]
    step = min(rows, 32)
    return pl.pallas_call(
        grad_x_kernel,
        grid=(rows // step,),
        in_specs=[
            pl.BlockSpec((step, model), lambda i: (i, 0)),
            pl.BlockSpec((1, model), lambda i: (0, 0)),
            pl.BlockSpec((step, feats), lambda i: (i, 0)),
        ]
        + [pl.BlockSpec((step, g.shape[1]), lambda i: (i, 0)) for g in grads],
        out_specs=[
            pl.BlockSpec((step, model), lambda i: (i, 0)),
            pl.BlockSpec((step, feats), lambda i: (i, 0)),
        ],
        out_shape=[
            jax.ShapeDtypeStruct((rows, model), bf16),
            jax.ShapeDtypeStruct((rows, feats), bf16),
        ],
        compiler_params=limit(24),
        cost_estimate=cost(16 * rows * model, 6 * rows * model),
        name="grad_x_blocks",
    )(tokens, gain, part, *grads)


def add_kernel(halves_of, *refs):
    outs = refs[-len(halves_of) :]
    at = 0
    for half_of, out_ref in zip(halves_of, outs):
        rows = out_ref.shape[0]
        total = None
        for half in half_of:
            first = (half or 0) * rows
            term = refs[at][first : first + rows, :].astype(f32)
            total = term if total is None else total + term
            at += 1
        out_ref[...] = total.astype(out_ref.dtype)


def relay(sums, after):
    arrays = [array for group in sums for array, _ in group]
    rows, width = sums[0][0][0].shape
    shape = (rows if sums[0][0][1] is None else rows // 2, width)
    return pl.pallas_call(
        functools.partial(add_kernel, [[half for _, half in group] for group in sums]),
        in_specs=[pl.BlockSpec(memory_space=pltpu.VMEM)] * len(arrays)
        + [pl.BlockSpec(memory_space=pl.ANY)] * len(after),
        out_shape=[jax.ShapeDtypeStruct(shape, bf16)] * len(sums),
        compiler_params=limit(16),
        name="relay",
    )(*arrays, *after)


def adam_kernel(token_total, count, owner_ref, *refs):
    part_refs, got_ref, refs = refs[:count], refs[count], refs[count + 1 :]
    master_ref, moment1_ref, moment2_ref = refs[:3]
    out_refs = refs[3:]
    step, width = got_ref.shape
    dp = lax.axis_index("dp")
    owned = (owner_ref[...] == dp).astype(f32)
    count = jnp.sum(owned, axis=1, keepdims=True)
    index = pl.program_id(0) * step + lax.broadcasted_iota(jnp.int32, (step, 1), 0)
    occupied = (index.astype(f32) < count).astype(f32)
    for i, refs in enumerate((part_refs, (got_ref,))):
        total = refs[0][...].astype(f32)
        for ref in refs[1:]:
            total += ref[...].astype(f32)
        cols = pl.ds(pl.multiple_of(((dp % 2) ^ i) * width, width), width)
        slot_grad = total / token_total
        new_moment1 = (beta_one * moment1_ref[:, cols] + (1.0 - beta_one) * slot_grad) * occupied
        new_moment2 = (
            beta_two * moment2_ref[:, cols] + (1.0 - beta_two) * slot_grad * slot_grad
        ) * occupied
        step_dir = new_moment1 / bias_one / (jnp.sqrt(new_moment2 / bias_two) + adam_eps)
        out_refs[0][:, cols] = (master_ref[:, cols] - learn_rate * step_dir) * occupied
        out_refs[1][:, cols] = new_moment1
        out_refs[2][:, cols] = new_moment2


def adam(owner, parts, got, states, token_total):
    slots, cols = states[0].shape
    width = got.shape[-1]
    step = min(slots, 32)
    return pl.pallas_call(
        functools.partial(adam_kernel, token_total, len(parts)),
        grid=(slots // step,),
        in_specs=[pl.BlockSpec(owner.shape, lambda i: (0, 0))]
        + [pl.BlockSpec((step, width), lambda i: (i, 0))] * (len(parts) + 1)
        + [pl.BlockSpec((step, cols), lambda i: (i, 0))] * 3,
        out_specs=[pl.BlockSpec((step, cols), lambda i: (i, 0))] * 3,
        out_shape=[jax.ShapeDtypeStruct((slots, cols), f32)] * 3,
        compiler_params=limit(24),
        cost_estimate=cost(20 * slots * cols, 30 * slots * cols),
        name="adam",
    )(owner, *parts, got, *states)


def on_device(groups, seqs, tokens, gain, w_t, grad_values, owner, master, moment1, moment2):
    planes = groups // 2
    chips = seqs
    parts = column_parts
    tokens, value_grad = tokens[0], grad_values[0]
    rows, model = tokens.shape
    feats = owner.shape[0]
    slots = master.shape[1]
    width = model // (2 * seqs)
    own_x = lax.axis_index("dp") % 2

    def permute(value, target):
        pairs = []
        for dp in range(groups):
            for seq in range(seqs):
                to = target(dp, seq)
                if to is not None:
                    pairs.append((dp * seqs + seq, to[0] * seqs + to[1]))
        return lax.ppermute(value, ("dp", "seq"), pairs)

    def to_chip(value, k):
        return permute(value, lambda dp, seq: (dp ^ (k & 1), seq ^ (k >> 1 << 1)))

    def to_core(value):
        return permute(value, lambda dp, seq: (dp, seq ^ 1))

    def to_x(value):
        return permute(value, lambda dp, seq: (dp ^ 1, seq))

    def to_plane(value, turn):
        return permute(value, lambda dp, seq: (dp ^ (2 * turn), seq))

    def busy(z, step, even):
        rightward = (z % 2 == 0) == even
        return z < step if rightward else planes - 1 - z < step

    def across(value, step, even):
        def target(dp, seq):
            z = dp // 2
            way = 1 if (z % 2 == 0) == even else -1
            return (dp + 2 * way, seq) if busy(z, step, even) else None

        return permute(value, target)

    tokens_far = to_core(tokens)
    grads = [value_grad] + [to_chip(value_grad, k) for k in range(chips - 1, 0, -1)][::-1]

    w_keep, w_send = halves(w_t, width)
    w_got = to_x(w_send)

    gain_row, owner_row = gain[None, :], owner[None, :]
    sent = norm_blocks(tokens, tokens_far, gain_row, chips, width, parts, w_keep)
    grads = stack(grads, 2, [sent[0][0], w_keep])
    pieces = [sent[0]] + [[to_chip(p, k) for p in sent[k]] for k in range(1, chips)]
    grads_far = [to_core(grads[-1])]
    grads = grads[:2]
    selected = select_rows(owner_row, groups, slots, (sent[0][0],))

    weights = stack([w_keep, w_got], 1, grads_far[:1])
    turn = planes // 2
    while turn:
        weights = [w for value in weights for w in (value, to_plane(value, turn))]
        turn //= 2
    weights_far = [to_core(w) for w in weights]

    plan = [
        (step, even)
        for step in range(1, planes)
        for even in (True, False)
        if any(busy(z, step, even) for z in range(planes))
    ]
    every = [*grads, *grads_far]
    early = early_weight(every, [piece[0] for piece in pieces[:-1]])
    base, *outs = weight_blocks(
        selected, early, every, pieces[-1][0], chips, planes, plan[:2], weights
    )
    outs += later_blocks(selected, base, planes, plan[2:], outs[:1])
    ready = dict(zip(plan, outs))
    got = {even: across(ready[1, even], 1, even) for even in (True, False) if (1, even) in ready}
    held = [{even: (value, chunk) for even, value in got.items()} for chunk in range(2)]

    def advance(step, chunks, after):
        here = [even for even in (True, False) if (step, even) in ready]
        adds = [even for even in here if (not even) in held[0]]
        keys = [(chunk, even) for chunk in chunks for even in adds]
        sums = relay(
            [[(ready[step, even], chunk), held[chunk][not even]] for chunk, even in keys], after
        )
        new = [{}, {}]
        for (chunk, even), value in zip(keys, sums):
            new[chunk][even] = (across(value, step, even), None)
        for even in here:
            if even not in adds:
                whole = across(ready[step, even], step, even)
                for chunk in chunks:
                    new[chunk][even] = (whole, chunk)
        for chunk in chunks:
            held[chunk] = new[chunk]
        return sums

    *far_sums, near_sum = value_parts(pieces, weights, feats, outs[:1])
    sums = [near_sum] + [to_core(f) for f in far_sums]
    back = back_blocks(grads, sums, weights + weights_far, chips, [])
    home = [back[0]] + [to_chip(back[k], k) for k in range(1, chips)]
    advance(2, (1, 0), [])
    for step in range(3, planes):
        advance(step, (1,), [])
        advance(step, (0,), [])
    other = relay([[(outs[-1], 1), *held[1].values()]], home[-1:])
    got = to_x(other[0])
    grad_x, values = grad_x_blocks(tokens, gain_row, back[-1], home)
    mine = [outs[-1][:slots]] + [value for value, _ in held[0].values()]
    total = rows * seqs * groups
    states = (master[0], moment1[0], moment2[0])
    states = adam(owner_row, mine, got, states, total)
    return (values[None], grad_x[None], *(s[None] for s in states))


def solution(mesh):
    placed = (
        P("dp", "seq", None),
        P(),
        P("dp", "seq"),
        P("dp", "seq", None),
        P(),
        P("dp", None, "seq"),
        P("dp", None, "seq"),
        P("dp", None, "seq"),
    )
    return jax.shard_map(
        functools.partial(on_device, mesh.shape["dp"], mesh.shape["seq"]),
        mesh=mesh,
        in_specs=placed,
        out_specs=(
            P("dp", "seq", None),
            P("dp", "seq", None),
            P("dp", None, "seq"),
            P("dp", None, "seq"),
            P("dp", None, "seq"),
        ),
        check_vma=False,
    )
```
